32 devices in a mesh: dp: 8 (over z, y), strip: 4 (over x, core).
Axes of the slice: x: 2, y: 2, z: 4, core: 2. Of those that a mesh axis runs over, the one named last changes fastest.
Arguments:
- images: bfloat16 [48, 36, 36, 320], P('dp', 'strip'), may hold values from -6 to 6
- counts: int32 [8], replicated, may hold values from 1 to 6, as said below
- gain_one: bfloat16 [320], replicated, may hold values from 0.5 to 1.5
- shift_one: bfloat16 [320], replicated, may hold values from -3 to 3
- proj_in: bfloat16 [320, 320], replicated, may hold values from -0.3125 to 0.3125
- kernel_five: bfloat16 [25, 320], replicated, may hold values from -1.25 to 1.25
- kernel_seven: bfloat16 [49, 320], replicated, may hold values from -0.875 to 0.875
- lka_proj: bfloat16 [320, 320], replicated, may hold values from -0.3125 to 0.3125
- proj_out: bfloat16 [320, 320], replicated, may hold values from -0.3125 to 0.3125
- scale_one: bfloat16 [320], replicated, may hold values from 0.5 to 1.5
- gain_two: bfloat16 [320], replicated, may hold values from 0.5 to 1.5
- shift_two: bfloat16 [320], replicated, may hold values from -3 to 3
- fc_in: bfloat16 [320, 1280], replicated, may hold values from -0.3125 to 0.3125
- kernel_three: bfloat16 [9, 1280], replicated, may hold values from -2 to 2
- fc_out: bfloat16 [1280, 320], replicated, may hold values from -0.15625 to 0.15625
- scale_two: bfloat16 [320], replicated, may hold values from 0.5 to 1.5
- cotangent: bfloat16 [48, 36, 36, 320], P('dp', 'strip'), may hold values from -6 to 6
Outputs:
- out_image: bfloat16 [48, 36, 36, 320], P('dp', 'strip')
- grad_images: float32 [48, 36, 36, 320], P('dp', 'strip')
- gradient_first_gain: float32 [320], replicated
- gradient_first_shift: float32 [320], replicated
- grad_proj_in: float32 [320, 320], replicated
- grad_kernel_five: float32 [25, 320], replicated
- grad_kernel_seven: float32 [49, 320], replicated
- grad_lka_proj: float32 [320, 320], replicated
- grad_proj_out: float32 [320, 320], replicated
- grad_scale_one: float32 [320], replicated
- grad_gain_two: float32 [320], replicated
- grad_shift_two: float32 [320], replicated
- grad_fc_in: float32 [320, 1280], replicated
- grad_kernel_three: float32 [9, 1280], replicated
- grad_fc_out: float32 [1280, 320], replicated
- grad_scale_two: float32 [320], replicated
The draws below stay inside these ranges and needn't reach their ends.
Inputs may be any that keep to these rules, and one draw needn't show every extreme that they name: `counts`: live images of each index of dp; some index has all 6 slots live.
All inputs are finite; a program needn't handle non-finite values.
Results may differ from the reference program's by a relative error of at most 0.012.
Values may be sent and summed in bfloat16 or wider, within the bound.
No kernel may reach another device: no remote copies, remote signals or barrier semaphores. Data moves between devices by JAX's collectives and lax.ppermute only.
A program may use at most 256 MiB of HBM per device.

```python
import jax
import jax.numpy as jnp
from jax import lax

D = 320
HID = 1280
IMG_DEV = 6
WIDE = 36
HEIGHT = 36
IMAGES = 48
N_DP = 8


def draw_counts(key, part):
    key = jax.random.fold_in(key, 11)
    key_draw, key_full = jax.random.split(key)
    numbers = jax.random.randint(key_draw, (N_DP,), 1, IMG_DEV + 1)
    full_slot = jax.random.randint(key_full, (), 0, N_DP)
    return jnp.where(jnp.arange(N_DP) == full_slot, IMG_DEV, numbers).astype(jnp.int32)


def block_levels(own_key, dims, cuts, smallest, largest):
    factor_of = 1.0
    for position, shards_of in cuts:
        draws = jax.random.uniform(jax.random.fold_in(jax.random.fold_in(own_key, 6), position), (shards_of,), jnp.float32, smallest / len(cuts), largest / len(cuts))
        factor_of = factor_of * jnp.repeat(jnp.exp(draws), dims[position] // shards_of).reshape((-1,) + (1,) * (len(dims) - 1 - position))
    return factor_of


def normal_values(rng, shape, scale, limit, cuts=(), dtype=jnp.bfloat16):
    drawn = scale * jax.random.normal(rng, shape, jnp.float32)
    if cuts:
        drawn = drawn * block_levels(rng, shape, cuts, -0.22, 0.18)
    return jnp.clip(drawn, -limit, limit).astype(dtype)


def setup_inputs(seed: int = 0) -> dict:
    arg_keys = jax.random.split(jax.random.key(seed), 18)
    return {
        "images": normal_values(arg_keys[0], (IMAGES, HEIGHT, WIDE, D), 1.0, 6.0, ((0, 8), (1, 4))),
        "counts": draw_counts(jax.random.fold_in(arg_keys[17], 71), 0),
        "gain_one": jnp.clip(1.0 + 0.1 * jax.random.normal(arg_keys[2], (D,), jnp.float32), 0.5, 1.5).astype(jnp.bfloat16),
        "shift_one": normal_values(arg_keys[3], (D,), 0.3, 3.0),
        "proj_in": normal_values(arg_keys[4], (D, D), D ** -0.5, 0.3125),
        "kernel_five": normal_values(arg_keys[5], (25, D), 25 ** -0.5, 1.25),
        "kernel_seven": normal_values(arg_keys[6], (49, D), 49 ** -0.5, 0.875),
        "lka_proj": normal_values(arg_keys[7], (D, D), D ** -0.5, 0.3125),
        "proj_out": normal_values(arg_keys[8], (D, D), D ** -0.5, 0.3125),
        "scale_one": jnp.clip(1.0 + 0.1 * jax.random.normal(arg_keys[9], (D,), jnp.float32), 0.5, 1.5).astype(jnp.bfloat16),
        "gain_two": jnp.clip(1.0 + 0.1 * jax.random.normal(arg_keys[10], (D,), jnp.float32), 0.5, 1.5).astype(jnp.bfloat16),
        "shift_two": normal_values(arg_keys[11], (D,), 0.3, 3.0),
        "fc_in": normal_values(arg_keys[12], (D, HID), D ** -0.5, 0.3125),
        "kernel_three": normal_values(arg_keys[13], (9, HID), 9 ** -0.5, 2.0),
        "fc_out": normal_values(arg_keys[14], (HID, D), HID ** -0.5, 0.15625),
        "scale_two": jnp.clip(1.0 + 0.1 * jax.random.normal(arg_keys[15], (D,), jnp.float32), 0.5, 1.5).astype(jnp.bfloat16),
        "cotangent": normal_values(arg_keys[16], (IMAGES, HEIGHT, WIDE, D), 1.0, 6.0, ((0, 8), (1, 4))),
    }


epsilon = 1e-05
exact = lax.Precision.HIGHEST

@jax.custom_vjp
def low(v):
    return lax.optimization_barrier(v.astype(jnp.bfloat16)).astype(jnp.float32)

@jax.custom_vjp
def low_back(v):
    return v

def low_keep(v):
    return (low(v), None)

def low_pass(kept, grad):
    return (grad,)

def back_keep(v):
    return (v, None)

def back_low(kept, grad):
    return (low(grad),)
low.defvjp(low_keep, low_pass)
low_back.defvjp(back_keep, back_low)

def depthwise(padded, kernel, across, spread):
    margin = across // 2 * spread
    height = padded.shape[1] - 2 * margin
    breadth = padded.shape[2]
    padded = jnp.pad(padded, ((0, 0), (0, 0), (margin, margin), (0, 0)))
    total = jnp.zeros((padded.shape[0], height, breadth, padded.shape[3]), jnp.float32)
    for row_tap in range(across):
        for col_tap in range(across):
            window = padded[:, row_tap * spread:row_tap * spread + height, col_tap * spread:col_tap * spread + breadth, :]
            total = total + window * kernel[row_tap * across + col_tap]
    return total

def pad_rows(values, margin):
    return jnp.pad(values, ((0, 0), (margin, margin), (0, 0), (0, 0)))

def project(values, matrix):
    return jnp.einsum('bhwc,cd->bhwd', values, matrix, precision=exact)

def reference(images, counts, gain_one, shift_one, proj_in, kernel_five, kernel_seven, lka_proj, proj_out, scale_one, gain_two, shift_two, fc_in, kernel_three, fc_out, scale_two, cotangent):
    slot_ids = jnp.arange(IMAGES)
    alive_mask = (slot_ids % IMG_DEV < counts[slot_ids // IMG_DEV]).astype(jnp.float32)[:, None, None, None]
    pixel_count = jnp.sum(counts).astype(jnp.float32) * (HEIGHT * WIDE)

    def stats(values):
        total = lax.optimization_barrier(jnp.sum(values * alive_mask, axis=(0, 1, 2)))
        square = lax.optimization_barrier(jnp.sum(values * values * alive_mask, axis=(0, 1, 2)))
        mean_value = total / pixel_count
        return (mean_value, lax.rsqrt(square / pixel_count - mean_value * mean_value + epsilon))

    def forward(input_images, gain_one, shift_one, proj_in, kernel_five, kernel_seven, lka_proj, proj_out, scale_one, gain_two, shift_two, fc_in, kernel_three, fc_out, scale_two):

        def attention_fn(normalized_input):
            pre_gelu = low_back(project(low(normalized_input), proj_in))
            gelu_low = low(jax.nn.gelu(pre_gelu, approximate=False))
            lka_mid = low(depthwise(pad_rows(gelu_low, 2), kernel_five, 5, 1))
            lka_out = depthwise(pad_rows(lka_mid, 9), kernel_seven, 7, 3)
            attend = low_back(project(low(lka_out), lka_proj))
            branch = low_back(project(low(gelu_low * attend), proj_out))
            return branch + normalized_input

        def mlp_fn(normed_two):
            hidden = low(low_back(project(low(normed_two), fc_in)))
            mixed = depthwise(pad_rows(hidden, 1), kernel_three, 3, 1)
            active = low(jax.nn.gelu(mixed, approximate=False))
            return low_back(project(active, fc_out))
        blocked = (N_DP, IMG_DEV, HEIGHT, WIDE, D)
        first_mean, first_inverse_deviation = stats(input_images)
        normalized_input = (input_images - first_mean) * first_inverse_deviation * gain_one + shift_one
        attn = lax.map(jax.checkpoint(attention_fn), normalized_input.reshape(blocked)).reshape(input_images.shape)
        first_sum = input_images + scale_one * attn
        mean_two, rstd_two = stats(first_sum)
        normed_two = (first_sum - mean_two) * rstd_two * gain_two + shift_two
        mlp_out = lax.map(jax.checkpoint(mlp_fn), normed_two.reshape(blocked)).reshape(input_images.shape)
        return alive_mask * (first_sum + scale_two * mlp_out)
    params = (gain_one, shift_one, proj_in, kernel_five, kernel_seven, lka_proj, proj_out, scale_one, gain_two, shift_two, fc_in, kernel_three, fc_out, scale_two)
    params = tuple((weight.astype(jnp.float32) for weight in params))
    outputs, pullback = jax.vjp(forward, images.astype(jnp.float32), *params)
    grads = pullback(cotangent.astype(jnp.float32))
    return (outputs.astype(jnp.bfloat16), grads[0], grads[1], grads[2], grads[3], grads[4], grads[5], grads[6], grads[7], grads[8], grads[9], grads[10], grads[11], grads[12], grads[13], grads[14])
```

```python
import jax
import jax.numpy as jnp
from jax import lax
from jax.sharding import PartitionSpec as P

epsilon = 1e-05


def exchange_steps():
    return [
        (axis, 1 << bit)
        for axis in ("strip", "dp")
        for bit in range(lax.axis_size(axis).bit_length() - 1)
    ]


def swapped(value, axis, bit):
    return lax.ppermute(value, axis, [(i, i ^ bit) for i in range(lax.axis_size(axis))])


def summed_everywhere(value):
    for axis, bit in exchange_steps():
        value = value + swapped(value, axis, bit)
    return value


def summed_by_halves(rows):
    steps = exchange_steps()
    part = rows.astype(jnp.bfloat16)
    for axis, bit in steps:
        upper = (lax.axis_index(axis) // bit) % 2
        halves = part.reshape((2, part.shape[0] // 2) + part.shape[1:])
        got = swapped(lax.dynamic_index_in_dim(halves, 1 - upper, 0, False), axis, bit)
        kept = lax.dynamic_index_in_dim(halves, upper, 0, False)
        part = (kept.astype(jnp.float32) + got.astype(jnp.float32)).astype(jnp.bfloat16)
    for axis, bit in reversed(steps):
        upper = (lax.axis_index(axis) // bit) % 2
        got = swapped(part, axis, bit)
        part = jnp.where(
            upper == 0, jnp.concatenate([part, got]), jnp.concatenate([got, part])
        )
    return part.astype(jnp.float32)


def extended(value, sides, width):
    for axis, dim in sides:
        devices, length = (lax.axis_size(axis), value.shape[dim])
        up = [(i, (i + 1) % devices) for i in range(devices - 1)]
        down = [(j, i) for i, j in up]
        last = lax.slice_in_dim(value, length - width, length, axis=dim)
        leading = lax.slice_in_dim(value, 0, width, axis=dim)
        before = lax.ppermute(last, axis, up)
        after = lax.ppermute(leading, axis, down)
        value = jnp.concatenate([before, value, after], axis=dim)
    return value


def depthwise(padded, kernel, across, spread):
    margin = across // 2 * spread
    height = padded.shape[1] - 2 * margin
    breadth = padded.shape[2]
    padded = jnp.pad(padded, ((0, 0), (0, 0), (margin, margin), (0, 0)))
    total = jnp.zeros((padded.shape[0], height, breadth, padded.shape[3]), jnp.float32)
    for row_tap in range(across):
        for col_tap in range(across):
            window = padded[
                :,
                row_tap * spread : row_tap * spread + height,
                col_tap * spread : col_tap * spread + breadth,
                :,
            ]
            total = total + window * kernel[row_tap * across + col_tap]
    return total


def kernel_grad(padded, grad_out, across, spread):
    margin = across // 2 * spread
    height = grad_out.shape[1]
    breadth = grad_out.shape[2]
    padded = jnp.pad(padded, ((0, 0), (0, 0), (margin, margin), (0, 0)))
    tap_sums = []
    for row_tap in range(across):
        for col_tap in range(across):
            window = padded[
                :,
                row_tap * spread : row_tap * spread + height,
                col_tap * spread : col_tap * spread + breadth,
                :,
            ]
            tap_sums.append(jnp.sum(window * grad_out, axis=(0, 1, 2)))
    return jnp.stack(tap_sums)


def project(values, matrix):
    return jnp.einsum("bhwc,cd->bhwd", values, matrix, preferred_element_type=jnp.float32)


def project_back(grads, matrix):
    return jnp.einsum("bhwd,cd->bhwc", grads, matrix, preferred_element_type=jnp.float32)


def outer_sum(values, grads):
    return jnp.einsum("bhwc,bhwd->cd", values, grads, preferred_element_type=jnp.float32)


def gelu_grad(before, grad):
    return jax.vjp(lambda value: jax.nn.gelu(value, approximate=False), before)[1](grad)[0]


def per_channel_sum(values):
    return jnp.sum(values, axis=(0, 1, 2))


def body(
    images,
    counts,
    gain_one,
    shift_one,
    proj_in,
    kernel_five,
    kernel_seven,
    lka_proj,
    proj_out,
    scale_one,
    gain_two,
    shift_two,
    fc_in,
    kernel_three,
    fc_out,
    scale_two,
    cotangent,
):
    slots_here = images.shape[0]
    alive = (jnp.arange(slots_here) < counts[lax.axis_index("dp")]).astype(jnp.float32)[
        :, None, None, None
    ]
    pixel_count = jnp.sum(counts).astype(jnp.float32) * (
        images.shape[1] * lax.axis_size("strip") * images.shape[2]
    )
    first_gain = gain_one.astype(jnp.float32)
    first_shift = shift_one.astype(jnp.float32)
    gain_b = gain_two.astype(jnp.float32)
    shift_b = shift_two.astype(jnp.float32)
    layer_one = scale_one.astype(jnp.float32)
    layer_two = scale_two.astype(jnp.float32)
    taps_five = kernel_five.astype(jnp.float32)
    taps_seven = kernel_seven.astype(jnp.float32)
    taps_three = kernel_three.astype(jnp.float32)
    input_images = images.astype(jnp.float32)
    first_sums = summed_everywhere(
        jnp.stack(
            [
                per_channel_sum(input_images * alive),
                per_channel_sum(input_images * input_images * alive),
            ]
        )
    )
    first_mean = first_sums[0] / pixel_count
    first_inverse_deviation = lax.rsqrt(
        first_sums[1] / pixel_count - first_mean * first_mean + epsilon
    )
    centered_scaled_input = (input_images - first_mean) * first_inverse_deviation
    normalized_input = centered_scaled_input * first_gain + first_shift
    normed_low = normalized_input.astype(jnp.bfloat16)
    pre_gelu = project(normed_low, proj_in)
    gelu_low = jax.nn.gelu(pre_gelu, approximate=False).astype(jnp.bfloat16)
    gelu_rim = extended(gelu_low, (("strip", 1),), 2)
    lka_mid = depthwise(gelu_rim.astype(jnp.float32), taps_five, 5, 1).astype(jnp.bfloat16)
    mid_rim = extended(lka_mid, (("strip", 1),), 9)
    lka_out = depthwise(mid_rim.astype(jnp.float32), taps_seven, 7, 3)
    lka_low = lka_out.astype(jnp.bfloat16)
    attend = project(lka_low, lka_proj)
    gelu_value = gelu_low.astype(jnp.float32)
    gated_low = (gelu_value * attend).astype(jnp.bfloat16)
    branch = project(gated_low, proj_out)
    attn = branch + normalized_input
    first_sum = input_images + layer_one * attn
    second_sums = summed_everywhere(
        jnp.stack(
            [per_channel_sum(first_sum * alive), per_channel_sum(first_sum * first_sum * alive)]
        )
    )
    mean_two = second_sums[0] / pixel_count
    rstd_two = lax.rsqrt(second_sums[1] / pixel_count - mean_two * mean_two + epsilon)
    yhat = (first_sum - mean_two) * rstd_two
    normed_two_low = (yhat * gain_b + shift_b).astype(jnp.bfloat16)
    hidden_low = project(normed_two_low, fc_in).astype(jnp.bfloat16)
    hidden_pad = extended(hidden_low, (("strip", 1),), 1).astype(jnp.float32)
    mixed = depthwise(hidden_pad, taps_three, 3, 1)
    active_low = jax.nn.gelu(mixed, approximate=False).astype(jnp.bfloat16)
    mlp_out = project(active_low, fc_out)
    out_image = (alive * (first_sum + layer_two * mlp_out)).astype(jnp.bfloat16)
    grad_out = cotangent.astype(jnp.float32) * alive
    grad_scale_two = per_channel_sum(grad_out * mlp_out)
    grad_mlp_low = (grad_out * layer_two).astype(jnp.bfloat16)
    grad_active = project_back(grad_mlp_low, fc_out)
    grad_fc_out = outer_sum(active_low, grad_mlp_low)
    grad_mixed = gelu_grad(mixed, grad_active)
    grad_mixed_pad = extended(grad_mixed.astype(jnp.bfloat16), (("strip", 1),), 1).astype(
        grad_mixed.dtype
    )
    grad_hidden = depthwise(grad_mixed_pad, taps_three[::-1], 3, 1).astype(jnp.bfloat16)
    grad_kernel_three = kernel_grad(hidden_pad, grad_mixed, 3, 1)
    grad_normed_two = project_back(grad_hidden, fc_in)
    grad_fc_in = outer_sum(normed_two_low, grad_hidden)
    grad_shift_two, grad_gain_two = summed_everywhere(
        jnp.stack(
            [per_channel_sum(grad_normed_two), per_channel_sum(grad_normed_two * yhat)]
        )
    )
    fc_grads = summed_by_halves(
        jnp.concatenate([grad_fc_in, grad_fc_out.T]).reshape(-1, 128)
    ).reshape(2, grad_fc_in.shape[0], -1)
    grad_first = grad_out + alive * rstd_two * gain_b * (
        grad_normed_two - (grad_shift_two + yhat * grad_gain_two) / pixel_count
    )
    grad_scale_one = per_channel_sum(grad_first * attn)
    grad_attn = grad_first * layer_one
    grad_branch_low = grad_attn.astype(jnp.bfloat16)
    grad_gated = project_back(grad_branch_low, proj_out)
    grad_proj_out = outer_sum(gated_low, grad_branch_low)
    grad_attend_low = (grad_gated * gelu_value).astype(jnp.bfloat16)
    grad_lka_out = project_back(grad_attend_low, lka_proj)
    grad_lka_proj = outer_sum(lka_low, grad_attend_low)
    grad_out_rim = extended(grad_lka_out.astype(jnp.bfloat16), (("strip", 1),), 9).astype(
        grad_lka_out.dtype
    )
    grad_mid = depthwise(grad_out_rim, taps_seven[::-1], 7, 3)
    grad_kernel_seven = kernel_grad(mid_rim.astype(jnp.float32), grad_lka_out, 7, 3)
    grad_mid_rim = extended(grad_mid.astype(jnp.bfloat16), (("strip", 1),), 2).astype(
        grad_mid.dtype
    )
    grad_gelu = grad_gated * attend + depthwise(grad_mid_rim, taps_five[::-1], 5, 1)
    grad_kernel_five = kernel_grad(gelu_rim.astype(jnp.float32), grad_mid, 5, 1)
    grad_pre_low = gelu_grad(pre_gelu, grad_gelu).astype(jnp.bfloat16)
    normalized_gradient = grad_attn + project_back(grad_pre_low, proj_in)
    grad_proj_in = outer_sum(normed_low, grad_pre_low)
    width = grad_proj_in.shape[0]
    vectors = summed_everywhere(
        jnp.stack(
            [
                per_channel_sum(normalized_gradient),
                per_channel_sum(normalized_gradient * centered_scaled_input),
                grad_scale_one,
                grad_scale_two,
            ]
        )
    )
    matrices = summed_by_halves(
        jnp.concatenate(
            [
                grad_proj_in,
                grad_lka_proj,
                grad_proj_out,
                grad_kernel_five,
                grad_kernel_seven,
                grad_kernel_three.reshape(-1, width),
                jnp.zeros((-(3 * width + 110) % 256, width), jnp.float32),
            ]
        )
    )
    ends = [0]
    for count in (width, width, width, 25, 49, 36):
        ends.append(ends[-1] + count)
    pieces = [matrices[i:j] for i, j in zip(ends, ends[1:])]
    totals = (
        vectors[0],
        vectors[1],
        pieces[0],
        pieces[3],
        pieces[4],
        pieces[1],
        pieces[2],
        vectors[2],
        fc_grads[0],
        pieces[5].reshape(9, -1),
        fc_grads[1].T,
        vectors[3],
    )
    gradient_first_shift = totals[0]
    gradient_first_gain = totals[1]
    grad_images = grad_first + alive * first_inverse_deviation * first_gain * (
        normalized_gradient
        - (gradient_first_shift + centered_scaled_input * gradient_first_gain) / pixel_count
    )
    return (
        out_image,
        grad_images,
        gradient_first_gain,
        gradient_first_shift,
        totals[2],
        totals[3],
        totals[4],
        totals[5],
        totals[6],
        totals[7],
        grad_gain_two,
        grad_shift_two,
        totals[8],
        totals[9],
        totals[10],
        totals[11],
    )


def solution(mesh):
    return jax.shard_map(
        body,
        mesh=mesh,
        in_specs=(
            P("dp", "strip", None, None),
            P(),
            P(),
            P(),
            P(),
            P(),
            P(),
            P(),
            P(),
            P(),
            P(),
            P(),
            P(),
            P(),
            P(),
            P(),
            P("dp", "strip", None, None),
        ),
        out_specs=(
            P("dp", "strip", None, None),
            P("dp", "strip", None, None),
            P(),
            P(),
            P(),
            P(),
            P(),
            P(),
            P(),
            P(),
            P(),
            P(),
            P(),
            P(),
            P(),
            P(),
        ),
        check_vma=False,
    )
```

```python
import functools

import jax
import jax.numpy as jnp
from jax import lax
from jax.experimental import pallas as pl
from jax.experimental.pallas import tpu as pltpu
from jax.sharding import PartitionSpec as P

epsilon = 1e-05
lanes = 128
wide = jnp.float32
low = jnp.bfloat16


def exchange_steps():
    return [
        (axis, 1 << bit)
        for axis in ("strip", "dp")
        for bit in range(lax.axis_size(axis).bit_length() - 1)
    ]


def swapped(value, axis, bit):
    return lax.ppermute(value, axis, [(i, i ^ bit) for i in range(lax.axis_size(axis))])


def summed_everywhere(value):
    for axis, bit in exchange_steps():
        value = value + swapped(value, axis, bit)
    return value


def summed_by_halves(rows):
    steps = exchange_steps()
    part = rows.astype(low)
    for axis, bit in steps:
        upper = (lax.axis_index(axis) // bit) % 2
        halves = part.reshape((2, part.shape[0] // 2) + part.shape[1:])
        got = swapped(lax.dynamic_index_in_dim(halves, 1 - upper, 0, False), axis, bit)
        kept = lax.dynamic_index_in_dim(halves, upper, 0, False)
        part = (kept.astype(wide) + got.astype(wide)).astype(low)
    for axis, bit in reversed(steps):
        upper = (lax.axis_index(axis) // bit) % 2
        got = swapped(part, axis, bit)
        part = jnp.where(
            upper == 0, jnp.concatenate([part, got]), jnp.concatenate([got, part])
        )
    return part.astype(wide)


def neighbours(value, width):
    devices, length = lax.axis_size("strip"), value.shape[1]
    up = [(i, i + 1) for i in range(devices - 1)]
    down = [(j, i) for i, j in up]
    before = lax.ppermute(value[:, length - width :], "strip", up)
    after = lax.ppermute(value[:, :width], "strip", down)
    return before, after


def normal_parts(x):
    density = 0.3989422804014327 * jnp.exp(-0.5 * x * x)
    scale = 1.0 + 0.2316419 * jnp.abs(x)
    guess = pl.reciprocal(scale, approx=True)
    t = guess * (2.0 - scale * guess)
    poly = 1.781477937 + t * (-1.821255978 + t * 1.330274429)
    poly = t * (0.319381530 + t * (-0.356563782 + t * poly))
    tail = density * poly
    return jnp.where(x > 0, 1.0 - tail, tail), density


def window_sums(load, weight, across, spread, rows, back, center=None, add_tap=None):
    total = [None] * rows
    reach = spread * (across - 1)
    for j in range(across):
        shift = (j - across // 2) * spread * (-1 if back else 1)
        w = [weight(i * across + j) for i in range(across)]
        tap = [None] * across
        for r in range(rows + reach):
            v = load(r, shift)
            for i in range(across):
                o = r - reach + spread * i if back else r - spread * i
                if 0 <= o < rows:
                    term = v * w[i]
                    total[o] = term if total[o] is None else total[o] + term
                    if center is not None:
                        term = v * center[o]
                        tap[i] = term if tap[i] is None else tap[i] + term
        if center is not None:
            for i in range(across):
                add_tap(i * across + j, tap[i])
    return total


def lane_groups(width):
    return [(start, min(lanes, width - start)) for start in range(0, width, lanes)]


def fill_weights(weights, taps, width):
    weights[...] = jnp.zeros_like(weights)
    for g, (start, size) in enumerate(lane_groups(width)):
        for t in range(taps.shape[0]):
            weights[g, t, :, 0:size] = jnp.broadcast_to(
                taps[t : t + 1, start : start + size].astype(wide), (8, size)
            )


def store_taps(grad_taps, tap_sums, width):
    for g, (start, size) in enumerate(lane_groups(width)):
        for t in range(grad_taps.shape[0]):
            grad_taps[t : t + 1, start : start + size] = jnp.sum(
                tap_sums[g, t, :, 0:size], axis=0, keepdims=True
            )


def inside(rows, pitch, breadth, width):
    place = lax.broadcasted_iota(jnp.int32, (rows, pitch, width), 1)
    return jnp.where(place < breadth, 1.0, 0.0).reshape(rows * pitch, width)


def norm_of(stats, pixels):
    mean = stats[0:1, :] / pixels
    return mean, lax.rsqrt(stats[1:2, :] / pixels - mean * mean + epsilon)


def spec_image(*shape):
    return pl.BlockSpec((1,) + shape, lambda i: (i,) + (0,) * len(shape))


def spec_whole(*shape):
    return pl.BlockSpec(shape, lambda i: (0,) * len(shape))


def call(kernel, images, ins, outs, scratch, flops, moved, name, **sizes):
    return pl.pallas_call(
        functools.partial(kernel, **sizes),
        grid=(images,),
        in_specs=[spec for _, spec in ins],
        out_specs=[spec for _, _, spec in outs],
        out_shape=[jax.ShapeDtypeStruct(shape, dtype) for shape, dtype, _ in outs],
        scratch_shapes=[pltpu.VMEM(shape, dtype) for shape, dtype in scratch],
        compiler_params=pltpu.CompilerParams(vmem_limit_bytes=48 * 1024 * 1024),
        cost_estimate=pl.CostEstimate(flops=flops, bytes_accessed=moved, transcendentals=0),
        name=name,
    )(*[array for array, _ in ins])


def stats_kernel(flags, images, sums):
    image = pl.program_id(0)

    @pl.when(image == 0)
    def _():
        sums[...] = jnp.zeros_like(sums)

    alive = (image < flags[0]).astype(wide)
    total = jnp.zeros((images.shape[2], images.shape[3]), wide)
    square = total
    for r in range(images.shape[1]):
        value = images[0, r].astype(wide)
        total += value
        square += value * value
    sums[0:1, :] += jnp.sum(total, axis=0, keepdims=True) * alive
    sums[1:2, :] += jnp.sum(square, axis=0, keepdims=True) * alive


def front_kernel(
    flags,
    images,
    above,
    below,
    params,
    stats,
    proj_in,
    taps,
    gelu_low,
    pre_gelu,
    lka_mid,
    values,
    gelu,
    weights,
    mask,
    mid,
    *,
    rows,
    breadth,
    pitch,
    strips,
):
    width = images.shape[3]
    pixels = flags[3].astype(wide) * (rows * strips * breadth)
    mean, rstd = norm_of(stats, pixels)
    gain, shift = params[0:1, :], params[1:2, :]

    @pl.when(pl.program_id(0) == 0)
    def _():
        values[...] = jnp.zeros_like(values)
        gelu[...] = jnp.zeros_like(gelu)
        mid[...] = jnp.zeros_like(mid)
        fill_weights(weights, taps, width)
        mask[...] = inside(rows + 4, pitch, breadth, width)
        mask[0 : 2 * pitch, :] *= (flags[1] == 0).astype(wide)
        mask[(rows + 2) * pitch :, :] *= (flags[2] == 0).astype(wide)

    def place(at, value):
        values[at : at + breadth, :] = (value.astype(wide) - mean) * rstd * gain + shift

    for r in range(2):
        place(r * pitch, above[0, r])
        place((rows + 2 + r) * pitch, below[0, r])
    for r in range(rows):
        place((r + 2) * pitch, images[0, r])
    pre = jnp.dot(values[...].astype(low), proj_in[...], preferred_element_type=wide)
    pre_gelu[0] = pre[2 * pitch : (rows + 2) * pitch, :]
    cdf, _ = normal_parts(pre)
    rounded = (pre * cdf * mask[...]).astype(low).astype(wide)
    gelu_low[0] = rounded[2 * pitch : (rows + 2) * pitch, :].astype(low)
    for g, (start, size) in enumerate(lane_groups(width)):
        gelu[g, 8 : 8 + (rows + 4) * pitch, 0:size] = rounded[:, start : start + size]
    for g, (start, size) in enumerate(lane_groups(width)):

        def step(block, carry, g=g, start=start):
            base = pl.multiple_of(block * 8, 8)
            total = window_sums(
                lambda r, s: gelu[g, pl.ds(base + (8 + r * pitch + s), 8), :],
                lambda t: weights[g, t],
                5,
                1,
                rows,
                False,
            )
            for o in range(rows):
                mid[pl.ds(base + o * pitch, 8), start : start + lanes] = total[o]
            return carry

        lax.fori_loop(0, pitch // 8, step, 0)
    for r in range(rows):
        at = r * pitch
        lka_mid[0, r] = (
            mid[at : at + pitch, 0:width] * inside(1, pitch, breadth, width)
        ).astype(low)


def attend_kernel(
    flags,
    images,
    lka_mid,
    above,
    below,
    gelu_low,
    params,
    stats,
    lka_proj,
    proj_out,
    taps,
    lka_low,
    attend_out,
    attn_out,
    first_sum,
    sums,
    window,
    weights,
    lka,
    values,
    mask,
    *,
    rows,
    breadth,
    pitch,
    gap,
    strips,
):
    image = pl.program_id(0)
    width = images.shape[3]
    alive = (image < flags[0]).astype(wide)
    pixels = flags[3].astype(wide) * (rows * strips * breadth)
    mean, rstd = norm_of(stats, pixels)
    gain, shift, scale = params[0:1, :], params[1:2, :], params[2:3, :]

    @pl.when(image == 0)
    def _():
        window[...] = jnp.zeros_like(window)
        values[...] = jnp.zeros_like(values)
        lka[...] = jnp.zeros_like(lka)
        sums[...] = jnp.zeros_like(sums)
        fill_weights(weights, taps, width)
        mask[...] = inside(rows, pitch, breadth, width)

    for part, source in enumerate((above, lka_mid, below)):
        for r in range(rows):
            at = 16 + (part * rows + r) * gap
            for g, (start, size) in enumerate(lane_groups(width)):
                window[g, at : at + pitch, 0:size] = source[0, r, :, start : start + size].astype(
                    wide
                )
    for g, (start, size) in enumerate(lane_groups(width)):

        def step(block, carry, g=g, start=start):
            base = pl.multiple_of(block * 8, 8)
            total = window_sums(
                lambda r, s: window[g, pl.ds(base + (16 + r * gap + s), 8), :],
                lambda t: weights[g, t],
                7,
                3,
                rows,
                False,
            )
            for o in range(rows):
                lka[pl.ds(base + o * pitch, 8), start : start + lanes] = total[o]
            return carry

        lax.fori_loop(0, pitch // 8, step, 0)
    for r in range(rows):
        values[r * pitch : r * pitch + breadth, :] = images[0, r].astype(wide)
    low_lka = lka[:, 0:width].astype(low)
    lka_low[0] = low_lka
    attend = jnp.dot(low_lka, lka_proj[...], preferred_element_type=wide)
    attend_out[0] = attend
    gated = (gelu_low[0].astype(wide) * attend).astype(low)
    branch = jnp.dot(gated, proj_out[...], preferred_element_type=wide)
    attn = (branch + ((values[...] - mean) * rstd * gain + shift)) * mask[...]
    attn_out[0] = attn
    first = values[...] + scale * attn
    first_sum[0] = first
    sums[0:1, :] += jnp.sum(first, axis=0, keepdims=True) * alive
    sums[1:2, :] += jnp.sum(first * first, axis=0, keepdims=True) * alive


def gate_kernel(
    flags,
    first_sum,
    attn,
    cot,
    grad_normed,
    lka_low,
    attend,
    gelu_low,
    params,
    stats,
    grad_stats,
    lka_proj,
    proj_out,
    grad_first,
    grad_lka,
    grad_direct,
    grad_lka_proj,
    grad_proj_out,
    sums,
    values,
    mask,
    *,
    rows,
    breadth,
    pitch,
    strips,
):
    image = pl.program_id(0)
    width = cot.shape[3]
    alive = (image < flags[0]).astype(wide)
    pixels = flags[3].astype(wide) * (rows * strips * breadth)
    mean, rstd = norm_of(stats, pixels)
    scale, gain = params[2:3, :], params[3:4, :]

    @pl.when(image == 0)
    def _():
        values[...] = jnp.zeros_like(values)
        mask[...] = inside(rows, pitch, breadth, width)
        sums[...] = jnp.zeros_like(sums)
        grad_lka_proj[...] = jnp.zeros_like(grad_lka_proj)
        grad_proj_out[...] = jnp.zeros_like(grad_proj_out)

    for r in range(rows):
        values[r * pitch : r * pitch + breadth, :] = cot[0, r].astype(wide)
    yhat = (first_sum[0] - mean) * rstd
    inner = grad_normed[0] - (grad_stats[0:1, :] + yhat * grad_stats[1:2, :]) / pixels
    first = alive * (values[...] + rstd * gain * inner) * mask[...]
    grad_first[0] = first
    sums[0:1, :] += jnp.sum(first * attn[0], axis=0, keepdims=True)
    branch = (first * scale).astype(low)
    gated_back = lax.dot_general(
        branch, proj_out[...], (((1,), (1,)), ((), ())), preferred_element_type=wide
    )
    gelu = gelu_low[0].astype(wide)
    gated = gelu * attend[0]
    grad_proj_out[...] += jnp.dot(
        gated.T.astype(low), branch, preferred_element_type=wide
    )
    grad_direct[0] = gated_back * attend[0]
    back = (gated_back * gelu).astype(low)
    lka = lax.dot_general(
        back, lka_proj[...], (((1,), (1,)), ((), ())), preferred_element_type=wide
    )
    grad_lka_proj[...] += jnp.dot(
        lka_low[0].astype(wide).T.astype(low), back, preferred_element_type=wide
    )
    for r in range(rows):
        grad_lka[0, r] = lka[r * pitch : (r + 1) * pitch, :].astype(low)


def seven_kernel(
    grad_lka,
    above,
    below,
    lka_mid,
    taps,
    grad_mid,
    grad_taps,
    window,
    middle,
    out,
    weights,
    tap_sums,
    *,
    rows,
    breadth,
    pitch,
    gap,
):
    image = pl.program_id(0)
    width = grad_lka.shape[3]

    @pl.when(image == 0)
    def _():
        window[...] = jnp.zeros_like(window)
        middle[...] = jnp.zeros_like(middle)
        tap_sums[...] = jnp.zeros_like(tap_sums)
        fill_weights(weights, taps, width)

    for g, (start, size) in enumerate(lane_groups(width)):
        for part, source in enumerate((above, grad_lka, below)):
            for r in range(rows):
                at = 16 + (part * rows + r) * gap
                window[g, at : at + pitch, 0:size] = source[0, r, :, start : start + size].astype(
                    wide
                )
        for r in range(rows):
            middle[g, r * pitch : (r + 1) * pitch, 0:size] = lka_mid[
                0, r, :, start : start + size
            ].astype(wide)
    for g, (start, size) in enumerate(lane_groups(width)):

        def step(block, carry, g=g, start=start):
            base = pl.multiple_of(block * 8, 8)

            def add_tap(t, value):
                tap_sums[g, t] += value

            total = window_sums(
                lambda r, s: window[g, pl.ds(base + (16 + r * gap + s), 8), :],
                lambda t: weights[g, t],
                7,
                3,
                rows,
                True,
                [middle[g, pl.ds(base + p * pitch, 8), :] for p in range(rows)],
                add_tap,
            )
            for o in range(rows):
                out[pl.ds(base + o * pitch, 8), start : start + lanes] = total[o]
            return carry

        lax.fori_loop(0, pitch // 8, step, 0)
    for r in range(rows):
        at = r * pitch
        grad_mid[0, r] = (
            out[at : at + pitch, 0:width] * inside(1, pitch, breadth, width)
        ).astype(low)

    @pl.when(image == pl.num_programs(0) - 1)
    def _():
        store_taps(grad_taps, tap_sums, width)


def five_kernel(
    flags,
    images,
    grad_mid,
    above,
    below,
    gelu_low,
    pre_gelu,
    grad_direct,
    grad_first,
    params,
    stats,
    proj_in,
    taps,
    grad_partial,
    grad_proj_in,
    grad_taps,
    sums,
    window,
    middle,
    out,
    weights,
    tap_sums,
    values,
    mask,
    *,
    rows,
    breadth,
    pitch,
    strips,
):
    image = pl.program_id(0)
    width = images.shape[3]
    alive = (image < flags[0]).astype(wide)
    pixels = flags[3].astype(wide) * (rows * strips * breadth)
    mean, rstd = norm_of(stats, pixels)
    gain, shift, scale = params[0:1, :], params[1:2, :], params[2:3, :]

    @pl.when(image == 0)
    def _():
        window[...] = jnp.zeros_like(window)
        middle[...] = jnp.zeros_like(middle)
        tap_sums[...] = jnp.zeros_like(tap_sums)
        values[...] = jnp.zeros_like(values)
        sums[...] = jnp.zeros_like(sums)
        grad_proj_in[...] = jnp.zeros_like(grad_proj_in)
        mask[...] = inside(rows, pitch, breadth, width)
        fill_weights(weights, taps, width)

    for g, (start, size) in enumerate(lane_groups(width)):
        for r in range(2):
            at = 8 + r * pitch
            window[g, at : at + pitch, 0:size] = above[0, r, :, start : start + size].astype(wide)
            at = 8 + (rows + 2 + r) * pitch
            window[g, at : at + pitch, 0:size] = below[0, r, :, start : start + size].astype(wide)
        for r in range(rows):
            at = 8 + (r + 2) * pitch
            window[g, at : at + pitch, 0:size] = grad_mid[0, r, :, start : start + size].astype(
                wide
            )
        middle[g, :, 0:size] = gelu_low[0, :, start : start + size].astype(wide)
    for g, (start, size) in enumerate(lane_groups(width)):

        def step(block, carry, g=g, start=start):
            base = pl.multiple_of(block * 8, 8)

            def add_tap(t, value):
                tap_sums[g, t] += value

            total = window_sums(
                lambda r, s: window[g, pl.ds(base + (8 + r * pitch + s), 8), :],
                lambda t: weights[g, t],
                5,
                1,
                rows,
                True,
                [middle[g, pl.ds(base + p * pitch, 8), :] for p in range(rows)],
                add_tap,
            )
            for o in range(rows):
                out[pl.ds(base + o * pitch, 8), start : start + lanes] = total[o]
            return carry

        lax.fori_loop(0, pitch // 8, step, 0)
    for r in range(rows):
        values[r * pitch : r * pitch + breadth, :] = images[0, r].astype(wide)
    pre = pre_gelu[0]
    cdf, density = normal_parts(pre)
    grad_pre = ((grad_direct[0] + out[:, 0:width]) * (cdf + pre * density)).astype(low)
    xhat = (values[...] - mean) * rstd
    normed = (xhat * gain + shift) * mask[...]
    grad_proj_in[...] += jnp.dot(normed.T.astype(low), grad_pre, preferred_element_type=wide)
    back = lax.dot_general(
        grad_pre, proj_in[...], (((1,), (1,)), ((), ())), preferred_element_type=wide
    )
    first = grad_first[0]
    grad_normed = (first * scale + back) * mask[...]
    sums[0:1, :] += jnp.sum(grad_normed, axis=0, keepdims=True)
    sums[1:2, :] += jnp.sum(grad_normed * xhat, axis=0, keepdims=True)
    grad_partial[0] = first + alive * rstd * gain * grad_normed

    @pl.when(image == pl.num_programs(0) - 1)
    def _():
        store_taps(grad_taps, tap_sums, width)


def last_kernel(
    flags, images, grad_partial, params, stats, grad_stats, grad_images, *, rows, breadth, pitch, strips
):
    alive = (pl.program_id(0) < flags[0]).astype(wide)
    pixels = flags[3].astype(wide) * (rows * strips * breadth)
    mean, rstd = norm_of(stats, pixels)
    factor = alive * rstd * params[0:1, :] / pixels
    for r in range(rows):
        xhat = (images[0, r].astype(wide) - mean) * rstd
        part = grad_partial[0, r * pitch : r * pitch + breadth, :]
        grad_images[0, r] = part - factor * (grad_stats[0:1, :] + xhat * grad_stats[1:2, :])


def mlp_kernel(
    flags,
    first_sum,
    above,
    below,
    cot,
    cot_above,
    cot_below,
    params,
    stats,
    fc_in,
    fc_out,
    taps,
    out_image,
    grad_normed,
    sums,
    grad_in,
    grad_out,
    grad_taps,
    normed_wide,
    mlp_wide,
    normed_low,
    normed_turned,
    grads_low,
    grads_turned,
    hidden,
    from_active,
    grad_mixed,
    active,
    grad_hidden,
    mlp_sum,
    normed_sum,
    weights,
    tap_sums,
    in_sum,
    out_sum,
    *,
    rows,
    breadth,
    pitch,
    strips,
):
    image = pl.program_id(0)
    alive = (image < flags[0]).astype(jnp.float32)
    upper = (flags[1] == 0).astype(jnp.float32)
    lower = (flags[2] == 0).astype(jnp.float32)
    groups = fc_in.shape[1] // (2 * lanes)
    blocks = pitch // 8
    pixels = flags[3].astype(wide) * (rows * strips * breadth)
    mean_two, rstd_two = norm_of(stats, pixels)
    gain_two, shift_two, scale_two = params[3:4, :], params[4:5, :], params[5:6, :]

    @pl.when(image == 0)
    def _():
        normed_wide[...] = jnp.zeros_like(normed_wide)
        mlp_wide[...] = jnp.zeros_like(mlp_wide)
        hidden[...] = jnp.zeros_like(hidden)
        grad_mixed[...] = jnp.zeros_like(grad_mixed)
        tap_sums[...] = jnp.zeros_like(tap_sums)
        in_sum[...] = jnp.zeros_like(in_sum)
        out_sum[...] = jnp.zeros_like(out_sum)
        sums[...] = jnp.zeros_like(sums)
        fill_weights(weights, taps, taps.shape[1])

    def normalized(value):
        return (value - mean_two) * rstd_two * gain_two + shift_two

    for r in range(2):
        normed_wide[r * pitch : r * pitch + breadth, :] = upper * normalized(
            above[0, r, 0:breadth, :]
        )
        at = (rows + 2 + r) * pitch
        normed_wide[at : at + breadth, :] = lower * normalized(below[0, r, 0:breadth, :])
    for r in range(rows):
        at = (r + 2) * pitch
        normed_wide[at : at + breadth, :] = normalized(first_sum[0, r, 0:breadth, :])
        at = (r + 1) * pitch
        mlp_wide[at : at + breadth, :] = cot[0, r].astype(jnp.float32) * alive * scale_two
    mlp_wide[0:breadth, :] = cot_above[0, 0].astype(jnp.float32) * alive * scale_two
    at = (rows + 1) * pitch
    mlp_wide[at : at + breadth, :] = cot_below[0, 0].astype(jnp.float32) * alive * scale_two
    normed_low[...] = normed_wide[...].astype(jnp.bfloat16)
    grads_low[...] = mlp_wide[...].astype(jnp.bfloat16)
    inner = normed_wide[2 * pitch : (rows + 2) * pitch, :]
    normed_turned[...] = inner.T.astype(jnp.bfloat16)
    grads_turned[...] = mlp_wide[pitch : (rows + 1) * pitch, :].T.astype(jnp.bfloat16)
    mlp_sum[...] = jnp.zeros_like(mlp_sum)
    normed_sum[...] = jnp.zeros_like(normed_sum)

    def group_step(group, carry):
        columns = pl.ds(pl.multiple_of(group * (2 * lanes), 2 * lanes), 2 * lanes)
        in_part = fc_in[:, columns]
        out_part = fc_out[columns, :]
        hid = jnp.dot(normed_low[...], in_part, preferred_element_type=jnp.float32)
        hid = hid.astype(jnp.bfloat16).astype(jnp.float32)
        act = lax.dot_general(
            grads_low[...],
            out_part,
            (((1,), (1,)), ((), ())),
            preferred_element_type=jnp.float32,
        )
        for half in range(2):
            lane = slice(half * lanes, (half + 1) * lanes)
            hidden[half, 8 : 8 + (rows + 4) * pitch, :] = hid[:, lane]
            from_active[half] = act[:, lane]

        for half in range(2):
            lane = slice(half * lanes, (half + 1) * lanes)
            place = group * 2 + half

            def forward(block, carry, half=half, lane=lane, place=place):
                base = pl.multiple_of(block * 8, 8)
                mixed = window_sums(
                    lambda r, s: hidden[half, pl.ds(base + (8 + r * pitch + s), 8), :],
                    lambda t: weights[place, t],
                    3,
                    1,
                    rows + 2,
                    False,
                )
                for o in range(rows + 2):
                    x = mixed[o]
                    cdf, density = normal_parts(x)
                    slope = cdf + x * density
                    grad_mixed[half, pl.ds(base + (8 + o * pitch), 8), :] = (
                        from_active[half, pl.ds(base + o * pitch, 8), :] * slope
                    )
                    if 1 <= o <= rows:
                        active[pl.ds(base + (o - 1) * pitch, 8), lane] = x * cdf
                return carry

            lax.fori_loop(0, blocks, forward, 0)

            def backward(block, carry, half=half, lane=lane, place=place):
                base = pl.multiple_of(block * 8, 8)

                def add_tap(t, value):
                    tap_sums[place, t] += value

                total = window_sums(
                    lambda r, s: grad_mixed[half, pl.ds(base + (8 + r * pitch + s), 8), :],
                    lambda t: weights[place, t],
                    3,
                    1,
                    rows,
                    True,
                    [hidden[half, pl.ds(base + (8 + (p + 2) * pitch), 8), :] for p in range(rows)],
                    add_tap,
                )
                for p in range(rows):
                    grad_hidden[pl.ds(base + p * pitch, 8), lane] = total[p]
                return carry

            lax.fori_loop(0, blocks, backward, 0)

        act_low = active[...].astype(jnp.bfloat16)
        hid_low = grad_hidden[...].astype(jnp.bfloat16)
        mlp_sum[...] += jnp.dot(act_low, out_part, preferred_element_type=jnp.float32)
        normed_sum[...] += lax.dot_general(
            hid_low, in_part, (((1,), (1,)), ((), ())), preferred_element_type=jnp.float32
        )
        part_in = jnp.dot(normed_turned[...], hid_low, preferred_element_type=jnp.float32)
        part_out = jnp.dot(grads_turned[...], act_low, preferred_element_type=jnp.float32)
        for half in range(2):
            lane = slice(half * lanes, (half + 1) * lanes)
            in_sum[group * 2 + half] += part_in[:, lane]
            out_sum[group * 2 + half] += part_out[:, lane]
        return carry

    lax.fori_loop(0, groups, group_step, 0)

    scale_grad = jnp.zeros_like(scale_two)
    shift_grad = jnp.zeros_like(scale_two)
    gain_grad = jnp.zeros_like(scale_two)
    for r in range(rows):
        mlp = mlp_sum[r * pitch : r * pitch + breadth, :]
        back = normed_sum[r * pitch : r * pitch + breadth, :]
        first = first_sum[0, r, 0:breadth, :]
        out_image[0, r] = (alive * (first + scale_two * mlp)).astype(jnp.bfloat16)
        grad_normed[0, r * pitch : r * pitch + breadth, :] = back
        grad_normed[0, r * pitch + breadth : (r + 1) * pitch, :] = jnp.zeros(
            (pitch - breadth, back.shape[1]), wide
        )
        grad = cot[0, r].astype(jnp.float32) * alive
        scale_grad += jnp.sum(grad * mlp, axis=0, keepdims=True)
        shift_grad += jnp.sum(back, axis=0, keepdims=True)
        gain_grad += jnp.sum(back * (first - mean_two) * rstd_two, axis=0, keepdims=True)
    sums[0:1, :] += shift_grad
    sums[1:2, :] += gain_grad
    sums[2:3, :] += scale_grad

    @pl.when(image == pl.num_programs(0) - 1)
    def _():
        grad_in[...] = in_sum[...].astype(jnp.bfloat16)
        grad_out[...] = out_sum[...].astype(jnp.bfloat16)
        store_taps(grad_taps, tap_sums, taps.shape[1])


def mlp_block(
    flags, first_sum, above, below, cot, cot_above, cot_below, params, stats, fc_in, fc_out, taps
):
    images, rows, breadth, width = cot.shape
    pitch = first_sum.shape[2]
    deep = fc_in.shape[1]
    groups = deep // lanes
    count = images * rows * breadth
    return call(
        mlp_kernel,
        images,
        [
            (flags, pl.BlockSpec(memory_space=pltpu.SMEM)),
            (first_sum, spec_image(rows, pitch, width)),
            (above, spec_image(2, pitch, width)),
            (below, spec_image(2, pitch, width)),
            (cot, spec_image(rows, breadth, width)),
            (cot_above, spec_image(1, breadth, width)),
            (cot_below, spec_image(1, breadth, width)),
            (params, spec_whole(8, width)),
            (stats, spec_whole(2, width)),
            (fc_in, spec_whole(width, deep)),
            (fc_out, spec_whole(deep, width)),
            (taps, spec_whole(9, deep)),
        ],
        [
            (cot.shape, low, spec_image(rows, breadth, width)),
            ((images, rows * pitch, width), wide, spec_image(rows * pitch, width)),
            ((8, width), wide, spec_whole(8, width)),
            ((groups, width, lanes), low, spec_whole(groups, width, lanes)),
            ((groups, width, lanes), low, spec_whole(groups, width, lanes)),
            ((9, deep), wide, spec_whole(9, deep)),
        ],
        [
            (((rows + 4) * pitch, width), wide),
            (((rows + 2) * pitch, width), wide),
            (((rows + 4) * pitch, width), low),
            ((width, rows * pitch), low),
            (((rows + 2) * pitch, width), low),
            ((width, rows * pitch), low),
            ((2, (rows + 4) * pitch + 16, lanes), wide),
            ((2, (rows + 2) * pitch, lanes), wide),
            ((2, (rows + 2) * pitch + 16, lanes), wide),
            ((rows * pitch, 2 * lanes), wide),
            ((rows * pitch, 2 * lanes), wide),
            ((rows * pitch, width), wide),
            ((rows * pitch, width), wide),
            ((groups, 9, 8, lanes), wide),
            ((groups, 9, 8, lanes), wide),
            ((groups, width, lanes), wide),
            ((groups, width, lanes), wide),
        ],
        12 * count * width * deep,
        16 * count * width,
        "mlp",
        rows=rows,
        breadth=breadth,
        pitch=pitch,
        strips=lax.axis_size("strip"),
    )


def body(
    images,
    counts,
    gain_one,
    shift_one,
    proj_in,
    kernel_five,
    kernel_seven,
    lka_proj,
    proj_out,
    scale_one,
    gain_two,
    shift_two,
    fc_in,
    kernel_three,
    fc_out,
    scale_two,
    cotangent,
):
    slots, rows, breadth, width = images.shape
    strips = lax.axis_size("strip")
    strip = lax.axis_index("strip")
    pitch = -(-(breadth + 2) // 8) * 8
    gap = -(-(breadth + 9) // 8) * 8
    flat = rows * pitch
    flags = jnp.stack(
        [
            counts[lax.axis_index("dp")],
            (strip == 0).astype(jnp.int32),
            (strip == strips - 1).astype(jnp.int32),
            jnp.sum(counts),
        ]
    )
    blank = jnp.zeros_like(gain_one)
    params = jnp.stack(
        [gain_one, shift_one, scale_one, gain_two, shift_two, scale_two, blank, blank]
    ).astype(wide)
    sizes = dict(rows=rows, breadth=breadth, pitch=pitch)
    smem = pl.BlockSpec(memory_space=pltpu.SMEM)
    vec = spec_whole(8, width)
    two = spec_whole(2, width)
    square = spec_whole(width, width)
    image_spec = spec_image(rows, breadth, width)
    flat_spec = spec_image(flat, width)
    row_spec = spec_image(rows, pitch, width)
    flat_shape = (slots, flat, width)
    row_shape = (slots, rows, pitch, width)
    groups = len(lane_groups(width))
    area = slots * rows * breadth
    matmul = 2 * area * width * width

    image_above, image_below = neighbours(images, 2)
    cot_above, cot_below = neighbours(cotangent, 1)
    (first_part,) = call(
        stats_kernel,
        slots,
        [(flags, smem), (images, image_spec)],
        [((2, width), wide, two)],
        [],
        3 * area * width,
        2 * area * width,
        "input_sums",
    )
    first_stats = summed_everywhere(first_part)
    gelu_low, pre_gelu, lka_mid = call(
        front_kernel,
        slots,
        [
            (flags, smem),
            (images, image_spec),
            (image_above, spec_image(2, breadth, width)),
            (image_below, spec_image(2, breadth, width)),
            (params, vec),
            (first_stats, two),
            (proj_in, square),
            (kernel_five, spec_whole(*kernel_five.shape)),
        ],
        [
            (flat_shape, low, flat_spec),
            (flat_shape, wide, flat_spec),
            (row_shape, low, row_spec),
        ],
        [
            (((rows + 4) * pitch, width), wide),
            ((groups, (rows + 4) * pitch + 16, lanes), wide),
            ((groups, 25, 8, lanes), wide),
            (((rows + 4) * pitch, width), wide),
            ((flat, groups * lanes), wide),
        ],
        matmul + 50 * area * width,
        10 * area * width,
        "normed_to_five",
        strips=strips,
        **sizes,
    )
    mid_above, mid_below = neighbours(lka_mid, rows)
    lka_low, attend, attn, first_sum, second_part = call(
        attend_kernel,
        slots,
        [
            (flags, smem),
            (images, image_spec),
            (lka_mid, row_spec),
            (mid_above, row_spec),
            (mid_below, row_spec),
            (gelu_low, flat_spec),
            (params, vec),
            (first_stats, two),
            (lka_proj, square),
            (proj_out, square),
            (kernel_seven, spec_whole(*kernel_seven.shape)),
        ],
        [
            (flat_shape, low, flat_spec),
            (flat_shape, wide, flat_spec),
            (flat_shape, wide, flat_spec),
            (flat_shape, wide, flat_spec),
            ((2, width), wide, two),
        ],
        [
            ((groups, 3 * rows * gap + 48, lanes), wide),
            ((groups, 49, 8, lanes), wide),
            ((flat, groups * lanes), wide),
            ((flat, width), wide),
            ((flat, width), wide),
        ],
        2 * matmul + 98 * area * width,
        22 * area * width,
        "seven_to_first_sum",
        strips=strips,
        gap=gap,
        **sizes,
    )
    first_rows = first_sum.reshape(row_shape)
    sum_above, sum_below = neighbours(first_rows, 2)
    second_stats = summed_everywhere(second_part)
    out_image, grad_normed_two, mlp_sums, fc_in_part, fc_out_part, grad_kernel_three = mlp_block(
        flags,
        first_rows,
        sum_above,
        sum_below,
        cotangent,
        cot_above,
        cot_below,
        params,
        second_stats,
        fc_in,
        fc_out,
        kernel_three,
    )
    grad_second = summed_everywhere(mlp_sums[:2])
    fc_grads = summed_by_halves(
        jnp.concatenate([fc_in_part.reshape(-1, lanes), fc_out_part.reshape(-1, lanes)])
    ).reshape((2,) + fc_in_part.shape)
    fc_grads = fc_grads.transpose(0, 2, 1, 3).reshape(2, width, fc_in.shape[1])
    grad_first, grad_lka, grad_direct, grad_lka_proj, grad_proj_out, scale_sums = call(
        gate_kernel,
        slots,
        [
            (flags, smem),
            (first_sum, flat_spec),
            (attn, flat_spec),
            (cotangent, image_spec),
            (grad_normed_two, flat_spec),
            (lka_low, flat_spec),
            (attend, flat_spec),
            (gelu_low, flat_spec),
            (params, vec),
            (second_stats, two),
            (grad_second, two),
            (lka_proj, square),
            (proj_out, square),
        ],
        [
            (flat_shape, wide, flat_spec),
            (row_shape, low, row_spec),
            (flat_shape, wide, flat_spec),
            ((width, width), wide, square),
            ((width, width), wide, square),
            ((8, width), wide, vec),
        ],
        [((flat, width), wide), ((flat, width), wide)],
        4 * matmul,
        30 * area * width,
        "gate_backward",
        strips=strips,
        **sizes,
    )
    lka_above, lka_below = neighbours(grad_lka, rows)
    grad_mid, grad_kernel_seven = call(
        seven_kernel,
        slots,
        [
            (grad_lka, row_spec),
            (lka_above, row_spec),
            (lka_below, row_spec),
            (lka_mid, row_spec),
            (kernel_seven, spec_whole(*kernel_seven.shape)),
        ],
        [
            (row_shape, low, row_spec),
            (kernel_seven.shape, wide, spec_whole(*kernel_seven.shape)),
        ],
        [
            ((groups, 3 * rows * gap + 48, lanes), wide),
            ((groups, flat, lanes), wide),
            ((flat, groups * lanes), wide),
            ((groups, 49, 8, lanes), wide),
            ((groups, 49, 8, lanes), wide),
        ],
        200 * area * width,
        10 * area * width,
        "seven_backward",
        gap=gap,
        **sizes,
    )
    five_above, five_below = neighbours(grad_mid, 2)
    grad_partial, grad_proj_in, grad_kernel_five, last_sums = call(
        five_kernel,
        slots,
        [
            (flags, smem),
            (images, image_spec),
            (grad_mid, row_spec),
            (five_above, spec_image(2, pitch, width)),
            (five_below, spec_image(2, pitch, width)),
            (gelu_low, flat_spec),
            (pre_gelu, flat_spec),
            (grad_direct, flat_spec),
            (grad_first, flat_spec),
            (params, vec),
            (first_stats, two),
            (proj_in, square),
            (kernel_five, spec_whole(*kernel_five.shape)),
        ],
        [
            (flat_shape, wide, flat_spec),
            ((width, width), wide, square),
            (kernel_five.shape, wide, spec_whole(*kernel_five.shape)),
            ((8, width), wide, vec),
        ],
        [
            ((groups, (rows + 4) * pitch + 16, lanes), wide),
            ((groups, flat, lanes), wide),
            ((flat, groups * lanes), wide),
            ((groups, 25, 8, lanes), wide),
            ((groups, 25, 8, lanes), wide),
            ((flat, width), wide),
            ((flat, width), wide),
        ],
        2 * matmul + 100 * area * width,
        24 * area * width,
        "five_backward",
        strips=strips,
        **sizes,
    )
    vectors = summed_everywhere(
        jnp.concatenate([last_sums[0:2], scale_sums[0:1], mlp_sums[2:3]])
    )
    matrices = summed_by_halves(
        jnp.concatenate(
            [
                grad_proj_in,
                grad_lka_proj,
                grad_proj_out,
                grad_kernel_five,
                grad_kernel_seven,
                grad_kernel_three.reshape(-1, width),
                jnp.zeros((-(3 * width + 110) % 256, width), wide),
            ]
        )
    )
    ends = [0]
    for count in (width, width, width, 25, 49, 36):
        ends.append(ends[-1] + count)
    pieces = [matrices[i:j] for i, j in zip(ends, ends[1:])]
    (grad_images,) = call(
        last_kernel,
        slots,
        [
            (flags, smem),
            (images, image_spec),
            (grad_partial, flat_spec),
            (params, vec),
            (first_stats, two),
            (vectors, spec_whole(4, width)),
        ],
        [(images.shape, wide, image_spec)],
        [],
        6 * area * width,
        10 * area * width,
        "input_gradient",
        strips=strips,
        **sizes,
    )
    return (
        out_image,
        grad_images,
        vectors[1],
        vectors[0],
        pieces[0],
        pieces[3],
        pieces[4],
        pieces[1],
        pieces[2],
        vectors[2],
        grad_second[1],
        grad_second[0],
        fc_grads[0],
        pieces[5].reshape(9, -1),
        fc_grads[1].T,
        vectors[3],
    )


def solution(mesh):
    split = P("dp", "strip", None, None)
    return jax.shard_map(
        body,
        mesh=mesh,
        in_specs=(split,) + (P(),) * 15 + (split,),
        out_specs=(split, split) + (P(),) * 14,
        check_vma=False,
    )
```

```python
import functools

import jax
import jax.numpy as jnp
from jax import lax
from jax.experimental import pallas as pl
from jax.experimental.pallas import tpu as pltpu
from jax.sharding import PartitionSpec as P

epsilon = 1e-05
lanes = 128
smem = pl.BlockSpec(memory_space=pltpu.SMEM)
wide = jnp.float32
low = jnp.bfloat16


def exchange_steps():
    return [
        (axis, 1 << bit)
        for axis in ("strip", "dp")
        for bit in range(lax.axis_size(axis).bit_length() - 1)
    ]


def swapped(value, axis, bit):
    return lax.ppermute(value, axis, [(i, i ^ bit) for i in range(lax.axis_size(axis))])


def device_count():
    return lax.axis_size("dp") * lax.axis_size("strip")


def from_all(copies):
    return lax.all_to_all(copies, ("dp", "strip"), 0, 0)


def split_sums(rows, whole):
    size = whole.shape[0]
    part = jnp.concatenate([rows, whole])
    for place, (axis, bit) in enumerate(exchange_steps()):
        length = part.shape[0] - size
        if place < 3:
            upper = (lax.axis_index(axis) // bit) % 2
            tail = part[length:]
            halves = part[:length].reshape((2, length // 2) + part.shape[1:])
            sent = lax.dynamic_index_in_dim(halves, 1 - upper, 0, False)
            kept = lax.dynamic_index_in_dim(halves, upper, 0, False)
            sent, part = jnp.concatenate([sent, tail]), jnp.concatenate([kept, tail])
        else:
            sent = part
        got = swapped(sent, axis, bit)
        part = (part.astype(wide) + got.astype(wide)).astype(low)
    return part[: part.shape[0] - size], part[part.shape[0] - size :]


def joined(part):
    for axis, bit in reversed(exchange_steps()[:3]):
        upper = (lax.axis_index(axis) // bit) % 2
        got = swapped(part, axis, bit)
        part = jnp.where(
            upper == 0, jnp.concatenate([part, got]), jnp.concatenate([got, part])
        )
    return part.astype(wide)


def shifted(last, first):
    up = [(i, i + 1) for i in range(lax.axis_size("strip") - 1)]
    return (
        lax.ppermute(last, "strip", up),
        lax.ppermute(first, "strip", [(j, i) for i, j in up]),
    )


def neighbours(value, width):
    return shifted(value[:, value.shape[1] - width :], value[:, :width])


def normal_parts(x):
    density = 0.3989422804014327 * jnp.exp(-0.5 * x * x)
    scale = 1.0 + 0.2316419 * jnp.abs(x)
    guess = pl.reciprocal(scale, approx=True)
    t = guess * (2.0 - scale * guess)
    poly = 1.781477937 + t * (-1.821255978 + t * 1.330274429)
    poly = t * (0.319381530 + t * (-0.356563782 + t * poly))
    tail = density * poly
    return jnp.where(x > 0, 1.0 - tail, tail), density


def window_sums(load, weight, across, spread, rows, back, center=None, add_tap=None):
    total = [None] * rows
    reach = spread * (across - 1)
    for j in range(across):
        shift = (j - across // 2) * spread * (-1 if back else 1)
        w = [weight(i * across + j) for i in range(across)]
        tap = [None] * across
        for r in range(rows + reach):
            v = load(r, shift)
            for i in range(across):
                o = r - reach + spread * i if back else r - spread * i
                if 0 <= o < rows:
                    term = v * w[i]
                    total[o] = term if total[o] is None else total[o] + term
                    if center is not None:
                        term = v * center[o]
                        tap[i] = term if tap[i] is None else tap[i] + term
        if center is not None:
            for i in range(across):
                add_tap(i * across + j, tap[i])
    return total


def lane_groups(width):
    return [(start, min(lanes, width - start)) for start in range(0, width, lanes)]


def fill_weights(weights, taps, width):
    weights[...] = jnp.zeros_like(weights)
    for g, (start, size) in enumerate(lane_groups(width)):
        for t in range(taps.shape[0]):
            weights[g, t, :, 0:size] = jnp.broadcast_to(
                taps[t : t + 1, start : start + size].astype(wide), (8, size)
            )


def store_taps(grad_taps, tap_sums, width):
    for g, (start, size) in enumerate(lane_groups(width)):
        for t in range(grad_taps.shape[0]):
            grad_taps[t : t + 1, start : start + size] = jnp.sum(
                tap_sums[g, t, :, 0:size], axis=0, keepdims=True
            )


def inside(rows, pitch, breadth, width):
    place = lax.broadcasted_iota(jnp.int32, (rows, pitch, width), 1)
    return jnp.where(place < breadth, 1.0, 0.0).reshape(rows * pitch, width)


def live_here(counts):
    return counts[lax.axis_index("dp")]


def pixels_of(counts, area):
    total = counts[0]
    for k in range(1, counts.shape[0]):
        total += counts[k]
    return total.astype(wide) * (area * lax.axis_size("strip"))


def norm_of(blocks, pixels):
    stats = jnp.sum(blocks[...], axis=0) / pixels
    mean = stats[0:1, :]
    return mean, lax.rsqrt(stats[1:2, :] - mean * mean + epsilon)


def spec_image(*shape):
    return pl.BlockSpec((1,) + shape, lambda i: (i,) + (0,) * len(shape))


def spec_from(start, *shape):
    return pl.BlockSpec((1,) + shape, lambda i: (i + start,) + (0,) * len(shape))


def spec_two(start, *shape):
    return pl.BlockSpec((2,) + shape, lambda i: (i + start,) + (0,) * len(shape))


def spec_whole(*shape):
    return pl.BlockSpec(shape, lambda i: (0,) * len(shape))


def call(kernel, steps, ins, outs, scratch, flops, moved, name, vmem=20, **sizes):
    earlier = [out[3] for out in outs if len(out) > 3 and out[3] is not None]
    aliases, at = {}, len(ins)
    for place, out in enumerate(outs):
        if len(out) > 3 and out[3] is not None:
            aliases[at] = place
            at += 1

    def run(*refs):
        kernel(*refs[: len(ins)], *refs[at:], **sizes)

    return pl.pallas_call(
        run,
        grid=(steps,),
        in_specs=[spec for _, spec in ins] + [pl.BlockSpec(memory_space=pl.ANY)] * len(earlier),
        out_specs=[out[2] for out in outs],
        out_shape=[jax.ShapeDtypeStruct(out[0], out[1]) for out in outs],
        scratch_shapes=[pltpu.VMEM(shape, dtype) for shape, dtype in scratch],
        input_output_aliases=aliases,
        compiler_params=pltpu.CompilerParams(vmem_limit_bytes=vmem * 1024 * 1024),
        cost_estimate=pl.CostEstimate(flops=flops, bytes_accessed=moved, transcendentals=0),
        name=name,
    )(*[array for array, _ in ins], *earlier)


def paired(value):
    return pair_lanes(value, value)


def pair_lanes(left, right):
    main = left.shape[-1] // lanes * lanes
    tails = jnp.concatenate([left[..., main:], right[..., main:]], axis=-1)
    return jnp.concatenate([left[..., :main], right[..., :main], tails], axis=-1)


def split_lanes(value):
    width = value.shape[-1] // 2
    main = width // lanes * lanes
    left = jnp.concatenate([value[..., :main], value[..., 2 * main : main + width]], axis=-1)
    right = jnp.concatenate([value[..., main : 2 * main], value[..., main + width :]], axis=-1)
    return left, right


def folded(value):
    left, right = split_lanes(value)
    return left + right


def folded_square(value):
    width = value.shape[0] // 2
    main = width // lanes * lanes
    left = split_lanes(jnp.concatenate([value[:main], value[2 * main : main + width]], axis=0))[0]
    right = split_lanes(jnp.concatenate([value[main : 2 * main], value[main + width :]], axis=0))[1]
    return left + right


def pair_matrix(matrix):
    blank = jnp.zeros_like(matrix)
    left = jnp.concatenate([matrix, blank], axis=1)
    right = jnp.concatenate([blank, matrix], axis=1)
    width = matrix.shape[0]
    main = width // lanes * lanes

    def columns(value):
        return jnp.concatenate(
            [
                value[:, :main],
                value[:, width : width + main],
                value[:, main:width],
                value[:, width + main :],
            ],
            axis=1,
        )

    left, right = columns(left), columns(right)
    return jnp.concatenate([left[:main], right[:main], left[main:], right[main:]])


def pair_groups(width):
    main = width // lanes
    return [(g * lanes, g % main) for g in range(2 * main)] + [(2 * main * lanes, main)]


def fill_pair_weights(weights, taps, width):
    main = width // lanes * lanes
    for t in range(taps.shape[0]):
        row = taps[t : t + 1, :].astype(wide)
        tail = row[:, main:]
        for g in range(main // lanes):
            weights[g, t] = jnp.broadcast_to(row[:, g * lanes : (g + 1) * lanes], (8, lanes))
        weights[main // lanes, t] = jnp.broadcast_to(
            jnp.concatenate([tail, tail], axis=1), (8, lanes)
        )


def store_pair_taps(grad_taps, tap_sums, width):
    main = width // lanes * lanes
    for t in range(grad_taps.shape[0]):
        for g in range(main // lanes):
            grad_taps[t : t + 1, g * lanes : (g + 1) * lanes] = jnp.sum(
                tap_sums[g, t], axis=0, keepdims=True
            )
        tail = jnp.sum(tap_sums[main // lanes, t], axis=0, keepdims=True)
        grad_taps[t : t + 1, main:width] = tail[:, : width - main] + tail[:, width - main :]


def alive_lanes(counts, start, width):
    main = width // lanes * lanes
    image = 2 * (pl.program_id(0) + start)
    at = lax.broadcasted_iota(jnp.int32, (1, 2 * width), 1)
    second = ((at >= main) & (at < 2 * main)) | (at >= main + width)
    return jnp.where(image + second.astype(jnp.int32) < live_here(counts), 1.0, 0.0)


def stats_kernel(counts, images, copies, sums):
    image = pl.program_id(0)

    @pl.when(image == 0)
    def _():
        sums[...] = jnp.zeros_like(sums)

    alive = (image < live_here(counts)).astype(wide)
    total = jnp.zeros((images.shape[2], images.shape[3]), wide)
    square = total
    for r in range(images.shape[1]):
        value = images[0, r].astype(wide)
        total += value
        square += value * value
    sums[0:1, :] += jnp.sum(total, axis=0, keepdims=True) * alive
    sums[1:2, :] += jnp.sum(square, axis=0, keepdims=True) * alive

    @pl.when(image == pl.num_programs(0) - 1)
    def _():
        copies[...] = jnp.broadcast_to(sums[...][None], copies.shape)


def front_kernel(
    counts,
    images,
    above,
    below,
    params,
    stats,
    proj_in,
    taps,
    gelu_low,
    pre_gelu,
    lka_mid,
    values,
    gelu,
    weights,
    mask,
    mid,
    *,
    rows,
    breadth,
    pitch,
):
    width = images.shape[3]
    pixels = pixels_of(counts, rows * breadth)
    mean, rstd = norm_of(stats, pixels)
    mean, rstd = paired(mean), paired(rstd)
    gain, shift = paired(params[0:1, :]), paired(params[1:2, :])

    @pl.when(pl.program_id(0) == 0)
    def _():
        values[...] = jnp.zeros_like(values)
        gelu[...] = jnp.zeros_like(gelu)
        fill_pair_weights(weights, taps, width)
        mask[...] = inside(rows + 4, pitch, breadth, lanes)
        mask[0 : 2 * pitch, :] *= (lax.axis_index("strip") > 0).astype(wide)
        mask[(rows + 2) * pitch :, :] *= (lax.axis_index("strip") < lax.axis_size("strip") - 1).astype(wide)

    def place(at, source, r):
        value = pair_lanes(source[0, r].astype(wide), source[1, r].astype(wide))
        values[at : at + breadth, :] = (value - mean) * rstd * gain + shift

    for r in range(2):
        place(r * pitch, above, r)
        place((rows + 2 + r) * pitch, below, r)
    for r in range(rows):
        place((r + 2) * pitch, images, r)
    pre = jnp.dot(values[...].astype(low), proj_in[...], preferred_element_type=wide)
    pre_gelu[0] = pre[2 * pitch : (rows + 2) * pitch, :].astype(low)
    for g, (start, _) in enumerate(pair_groups(width)):
        part = pre[:, start : start + lanes]
        cdf, _ = normal_parts(part)
        rounded = (part * cdf * mask[...]).astype(low).astype(wide)
        gelu_low[0, :, start : start + lanes] = rounded[2 * pitch : (rows + 2) * pitch].astype(low)
        gelu[g, 8 : 8 + (rows + 4) * pitch, :] = rounded
    for g, (start, which) in enumerate(pair_groups(width)):

        def step(block, carry, g=g, start=start, which=which):
            base = pl.multiple_of(block * 8, 8)
            total = window_sums(
                lambda r, s: gelu[g, pl.ds(base + (8 + r * pitch + s), 8), :],
                lambda t: weights[which, t],
                5,
                1,
                rows,
                False,
            )
            for o in range(rows):
                mid[pl.ds(base + o * pitch, 8), start : start + lanes] = total[o]
            return carry

        lax.fori_loop(0, pitch // 8, step, 0)
    for r in range(rows):
        at = r * pitch
        lka_mid[0, r] = (
            mid[at : at + pitch, :] * inside(1, pitch, breadth, 2 * width)
        ).astype(low)


def attend_kernel(
    counts,
    images,
    lka_mid,
    above,
    below,
    gelu_low,
    params,
    stats,
    earlier_sums,
    lka_proj,
    proj_out,
    taps,
    lka_low,
    attend_out,
    attn_out,
    first_sum,
    copies,
    sums,
    window,
    weights,
    lka,
    values,
    mask,
    *,
    rows,
    breadth,
    pitch,
    gap,
    start_pair,
):
    width = images.shape[3]
    alive = alive_lanes(counts, start_pair, width)
    pixels = pixels_of(counts, rows * breadth)
    mean, rstd = norm_of(stats, pixels)
    mean, rstd = paired(mean), paired(rstd)
    gain, shift, scale = (paired(params[k : k + 1, :]) for k in range(3))

    @pl.when(pl.program_id(0) == 0)
    def _():
        window[...] = jnp.zeros_like(window)
        values[...] = jnp.zeros_like(values)
        sums[...] = earlier_sums[0]
        fill_pair_weights(weights, taps, width)
        mask[...] = inside(rows, pitch, breadth, 2 * width)

    for part, source in enumerate((above, lka_mid, below)):
        for r in range(rows):
            at = 16 + (part * rows + r) * gap
            for g, (start, _) in enumerate(pair_groups(width)):
                window[g, at : at + pitch, :] = source[0, r, :, start : start + lanes].astype(wide)
    for g, (start, which) in enumerate(pair_groups(width)):

        def step(block, carry, g=g, start=start, which=which):
            base = pl.multiple_of(block * 8, 8)
            total = window_sums(
                lambda r, s: window[g, pl.ds(base + (16 + r * gap + s), 8), :],
                lambda t: weights[which, t],
                7,
                3,
                rows,
                False,
            )
            for o in range(rows):
                lka[pl.ds(base + o * pitch, 8), start : start + lanes] = total[o]
            return carry

        lax.fori_loop(0, pitch // 8, step, 0)
    for r in range(rows):
        values[r * pitch : r * pitch + breadth, :] = pair_lanes(
            images[0, r].astype(wide), images[1, r].astype(wide)
        )
    low_lka = lka[...].astype(low)
    lka_low[0] = low_lka
    attend = jnp.dot(low_lka, lka_proj[...], preferred_element_type=wide)
    attend_out[0] = attend.astype(low)
    gated = (gelu_low[0].astype(wide) * attend).astype(low)
    branch = jnp.dot(gated, proj_out[...], preferred_element_type=wide)
    attn = (branch + ((values[...] - mean) * rstd * gain + shift)) * mask[...]
    attn_out[0] = attn.astype(low)
    first = values[...] + scale * attn
    first_sum[0], first_sum[1] = split_lanes(first)
    sums[0:1, :] += folded(jnp.sum(first, axis=0, keepdims=True) * alive)
    sums[1:2, :] += folded(jnp.sum(first * first, axis=0, keepdims=True) * alive)

    @pl.when(pl.program_id(0) == pl.num_programs(0) - 1)
    def _():
        copies[...] = jnp.broadcast_to(sums[...][None], copies.shape)


def gate_kernel(
    counts,
    first_sum,
    attn,
    cot,
    grad_normed,
    lka_low,
    attend,
    gelu_low,
    params,
    stats,
    grad_stats,
    lka_proj,
    proj_out,
    grad_first,
    grad_direct,
    grad_lka,
    grad_lka_proj,
    grad_proj_out,
    sums,
    values,
    mask,
    *,
    rows,
    breadth,
    pitch,
    start_pair,
):
    width = cot.shape[3]
    alive = alive_lanes(counts, start_pair, width)
    pixels = pixels_of(counts, rows * breadth)
    mean, rstd = norm_of(stats, pixels)
    mean, rstd = paired(mean), paired(rstd)
    scale, gain = paired(params[2:3, :]), paired(params[3:4, :])
    grad_sums = jnp.sum(grad_stats[...], axis=0)
    shift_sum, gain_sum = paired(grad_sums[0:1, :]), paired(grad_sums[1:2, :])

    @pl.when(pl.program_id(0) == 0)
    def _():
        values[...] = jnp.zeros_like(values)
        mask[...] = inside(rows, pitch, breadth, 2 * width)
        sums[...] = jnp.zeros_like(sums)
        grad_lka_proj[...] = jnp.zeros_like(grad_lka_proj)
        grad_proj_out[...] = jnp.zeros_like(grad_proj_out)

    for r in range(rows):
        values[r * pitch : r * pitch + breadth, :] = pair_lanes(
            cot[0, r].astype(wide), cot[1, r].astype(wide)
        )
    yhat = (pair_lanes(first_sum[0], first_sum[1]) - mean) * rstd
    inner = pair_lanes(grad_normed[0], grad_normed[1]) - (shift_sum + yhat * gain_sum) / pixels
    first = alive * (values[...] + rstd * gain * inner) * mask[...]
    grad_first[0] = first
    sums[0:1, :] += folded(jnp.sum(first * attn[0].astype(wide), axis=0, keepdims=True))
    branch = (first * scale).astype(low)
    gated_back = lax.dot_general(
        branch, proj_out[...], (((1,), (1,)), ((), ())), preferred_element_type=wide
    )
    gelu = gelu_low[0].astype(wide)
    attended = attend[0].astype(wide)
    gated = gelu * attended
    grad_proj_out[...] += folded_square(
        jnp.dot(gated.T.astype(low), branch, preferred_element_type=wide)
    )
    grad_direct[0] = (gated_back * attended).astype(low)
    back = (gated_back * gelu).astype(low)
    lka = lax.dot_general(
        back, lka_proj[...], (((1,), (1,)), ((), ())), preferred_element_type=wide
    )
    grad_lka_proj[...] += folded_square(
        jnp.dot(lka_low[0].astype(wide).T.astype(low), back, preferred_element_type=wide)
    )
    for r in range(rows):
        grad_lka[0, r] = lka[r * pitch : (r + 1) * pitch, :].astype(low)


def seven_kernel(
    grad_lka,
    above,
    below,
    lka_mid,
    taps,
    grad_mid,
    grad_taps,
    window,
    middle,
    out,
    weights,
    tap_sums,
    *,
    rows,
    breadth,
    pitch,
    gap,
):
    width = taps.shape[1]

    @pl.when(pl.program_id(0) == 0)
    def _():
        window[...] = jnp.zeros_like(window)
        tap_sums[...] = jnp.zeros_like(tap_sums)
        fill_pair_weights(weights, taps, width)

    for g, (start, _) in enumerate(pair_groups(width)):
        for part, source in enumerate((above, grad_lka, below)):
            for r in range(rows):
                at = 16 + (part * rows + r) * gap
                window[g, at : at + pitch, :] = source[0, r, :, start : start + lanes].astype(wide)
        for r in range(rows):
            middle[g, r * pitch : (r + 1) * pitch, :] = lka_mid[
                0, r, :, start : start + lanes
            ].astype(wide)
    for g, (start, which) in enumerate(pair_groups(width)):

        def step(block, carry, g=g, start=start, which=which):
            base = pl.multiple_of(block * 8, 8)

            def add_tap(t, value):
                tap_sums[which, t] += value

            total = window_sums(
                lambda r, s: window[g, pl.ds(base + (16 + r * gap + s), 8), :],
                lambda t: weights[which, t],
                7,
                3,
                rows,
                True,
                [middle[g, pl.ds(base + p * pitch, 8), :] for p in range(rows)],
                add_tap,
            )
            for o in range(rows):
                out[pl.ds(base + o * pitch, 8), start : start + lanes] = total[o]
            return carry

        lax.fori_loop(0, pitch // 8, step, 0, unroll=True)
    for r in range(rows):
        at = r * pitch
        grad_mid[0, r] = (
            out[at : at + pitch, :] * inside(1, pitch, breadth, 2 * width)
        ).astype(low)

    @pl.when(pl.program_id(0) == pl.num_programs(0) - 1)
    def _():
        store_pair_taps(grad_taps, tap_sums, width)


def five_kernel(
    counts,
    images,
    grad_mid,
    above,
    below,
    gelu_low,
    pre_gelu,
    grad_direct,
    grad_first,
    params,
    stats,
    proj_in,
    taps,
    grad_partial,
    grad_proj_in,
    grad_taps,
    sums,
    window,
    middle,
    out,
    weights,
    tap_sums,
    values,
    mask,
    *,
    rows,
    breadth,
    pitch,
):
    width = images.shape[3]
    alive = alive_lanes(counts, 0, width)
    pixels = pixels_of(counts, rows * breadth)
    mean, rstd = norm_of(stats, pixels)
    mean, rstd = paired(mean), paired(rstd)
    gain, shift, scale = (paired(params[k : k + 1, :]) for k in range(3))

    @pl.when(pl.program_id(0) == 0)
    def _():
        window[...] = jnp.zeros_like(window)
        tap_sums[...] = jnp.zeros_like(tap_sums)
        values[...] = jnp.zeros_like(values)
        sums[...] = jnp.zeros_like(sums)
        grad_proj_in[...] = jnp.zeros_like(grad_proj_in)
        mask[...] = inside(rows, pitch, breadth, 2 * width)
        fill_pair_weights(weights, taps, width)

    for g, (start, _) in enumerate(pair_groups(width)):
        for r in range(2):
            at = 8 + r * pitch
            window[g, at : at + pitch, :] = above[0, r, :, start : start + lanes].astype(wide)
            at = 8 + (rows + 2 + r) * pitch
            window[g, at : at + pitch, :] = below[0, r, :, start : start + lanes].astype(wide)
        for r in range(rows):
            at = 8 + (r + 2) * pitch
            window[g, at : at + pitch, :] = grad_mid[0, r, :, start : start + lanes].astype(wide)
        middle[g] = gelu_low[0, :, start : start + lanes].astype(wide)
    for g, (start, which) in enumerate(pair_groups(width)):

        def step(block, carry, g=g, start=start, which=which):
            base = pl.multiple_of(block * 8, 8)

            def add_tap(t, value):
                tap_sums[which, t] += value

            total = window_sums(
                lambda r, s: window[g, pl.ds(base + (8 + r * pitch + s), 8), :],
                lambda t: weights[which, t],
                5,
                1,
                rows,
                True,
                [middle[g, pl.ds(base + p * pitch, 8), :] for p in range(rows)],
                add_tap,
            )
            for o in range(rows):
                out[pl.ds(base + o * pitch, 8), start : start + lanes] = total[o]
            return carry

        lax.fori_loop(0, pitch // 8, step, 0, unroll=True)
    for r in range(rows):
        values[r * pitch : r * pitch + breadth, :] = pair_lanes(
            images[0, r].astype(wide), images[1, r].astype(wide)
        )
    pre = pre_gelu[0].astype(wide)
    cdf, density = normal_parts(pre)
    grad_pre = ((grad_direct[0].astype(wide) + out[...]) * (cdf + pre * density)).astype(low)
    xhat = (values[...] - mean) * rstd
    normed = (xhat * gain + shift) * mask[...]
    grad_proj_in[...] += folded_square(
        jnp.dot(normed.T.astype(low), grad_pre, preferred_element_type=wide)
    )
    back = lax.dot_general(
        grad_pre, proj_in[...], (((1,), (1,)), ((), ())), preferred_element_type=wide
    )
    first = grad_first[0]
    grad_normed = (first * scale + back) * mask[...]
    sums[0:1, :] += folded(jnp.sum(grad_normed, axis=0, keepdims=True))
    sums[1:2, :] += folded(jnp.sum(grad_normed * xhat, axis=0, keepdims=True))
    grad_partial[0], grad_partial[1] = split_lanes(first + alive * rstd * gain * grad_normed)

    @pl.when(pl.program_id(0) == pl.num_programs(0) - 1)
    def _():
        store_pair_taps(grad_taps, tap_sums, width)


def last_kernel(
    counts, images, grad_partial, params, stats, grad_stats, grad_images, *, rows, breadth, pitch
):
    alive = (pl.program_id(0) < live_here(counts)).astype(wide)
    pixels = pixels_of(counts, rows * breadth)
    mean, rstd = norm_of(stats, pixels)
    factor = alive * rstd * params[0:1, :] / pixels
    grad_sums = grad_stats[...].astype(wide)
    shift_sum, gain_sum = grad_sums[0:1, :], grad_sums[1:2, :]
    for r in range(rows):
        xhat = (images[0, r].astype(wide) - mean) * rstd
        part = grad_partial[0, r * pitch : r * pitch + breadth, :]
        grad_images[0, r] = part - factor * (shift_sum + xhat * gain_sum)


def mlp_kernel(
    counts,
    first_sum,
    above,
    below,
    cot,
    cot_above,
    cot_below,
    params,
    stats,
    fc_in,
    fc_out,
    taps,
    out_image,
    grad_normed,
    copies,
    scale_sum,
    grad_fc,
    grad_taps,
    sums,
    normed_wide,
    mlp_wide,
    normed_low,
    normed_turned,
    grads_low,
    grads_turned,
    hidden_even,
    hidden_odd,
    active_even,
    active_odd,
    grad_mixed,
    low_even,
    low_odd,
    back_even,
    back_odd,
    mlp_sum,
    normed_sum,
    weights,
    tap_sums,
    in_sum,
    out_sum,
    *,
    rows,
    breadth,
    pitch,
):
    image = pl.program_id(0)
    alive = (image < live_here(counts)).astype(jnp.float32)
    upper = (lax.axis_index("strip") > 0).astype(jnp.float32)
    lower = (lax.axis_index("strip") < lax.axis_size("strip") - 1).astype(jnp.float32)
    groups = fc_in.shape[1] // (2 * lanes)
    blocks = pitch // 8
    pixels = pixels_of(counts, rows * breadth)
    mean_two, rstd_two = norm_of(stats, pixels)
    gain_two, shift_two, scale_two = params[3:4, :], params[4:5, :], params[5:6, :]

    @pl.when(image == 0)
    def _():
        normed_wide[...] = jnp.zeros_like(normed_wide)
        mlp_wide[...] = jnp.zeros_like(mlp_wide)
        hidden_even[...] = jnp.zeros_like(hidden_even)
        hidden_odd[...] = jnp.zeros_like(hidden_odd)
        grad_mixed[...] = jnp.zeros_like(grad_mixed)
        tap_sums[...] = jnp.zeros_like(tap_sums)
        in_sum[...] = jnp.zeros_like(in_sum)
        out_sum[...] = jnp.zeros_like(out_sum)
        sums[...] = jnp.zeros_like(sums)
        scale_sum[...] = jnp.zeros_like(scale_sum)
        fill_weights(weights, taps, taps.shape[1])

    def normalized(value):
        return (value - mean_two) * rstd_two * gain_two + shift_two

    for r in range(2):
        normed_wide[r * pitch : r * pitch + breadth, :] = upper * normalized(
            above[0, r, 0:breadth, :]
        )
        at = (rows + 2 + r) * pitch
        normed_wide[at : at + breadth, :] = lower * normalized(below[0, r, 0:breadth, :])
    for r in range(rows):
        at = (r + 2) * pitch
        normed_wide[at : at + breadth, :] = normalized(first_sum[0, r, 0:breadth, :])
        at = (r + 1) * pitch
        mlp_wide[at : at + breadth, :] = cot[0, r].astype(jnp.float32) * alive * scale_two
    mlp_wide[0:breadth, :] = cot_above[0, 2].astype(jnp.float32) * alive * scale_two
    at = (rows + 1) * pitch
    mlp_wide[at : at + breadth, :] = cot_below[0, 2].astype(jnp.float32) * alive * scale_two
    normed_low[...] = normed_wide[...].astype(jnp.bfloat16)
    grads_low[...] = mlp_wide[...].astype(jnp.bfloat16)
    inner = normed_wide[2 * pitch : (rows + 2) * pitch, :]
    normed_turned[...] = inner.T.astype(jnp.bfloat16)
    grads_turned[...] = mlp_wide[pitch : (rows + 1) * pitch, :].T.astype(jnp.bfloat16)
    mlp_sum[...] = jnp.zeros_like(mlp_sum)
    normed_sum[...] = jnp.zeros_like(normed_sum)

    hiddens, sources = (hidden_even, hidden_odd), (active_even, active_odd)
    actives, backs = (low_even, low_odd), (back_even, back_odd)

    def columns(group):
        return slice(group * 2 * lanes, (group + 1) * 2 * lanes)

    def enter(group):
        hid = jnp.dot(normed_low[...], fc_in[:, columns(group)], preferred_element_type=wide)
        hid = hid.astype(low).astype(wide)
        act = jnp.dot(grads_low[...], fc_out[:, columns(group)], preferred_element_type=wide)
        for half in range(2):
            lane = slice(half * lanes, (half + 1) * lanes)
            hiddens[group % 2][half, 8 : 8 + (rows + 4) * pitch, :] = hid[:, lane]
            sources[group % 2][half] = act[:, lane]

    def forward(group, half, block):
        hidden, source, active = (refs[group % 2] for refs in (hiddens, sources, actives))
        lane = slice(half * lanes, (half + 1) * lanes)
        place, base = group * 2 + half, block * 8
        mixed = window_sums(
            lambda r, s: hidden[half, pl.ds(base + (8 + r * pitch + s), 8), :],
            lambda t: weights[place, t],
            3,
            1,
            rows + 2,
            False,
        )
        for o in range(rows + 2):
            x = mixed[o]
            cdf, density = normal_parts(x)
            slope = cdf + x * density
            grad_mixed[half, pl.ds(base + (8 + o * pitch), 8), :] = (
                source[half, pl.ds(base + o * pitch, 8), :] * slope
            )
            if 1 <= o <= rows:
                active[pl.ds(base + (o - 1) * pitch, 8), lane] = x * cdf

    def backward(group, half, block):
        hidden, back = hiddens[group % 2], backs[group % 2]
        lane = slice(half * lanes, (half + 1) * lanes)
        place, base = group * 2 + half, block * 8

        def add_tap(t, value):
            tap_sums[place, t] += value

        total = window_sums(
            lambda r, s: grad_mixed[half, pl.ds(base + (8 + r * pitch + s), 8), :],
            lambda t: weights[place, t],
            3,
            1,
            rows,
            True,
            [hidden[half, pl.ds(base + (8 + (p + 2) * pitch), 8), :] for p in range(rows)],
            add_tap,
        )
        for p in range(rows):
            back[pl.ds(base + p * pitch, 8), lane] = total[p]

    def leave(group):
        act_low = actives[group % 2][...].astype(low)
        hid_low = backs[group % 2][...].astype(low)
        mlp_sum[...] += lax.dot_general(
            act_low,
            fc_out[:, columns(group)],
            (((1,), (1,)), ((), ())),
            preferred_element_type=wide,
        )
        normed_sum[...] += lax.dot_general(
            hid_low,
            fc_in[:, columns(group)],
            (((1,), (1,)), ((), ())),
            preferred_element_type=wide,
        )
        part_in = jnp.dot(normed_turned[...], hid_low, preferred_element_type=wide)
        part_out = jnp.dot(grads_turned[...], act_low, preferred_element_type=wide)
        for half in range(2):
            lane = slice(half * lanes, (half + 1) * lanes)
            in_sum[group * 2 + half] += part_in[:, lane]
            out_sum[group * 2 + half] += part_out[:, lane]

    enter(0)
    for group in range(groups):
        if group + 1 < groups:
            enter(group + 1)
        if group > 0:
            leave(group - 1)
        for half in range(2):
            for block in range(blocks):
                forward(group, half, block)
        for half in range(2):
            for block in range(blocks):
                backward(group, half, block)
    leave(groups - 1)

    scale_grad = jnp.zeros_like(scale_two)
    shift_grad = jnp.zeros_like(scale_two)
    gain_grad = jnp.zeros_like(scale_two)
    for r in range(rows):
        mlp = mlp_sum[r * pitch : r * pitch + breadth, :]
        back = normed_sum[r * pitch : r * pitch + breadth, :]
        first = first_sum[0, r, 0:breadth, :]
        out_image[0, r] = (alive * (first + scale_two * mlp)).astype(jnp.bfloat16)
        grad_normed[0, r * pitch : r * pitch + breadth, :] = back
        grad_normed[0, r * pitch + breadth : (r + 1) * pitch, :] = jnp.zeros(
            (pitch - breadth, back.shape[1]), wide
        )
        grad = cot[0, r].astype(jnp.float32) * alive
        scale_grad += jnp.sum(grad * mlp, axis=0, keepdims=True)
        shift_grad += jnp.sum(back, axis=0, keepdims=True)
        gain_grad += jnp.sum(back * (first - mean_two) * rstd_two, axis=0, keepdims=True)
    sums[0:1, :] += shift_grad
    sums[1:2, :] += gain_grad
    scale_sum[...] += scale_grad

    @pl.when(image == pl.num_programs(0) - 1)
    def _():
        copies[...] = jnp.broadcast_to(sums[...][None], copies.shape)
        grad_fc[0 : 2 * groups] = in_sum[...].astype(low)
        grad_fc[2 * groups :] = out_sum[...].astype(low)
        store_taps(grad_taps, tap_sums, taps.shape[1])


def unpack_kernel(packed, grad_in, grad_out):
    groups = packed.shape[0] // 2
    for g in range(groups):
        grad_in[:, g * lanes : (g + 1) * lanes] = packed[g].astype(wide)
        grad_out[:, g * lanes : (g + 1) * lanes] = packed[groups + g].astype(wide)


def mlp_block(
    counts, first_sum, above, below, cot, cot_above, cot_below, params, stats, fc_in, fc_out, taps
):
    images, rows, breadth, width = cot.shape
    pitch = first_sum.shape[2]
    deep = fc_in.shape[1]
    groups = deep // lanes
    count = images * rows * breadth
    return call(
        mlp_kernel,
        images,
        [
            (counts, smem),
            (first_sum, spec_image(rows, pitch, width)),
            (above, spec_image(2, pitch, width)),
            (below, spec_image(2, pitch, width)),
            (cot, spec_image(rows, breadth, width)),
            (cot_above, spec_image(3, breadth, width)),
            (cot_below, spec_image(3, breadth, width)),
            (params, spec_whole(8, width)),
            (stats, spec_whole(*stats.shape)),
            (fc_in, spec_whole(width, deep)),
            (fc_out.T, spec_whole(width, deep)),
            (taps, spec_whole(9, deep)),
        ],
        [
            (cot.shape, low, spec_image(rows, breadth, width)),
            ((images, rows * pitch, width), wide, spec_image(rows * pitch, width)),
            (stats.shape, wide, spec_whole(*stats.shape)),
            ((1, width), wide, spec_whole(1, width)),
            ((2 * groups, width, lanes), low, spec_whole(2 * groups, width, lanes)),
            ((9, deep), wide, spec_whole(9, deep)),
        ],
        [
            ((2, width), wide),
            (((rows + 4) * pitch, width), wide),
            (((rows + 2) * pitch, width), wide),
            (((rows + 4) * pitch, width), low),
            ((width, rows * pitch), low),
            (((rows + 2) * pitch, width), low),
            ((width, rows * pitch), low),
            ((2, (rows + 4) * pitch + 16, lanes), wide),
            ((2, (rows + 4) * pitch + 16, lanes), wide),
            ((2, (rows + 2) * pitch, lanes), wide),
            ((2, (rows + 2) * pitch, lanes), wide),
            ((2, (rows + 2) * pitch + 16, lanes), wide),
            ((rows * pitch, 2 * lanes), wide),
            ((rows * pitch, 2 * lanes), wide),
            ((rows * pitch, 2 * lanes), wide),
            ((rows * pitch, 2 * lanes), wide),
            ((rows * pitch, width), wide),
            ((rows * pitch, width), wide),
            ((groups, 9, 8, lanes), wide),
            ((groups, 9, 8, lanes), wide),
            ((groups, width, lanes), wide),
            ((groups, width, lanes), wide),
        ],
        12 * count * width * deep,
        16 * count * width,
        "mlp",
        vmem=36,
        rows=rows,
        breadth=breadth,
        pitch=pitch,
    )


def body(
    images,
    counts,
    gain_one,
    shift_one,
    proj_in,
    kernel_five,
    kernel_seven,
    lka_proj,
    proj_out,
    scale_one,
    gain_two,
    shift_two,
    fc_in,
    kernel_three,
    fc_out,
    scale_two,
    cotangent,
):
    slots, rows, breadth, width = images.shape
    pitch = -(-(breadth + 2) // 8) * 8
    gap = -(-(breadth + 9) // 8) * 8
    flat = rows * pitch
    blank = jnp.zeros_like(gain_one)
    params = jnp.stack(
        [gain_one, shift_one, scale_one, gain_two, shift_two, scale_two, blank, blank]
    ).astype(wide)
    sizes = dict(rows=rows, breadth=breadth, pitch=pitch)
    vec = spec_whole(8, width)
    devices = device_count()
    blocks = (devices, 2, width)
    two = spec_whole(*blocks)
    square = spec_whole(width, width)
    image_spec = spec_image(rows, breadth, width)
    pairs = slots // 2
    chunks = [(0, pairs - 1), (pairs - 1, 1)]
    pair_width = 2 * width
    pair_square = spec_whole(pair_width, pair_width)
    pair_flat = (pairs, flat, pair_width)
    flat_spec = spec_image(flat, width)
    flat_shape = (slots, flat, width)
    row_shape = (slots, rows, pitch, width)
    groups = len(pair_groups(width))
    kinds = width // lanes + 1
    area = slots * rows * breadth
    matmul = 2 * area * width * width
    five_spec = spec_whole(*kernel_five.shape)
    seven_spec = spec_whole(*kernel_seven.shape)

    (first_part,) = call(
        stats_kernel,
        slots,
        [(counts, smem), (images, image_spec)],
        [(blocks, wide, two)],
        [((2, width), wide)],
        3 * area * width,
        2 * area * width,
        "input_sums",
    )
    pair_in, pair_lka, pair_out = (pair_matrix(m) for m in (proj_in, lka_proj, proj_out))
    last = jnp.concatenate([images[:, rows - 2 :], cotangent[:, rows - 1 :]], axis=1)
    first = jnp.concatenate([images[:, :2], cotangent[:, :1]], axis=1)
    first_part, last, first = lax.optimization_barrier((first_part, last, first))
    image_above, image_below = shifted(last, first)
    first_stats = from_all(first_part)
    gelu_low = pre_gelu = None
    mids, rims = [], []
    for start, count in chunks:
        part = matmul * count // pairs
        gelu_low, pre_gelu, mid = call(
            front_kernel,
            count,
            [
                (counts, smem),
                (images, spec_two(start, rows, breadth, width)),
                (image_above, spec_two(start, 3, breadth, width)),
                (image_below, spec_two(start, 3, breadth, width)),
                (params, vec),
                (first_stats, two),
                (pair_in, pair_square),
                (kernel_five, five_spec),
            ],
            [
                (pair_flat, low, spec_from(start, flat, pair_width), gelu_low),
                (pair_flat, low, spec_from(start, flat, pair_width), pre_gelu),
                ((count, rows, pitch, pair_width), low, spec_image(rows, pitch, pair_width)),
            ],
            [
                (((rows + 4) * pitch, pair_width), wide),
                ((groups, (rows + 4) * pitch + 16, lanes), wide),
                ((kinds, 25, 8, lanes), wide),
                (((rows + 4) * pitch, lanes), wide),
                ((flat, pair_width), wide),
            ],
            part,
            part // 40,
            f"normed_to_five_{start}",
            **sizes,
        )
        mids.append(mid)
        rims.append(neighbours(mid, rows))
    lka_low = attend = attn = first_sum = None
    second_part = jnp.zeros(blocks, wide)
    for (start, count), mid, (mid_above, mid_below) in zip(chunks, mids, rims):
        part = matmul * count // pairs
        rim_spec = spec_image(rows, pitch, pair_width)
        pair_spec = spec_from(start, flat, pair_width)
        lka_low, attend, attn, first_sum, second_part = call(
            attend_kernel,
            count,
            [
                (counts, smem),
                (images, spec_two(start, rows, breadth, width)),
                (mid, rim_spec),
                (mid_above, rim_spec),
                (mid_below, rim_spec),
                (gelu_low, pair_spec),
                (params, vec),
                (first_stats, two),
                (second_part, two),
                (pair_lka, pair_square),
                (pair_out, pair_square),
                (kernel_seven, seven_spec),
            ],
            [
                (pair_flat, low, pair_spec, lka_low),
                (pair_flat, low, pair_spec, attend),
                (pair_flat, low, pair_spec, attn),
                (flat_shape, wide, spec_two(start, flat, width), first_sum),
                (blocks, wide, two),
            ],
            [
                ((2, width), wide),
                ((groups, 3 * rows * gap + 48, lanes), wide),
                ((kinds, 49, 8, lanes), wide),
                ((flat, pair_width), wide),
                ((flat, pair_width), wide),
                ((flat, pair_width), wide),
            ],
            2 * part,
            part // 20,
            f"seven_to_first_sum_{start}",
            gap=gap,
            start_pair=start,
            **sizes,
        )
    first_rows = first_sum.reshape(row_shape)
    sum_above, sum_below = neighbours(first_rows, 2)
    second_stats = from_all(second_part)
    out_image, grad_normed_two, third_part, scale_two_part, grad_fc, grad_kernel_three = mlp_block(
        counts,
        first_rows,
        sum_above,
        sum_below,
        cotangent,
        image_above,
        image_below,
        params,
        second_stats,
        fc_in,
        fc_out,
        kernel_three,
    )
    grad_second = from_all(third_part)
    grad_first = grad_direct = None
    gates, rims = [], []
    lka_parts, out_parts, scale_parts = [], [], []
    for start, count in chunks:
        part = matmul * count // pairs
        pair_spec = spec_from(start, flat, pair_width)
        grad_first, grad_direct, grad_lka, lka_part, out_part, scale_part = call(
            gate_kernel,
            count,
            [
                (counts, smem),
                (first_sum, spec_two(start, flat, width)),
                (attn, pair_spec),
                (cotangent, spec_two(start, rows, breadth, width)),
                (grad_normed_two, spec_two(start, flat, width)),
                (lka_low, pair_spec),
                (attend, pair_spec),
                (gelu_low, pair_spec),
                (params, vec),
                (second_stats, two),
                (grad_second, two),
                (pair_lka, pair_square),
                (pair_out, pair_square),
            ],
            [
                (pair_flat, wide, pair_spec, grad_first),
                (pair_flat, low, pair_spec, grad_direct),
                ((count, rows, pitch, pair_width), low, spec_image(rows, pitch, pair_width)),
                ((width, width), wide, square),
                ((width, width), wide, square),
                ((1, width), wide, spec_whole(1, width)),
            ],
            [
                ((flat, pair_width), wide),
                ((flat, pair_width), wide),
            ],
            0,
            0,
            f"gate_backward_{start}",
            start_pair=start,
            **sizes,
        )
        gates.append(grad_lka)
        rims.append(neighbours(grad_lka, rows))
        lka_parts.append(lka_part)
        out_parts.append(out_part)
        scale_parts.append(scale_part)
    packed_shape = grad_fc.shape
    grad_fc = grad_fc.reshape(devices, -1, lanes)
    grad_fc, rims[-1] = lax.optimization_barrier((grad_fc, rims[-1]))
    fc_share = jnp.sum(from_all(grad_fc).astype(wide), axis=0).astype(low)
    grad_mid = None
    seven_parts = []
    for (start, count), grad_lka, mid, (lka_above, lka_below) in zip(chunks, gates, mids, rims):
        part = matmul * count // pairs
        rim_spec = spec_image(rows, pitch, pair_width)
        grad_mid, seven_part = call(
            seven_kernel,
            count,
            [
                (grad_lka, rim_spec),
                (lka_above, rim_spec),
                (lka_below, rim_spec),
                (mid, rim_spec),
                (kernel_seven, seven_spec),
            ],
            [
                (
                    (pairs, rows, pitch, pair_width),
                    low,
                    spec_from(start, rows, pitch, pair_width),
                    grad_mid,
                ),
                (kernel_seven.shape, wide, seven_spec),
            ],
            [
                ((groups, 3 * rows * gap + 48, lanes), wide),
                ((groups, flat, lanes), wide),
                ((flat, pair_width), wide),
                ((kinds, 49, 8, lanes), wide),
                ((kinds, 49, 8, lanes), wide),
            ],
            0,
            0,
            f"seven_backward_{start}",
            gap=gap,
            **sizes,
        )
        seven_parts.append(seven_part)
    five_above, five_below = neighbours(grad_mid, 2)
    fc_whole = lax.all_gather(fc_share, ("dp", "strip"), tiled=True)
    pair_spec = spec_image(flat, pair_width)
    grad_partial, grad_proj_in, grad_kernel_five, last_sums = call(
        five_kernel,
        pairs,
        [
            (counts, smem),
            (images, spec_two(0, rows, breadth, width)),
            (grad_mid, spec_image(rows, pitch, pair_width)),
            (five_above, spec_image(2, pitch, pair_width)),
            (five_below, spec_image(2, pitch, pair_width)),
            (gelu_low, pair_spec),
            (pre_gelu, pair_spec),
            (grad_direct, pair_spec),
            (grad_first, pair_spec),
            (params, vec),
            (first_stats, two),
            (pair_in, pair_square),
            (kernel_five, five_spec),
        ],
        [
            (flat_shape, wide, spec_two(0, flat, width)),
            ((width, width), wide, square),
            (kernel_five.shape, wide, five_spec),
            ((2, width), wide, spec_whole(2, width)),
        ],
        [
            ((groups, (rows + 4) * pitch + 16, lanes), wide),
            ((groups, flat, lanes), wide),
            ((flat, pair_width), wide),
            ((kinds, 25, 8, lanes), wide),
            ((kinds, 25, 8, lanes), wide),
            ((flat, pair_width), wide),
            ((flat, pair_width), wide),
        ],
        0,
        0,
        "five_backward",
        **sizes,
    )
    blank = jnp.zeros((4, width), wide)
    share, vectors = split_sums(
        jnp.concatenate(
            [
                grad_proj_in,
                sum(lka_parts),
                sum(out_parts),
                grad_kernel_five,
                sum(seven_parts),
                grad_kernel_three.reshape(-1, width),
                jnp.zeros((-(3 * width + 110) % 64, width), wide),
            ]
        ).astype(low),
        jnp.concatenate([last_sums, sum(scale_parts), scale_two_part, blank]).astype(low),
    )
    matrices = joined(share)
    ends = [0]
    for count in (width, width, width, 25, 49, 36):
        ends.append(ends[-1] + count)
    pieces = [matrices[i:j] for i, j in zip(ends, ends[1:])]
    (grad_images,) = call(
        last_kernel,
        slots,
        [
            (counts, smem),
            (images, image_spec),
            (grad_partial, flat_spec),
            (params, vec),
            (first_stats, two),
            (vectors, spec_whole(8, width)),
        ],
        [(images.shape, wide, image_spec)],
        [],
        6 * area * width,
        10 * area * width,
        "input_gradient",
        **sizes,
    )
    deep = fc_in.shape[1]
    grad_fc_in, grad_fc_out = call(
        unpack_kernel,
        1,
        [(fc_whole.reshape(packed_shape), spec_whole(*packed_shape))],
        [
            ((width, deep), wide, spec_whole(width, deep)),
            ((width, deep), wide, spec_whole(width, deep)),
        ],
        [],
        0,
        6 * width * deep,
        "weight_gradients",
    )
    vectors = vectors.astype(wide)
    grad_second = jnp.sum(grad_second, axis=0)
    return (
        out_image,
        grad_images,
        vectors[1],
        vectors[0],
        pieces[0],
        pieces[3],
        pieces[4],
        pieces[1],
        pieces[2],
        vectors[2],
        grad_second[1],
        grad_second[0],
        grad_fc_in,
        pieces[5].reshape(9, -1),
        grad_fc_out.T,
        vectors[3],
    )


def solution(mesh):
    split = P("dp", "strip", None, None)
    return jax.shard_map(
        body,
        mesh=mesh,
        in_specs=(split,) + (P(),) * 15 + (split,),
        out_specs=(split, split) + (P(),) * 14,
        check_vma=False,
    )
```

```python
import functools

import jax
import jax.numpy as jnp
from jax import lax
from jax.experimental import pallas as pl
from jax.experimental.pallas import tpu as pltpu
from jax.sharding import PartitionSpec as P

epsilon = 1e-05
lanes = 128
smem = pl.BlockSpec(memory_space=pltpu.SMEM)
wide = jnp.float32
low = jnp.bfloat16


def exchange_steps():
    return [
        (axis, 1 << bit)
        for axis in ("strip", "dp")
        for bit in range(lax.axis_size(axis).bit_length() - 1)
    ]


def swapped(value, axis, bit):
    return lax.ppermute(value, axis, [(i, i ^ bit) for i in range(lax.axis_size(axis))])


def device_count():
    return lax.axis_size("dp") * lax.axis_size("strip")


def from_all(copies):
    return lax.all_to_all(copies, ("dp", "strip"), 0, 0)


def split_sums(part, size):
    for place, (axis, bit) in enumerate(exchange_steps()):
        length = part.shape[0] - size
        if place < 3:
            upper = (lax.axis_index(axis) // bit) % 2
            tail = part[length:]
            halves = part[:length].reshape((2, length // 2) + part.shape[1:])
            sent = lax.dynamic_index_in_dim(halves, 1 - upper, 0, False)
            kept = lax.dynamic_index_in_dim(halves, upper, 0, False)
            sent, part = jnp.concatenate([sent, tail]), jnp.concatenate([kept, tail])
        else:
            sent = part
        got = swapped(sent, axis, bit)
        part = (part.astype(wide) + got.astype(wide)).astype(low)
    return part[: part.shape[0] - size], part[part.shape[0] - size :]


def joined(part):
    for axis, bit in reversed(exchange_steps()[:3]):
        upper = (lax.axis_index(axis) // bit) % 2
        got = swapped(part, axis, bit)
        part = jnp.where(
            upper == 0, jnp.concatenate([part, got]), jnp.concatenate([got, part])
        )
    return part


def far_and_near(far, near):
    count = lax.axis_size("strip")
    pairs = [(i, i + 1) for i in range(1, count - 1, 2)]
    return (
        lax.ppermute(far, "strip", pairs + [(j, i) for i, j in pairs]),
        lax.ppermute(near, "strip", [(i, i ^ 1) for i in range(count)]),
    )


def edge_rows(value, width):
    odd = lax.axis_index("strip") % 2
    length = value.shape[1] - width
    return (
        lax.dynamic_slice_in_dim(value, odd * length, width, 1),
        lax.dynamic_slice_in_dim(value, (1 - odd) * length, width, 1),
    )


def sides(length):
    odd = lax.axis_index("strip") % 2
    return odd * length, (1 - odd) * length


def present():
    strip, count = lax.axis_index("strip"), lax.axis_size("strip")
    above, below = (strip > 0).astype(wide), (strip < count - 1).astype(wide)
    odd = (strip % 2).astype(wide)
    return odd * below + (1 - odd) * above, odd * above + (1 - odd) * below


def normal_parts(x):
    density = jnp.exp2(x * x * -0.7213475204444817 - 1.3257480647361595)
    scale = 1.0 + 0.2316419 * jnp.abs(x)
    guess = pl.reciprocal(scale, approx=True)
    t = guess * (2.0 - scale * guess)
    poly = 1.781477937 + t * (-1.821255978 + t * 1.330274429)
    poly = t * (0.319381530 + t * (-0.356563782 + t * poly))
    tail = density * poly
    return jnp.where(x > 0, 1.0 - tail, tail), density


def window_sums(load, weight, across, spread, rows, back, center=None, add_tap=None):
    total = [None] * rows
    reach = spread * (across - 1)
    for j in range(across):
        shift = (j - across // 2) * spread * (-1 if back else 1)
        w = [weight(i * across + j) for i in range(across)]
        tap = [None] * across
        for r in range(rows + reach):
            v = load(r, shift)
            for i in range(across):
                o = r - reach + spread * i if back else r - spread * i
                if 0 <= o < rows:
                    term = v * w[i]
                    total[o] = term if total[o] is None else total[o] + term
                    if center is not None:
                        term = v * center[o]
                        tap[i] = term if tap[i] is None else tap[i] + term
        if center is not None:
            for i in range(across):
                add_tap(i * across + j, tap[i])
    return total


def lane_groups(width):
    return [(start, min(lanes, width - start)) for start in range(0, width, lanes)]


def fill_weights(weights, taps, width):
    weights[...] = jnp.zeros_like(weights)
    for g, (start, size) in enumerate(lane_groups(width)):
        for t in range(taps.shape[0]):
            weights[g, t, :, 0:size] = jnp.broadcast_to(
                taps[t : t + 1, start : start + size].astype(wide), (8, size)
            )


def store_taps(grad_taps, tap_sums, width):
    for g, (start, size) in enumerate(lane_groups(width)):
        for t in range(grad_taps.shape[0]):
            grad_taps[t : t + 1, start : start + size] = jnp.sum(
                tap_sums[g, t, :, 0:size], axis=0, keepdims=True
            )


def inside(rows, pitch, breadth, width):
    place = lax.broadcasted_iota(jnp.int32, (rows, pitch, width), 1)
    return jnp.where(place < breadth, 1.0, 0.0).reshape(rows * pitch, width)


def live_here(counts):
    return counts[lax.axis_index("dp")]


def pixels_of(counts, area):
    total = counts[0]
    for k in range(1, counts.shape[0]):
        total += counts[k]
    return total.astype(wide) * (area * lax.axis_size("strip"))


def norm_of(blocks, pixels):
    stats = jnp.sum(blocks[...], axis=0) / pixels
    mean = stats[0:1, :]
    return mean, lax.rsqrt(stats[1:2, :] - mean * mean + epsilon)


def spec_image(*shape):
    return pl.BlockSpec((1,) + shape, lambda i: (i,) + (0,) * len(shape))


def spec_from(start, *shape):
    return pl.BlockSpec((1,) + shape, lambda i: (i + start,) + (0,) * len(shape))


def spec_two(start, *shape):
    return pl.BlockSpec((2,) + shape, lambda i: (i + start,) + (0,) * len(shape))


def spec_whole(*shape):
    return pl.BlockSpec(shape, lambda i: (0,) * len(shape))


def call(kernel, steps, ins, outs, scratch, cost, name, vmem=44, **sizes):
    earlier = [out[3] for out in outs if len(out) > 3 and out[3] is not None]
    aliases, at = {}, len(ins)
    for place, out in enumerate(outs):
        if len(out) > 3 and out[3] is not None:
            aliases[at] = place
            at += 1

    def run(*refs):
        kernel(*refs[: len(ins)], *refs[at:], **sizes)

    return pl.pallas_call(
        run,
        grid=(steps,),
        in_specs=[spec for _, spec in ins] + [pl.BlockSpec(memory_space=pl.ANY)] * len(earlier),
        out_specs=[out[2] for out in outs],
        out_shape=[jax.ShapeDtypeStruct(out[0], out[1]) for out in outs],
        scratch_shapes=[pltpu.VMEM(shape, dtype) for shape, dtype in scratch],
        input_output_aliases=aliases,
        compiler_params=pltpu.CompilerParams(vmem_limit_bytes=vmem * 1024 * 1024),
        cost_estimate=pl.CostEstimate(
            flops=0, bytes_accessed=int(cost * 3.5e6), transcendentals=0
        ),
        name=name,
    )(*[array for array, _ in ins], *earlier)


def paired(value):
    return pair_lanes(value, value)


def pair_lanes(left, right):
    main = left.shape[-1] // lanes * lanes
    tails = jnp.concatenate([left[..., main:], right[..., main:]], axis=-1)
    return jnp.concatenate([left[..., :main], right[..., :main], tails], axis=-1)


def split_lanes(value):
    width = value.shape[-1] // 2
    main = width // lanes * lanes
    left = jnp.concatenate([value[..., :main], value[..., 2 * main : main + width]], axis=-1)
    right = jnp.concatenate([value[..., main : 2 * main], value[..., main + width :]], axis=-1)
    return left, right


def folded(value):
    left, right = split_lanes(value)
    return left + right


def folded_square(value):
    width = value.shape[0] // 2
    main = width // lanes * lanes
    left = split_lanes(jnp.concatenate([value[:main], value[2 * main : main + width]], axis=0))[0]
    right = split_lanes(jnp.concatenate([value[main : 2 * main], value[main + width :]], axis=0))[1]
    return left + right


def pair_matrix(matrix):
    blank = jnp.zeros_like(matrix)
    left = jnp.concatenate([matrix, blank], axis=1)
    right = jnp.concatenate([blank, matrix], axis=1)
    width = matrix.shape[0]
    main = width // lanes * lanes

    def columns(value):
        return jnp.concatenate(
            [
                value[:, :main],
                value[:, width : width + main],
                value[:, main:width],
                value[:, width + main :],
            ],
            axis=1,
        )

    left, right = columns(left), columns(right)
    return jnp.concatenate([left[:main], right[:main], left[main:], right[main:]])


def pair_groups(width):
    main = width // lanes
    return [(g * lanes, g % main) for g in range(2 * main)] + [(2 * main * lanes, main)]


def fill_pair_weights(weights, taps, width):
    main = width // lanes * lanes
    for t in range(taps.shape[0]):
        row = taps[t : t + 1, :].astype(wide)
        tail = row[:, main:]
        for g in range(main // lanes):
            weights[g, t] = jnp.broadcast_to(row[:, g * lanes : (g + 1) * lanes], (8, lanes))
        weights[main // lanes, t] = jnp.broadcast_to(
            jnp.concatenate([tail, tail], axis=1), (8, lanes)
        )


def store_pair_taps(grad_taps, tap_sums, width):
    main = width // lanes * lanes
    for t in range(grad_taps.shape[0]):
        for g in range(main // lanes):
            grad_taps[t : t + 1, g * lanes : (g + 1) * lanes] = jnp.sum(
                tap_sums[g, t], axis=0, keepdims=True
            )
        tail = jnp.sum(tap_sums[main // lanes, t], axis=0, keepdims=True)
        grad_taps[t : t + 1, main:width] = tail[:, : width - main] + tail[:, width - main :]


def alive_lanes(counts, start, width):
    main = width // lanes * lanes
    image = 2 * (pl.program_id(0) + start)
    at = lax.broadcasted_iota(jnp.int32, (1, 2 * width), 1)
    second = ((at >= main) & (at < 2 * main)) | (at >= main + width)
    return jnp.where(image + second.astype(jnp.int32) < live_here(counts), 1.0, 0.0)


def stats_kernel(counts, images, copies, sums):
    image = pl.program_id(0)

    @pl.when(image == 0)
    def _():
        sums[...] = jnp.zeros_like(sums)

    alive = (image < live_here(counts)).astype(wide)
    total = jnp.zeros((images.shape[2], images.shape[3]), wide)
    square = total
    for r in range(images.shape[1]):
        value = images[0, r].astype(wide)
        total += value
        square += value * value
    sums[0:1, :] += jnp.sum(total, axis=0, keepdims=True) * alive
    sums[1:2, :] += jnp.sum(square, axis=0, keepdims=True) * alive

    @pl.when(image == pl.num_programs(0) - 1)
    def _():
        copies[...] = jnp.broadcast_to(sums[...][None], copies.shape)


def front_kernel(
    counts,
    images,
    far,
    near,
    params,
    stats,
    proj_in,
    taps,
    gelu_low,
    pre_gelu,
    lka_mid,
    cot_far,
    cot_near,
    values,
    gelu,
    weights,
    mask,
    mid,
    *,
    rows,
    breadth,
    pitch,
):
    width = images.shape[3]
    pixels = pixels_of(counts, rows * breadth)
    mean, rstd = norm_of(stats, pixels)
    mean, rstd = paired(mean), paired(rstd)
    gain, shift = paired(params[0:1, :]), paired(params[1:2, :])

    @pl.when(pl.program_id(0) == 0)
    def _():
        values[...] = jnp.zeros_like(values)
        gelu[...] = jnp.zeros_like(gelu)
        fill_pair_weights(weights, taps, width)
        mask[...] = inside(rows + 4, pitch, breadth, lanes)
        for offset, there in zip(sides((rows + 2) * pitch), present()):
            at = pl.ds(pl.multiple_of(offset, 8), 2 * pitch)
            mask[at, :] = mask[at, :] * there

    def place(at, source, r):
        value = pair_lanes(source[0, r].astype(wide), source[1, r].astype(wide))
        values[pl.ds(at, breadth), :] = (value - mean) * rstd * gain + shift

    for k in range(2):
        cot_far[k, 0] = far[k, 2]
        cot_near[k, 0] = near[k, 2]
    for source, offset in zip((far, near), sides((rows + 2) * pitch)):
        for r in range(2):
            place(pl.multiple_of(offset + r * pitch, 8), source, r)
    for r in range(rows):
        place((r + 2) * pitch, images, r)
    pre = jnp.dot(values[...].astype(low), proj_in[...], preferred_element_type=wide)
    pre_gelu[0] = pre[2 * pitch : (rows + 2) * pitch, :].astype(low)
    for g, (start, _) in enumerate(pair_groups(width)):
        part = pre[:, start : start + lanes]
        cdf, _ = normal_parts(part)
        rounded = (part * cdf * mask[...]).astype(low).astype(wide)
        gelu_low[0, :, start : start + lanes] = rounded[2 * pitch : (rows + 2) * pitch].astype(low)
        gelu[g, 8 : 8 + (rows + 4) * pitch, :] = rounded
    for g, (start, which) in enumerate(pair_groups(width)):

        def step(block, carry, g=g, start=start, which=which):
            base = pl.multiple_of(block * 8, 8)
            total = window_sums(
                lambda r, s: gelu[g, pl.ds(base + (8 + r * pitch + s), 8), :],
                lambda t: weights[which, t],
                5,
                1,
                rows,
                False,
            )
            for o in range(rows):
                mid[pl.ds(base + o * pitch, 8), start : start + lanes] = total[o]
            return carry

        lax.fori_loop(0, pitch // 8, step, 0)
    for r in range(rows):
        at = r * pitch
        lka_mid[0, r] = (
            mid[at : at + pitch, :] * inside(1, pitch, breadth, 2 * width)
        ).astype(low)


def attend_kernel(
    counts,
    images,
    lka_mid,
    far,
    near,
    gelu_low,
    params,
    stats,
    earlier_sums,
    lka_proj,
    proj_out,
    taps,
    lka_low,
    attend_out,
    attn_out,
    first_sum,
    copies,
    sums,
    window,
    weights,
    lka,
    values,
    mask,
    *,
    rows,
    breadth,
    pitch,
    gap,
    start_pair,
):
    width = images.shape[3]
    alive = alive_lanes(counts, start_pair, width)
    pixels = pixels_of(counts, rows * breadth)
    mean, rstd = norm_of(stats, pixels)
    mean, rstd = paired(mean), paired(rstd)
    gain, shift, scale = (paired(params[k : k + 1, :]) for k in range(3))

    @pl.when(pl.program_id(0) == 0)
    def _():
        window[...] = jnp.zeros_like(window)
        values[...] = jnp.zeros_like(values)
        sums[...] = earlier_sums[0]
        fill_pair_weights(weights, taps, width)
        mask[...] = inside(rows, pitch, breadth, 2 * width)

    far_at, near_at = sides(2 * rows * gap)
    for offset, source in ((far_at, far), (rows * gap, lka_mid), (near_at, near)):
        for r in range(rows):
            at = pl.ds(pl.multiple_of(offset + (16 + r * gap), 8), pitch)
            for g, (start, _) in enumerate(pair_groups(width)):
                window[g, at, :] = source[0, r, :, start : start + lanes].astype(wide)
    for g, (start, which) in enumerate(pair_groups(width)):

        def step(block, carry, g=g, start=start, which=which):
            base = pl.multiple_of(block * 8, 8)
            total = window_sums(
                lambda r, s: window[g, pl.ds(base + (16 + r * gap + s), 8), :],
                lambda t: weights[which, t],
                7,
                3,
                rows,
                False,
            )
            for o in range(rows):
                lka[pl.ds(base + o * pitch, 8), start : start + lanes] = total[o]
            return carry

        lax.fori_loop(0, pitch // 8, step, 0)
    for r in range(rows):
        values[r * pitch : r * pitch + breadth, :] = pair_lanes(
            images[0, r].astype(wide), images[1, r].astype(wide)
        )
    low_lka = lka[...].astype(low)
    lka_low[0] = low_lka
    attend = jnp.dot(low_lka, lka_proj[...], preferred_element_type=wide)
    attend_out[0] = attend.astype(low)
    gated = (gelu_low[0].astype(wide) * attend).astype(low)
    branch = jnp.dot(gated, proj_out[...], preferred_element_type=wide)
    attn = (branch + ((values[...] - mean) * rstd * gain + shift)) * mask[...]
    attn_out[0] = attn.astype(low)
    first = values[...] + scale * attn
    first_sum[0], first_sum[1] = split_lanes(first)
    sums[0:1, :] += folded(jnp.sum(first, axis=0, keepdims=True) * alive)
    sums[1:2, :] += folded(jnp.sum(first * first, axis=0, keepdims=True) * alive)

    @pl.when(pl.program_id(0) == pl.num_programs(0) - 1)
    def _():
        copies[...] = jnp.broadcast_to(sums[...][None], copies.shape)


def gate_kernel(
    counts,
    first_sum,
    attn,
    cot,
    grad_normed,
    lka_low,
    attend,
    gelu_low,
    params,
    stats,
    grad_stats,
    lka_proj,
    proj_out,
    lka_before,
    out_before,
    scale_before,
    grad_first,
    grad_direct,
    grad_lka,
    grad_lka_proj,
    grad_proj_out,
    sums,
    values,
    mask,
    *,
    rows,
    breadth,
    pitch,
    start_pair,
):
    width = cot.shape[3]
    alive = alive_lanes(counts, start_pair, width)
    pixels = pixels_of(counts, rows * breadth)
    mean, rstd = norm_of(stats, pixels)
    mean, rstd = paired(mean), paired(rstd)
    scale, gain = paired(params[2:3, :]), paired(params[3:4, :])
    grad_sums = jnp.sum(grad_stats[...], axis=0)
    shift_sum, gain_sum = paired(grad_sums[0:1, :]), paired(grad_sums[1:2, :])

    @pl.when(pl.program_id(0) == 0)
    def _():
        values[...] = jnp.zeros_like(values)
        mask[...] = inside(rows, pitch, breadth, 2 * width)
        sums[...] = scale_before[...]
        grad_lka_proj[...] = lka_before[...]
        grad_proj_out[...] = out_before[...]

    for r in range(rows):
        values[r * pitch : r * pitch + breadth, :] = pair_lanes(
            cot[0, r].astype(wide), cot[1, r].astype(wide)
        )
    yhat = (pair_lanes(first_sum[0], first_sum[1]) - mean) * rstd
    inner = pair_lanes(grad_normed[0], grad_normed[1]) - (shift_sum + yhat * gain_sum) / pixels
    first = alive * (values[...] + rstd * gain * inner) * mask[...]
    grad_first[0] = first
    sums[...] += folded(jnp.sum(first * attn[0].astype(wide), axis=0, keepdims=True))
    branch = (first * scale).astype(low)
    gated_back = lax.dot_general(
        branch, proj_out[...], (((1,), (1,)), ((), ())), preferred_element_type=wide
    )
    gelu = gelu_low[0].astype(wide)
    attended = attend[0].astype(wide)
    gated = gelu * attended
    grad_proj_out[...] += folded_square(
        jnp.dot(gated.T.astype(low), branch, preferred_element_type=wide)
    )
    grad_direct[0] = (gated_back * attended).astype(low)
    back = (gated_back * gelu).astype(low)
    lka = lax.dot_general(
        back, lka_proj[...], (((1,), (1,)), ((), ())), preferred_element_type=wide
    )
    grad_lka_proj[...] += folded_square(
        jnp.dot(lka_low[0].astype(wide).T.astype(low), back, preferred_element_type=wide)
    )
    for r in range(rows):
        grad_lka[0, r] = lka[r * pitch : (r + 1) * pitch, :].astype(low)


def seven_kernel(
    grad_lka,
    far,
    near,
    lka_mid,
    taps,
    taps_before,
    grad_mid,
    grad_taps,
    window,
    middle,
    out,
    weights,
    tap_sums,
    *,
    rows,
    breadth,
    pitch,
    gap,
):
    width = taps.shape[1]

    @pl.when(pl.program_id(0) == 0)
    def _():
        window[...] = jnp.zeros_like(window)
        tap_sums[...] = jnp.zeros_like(tap_sums)
        fill_pair_weights(weights, taps, width)

    far_at, near_at = sides(2 * rows * gap)
    for g, (start, _) in enumerate(pair_groups(width)):
        for offset, source in ((far_at, far), (rows * gap, grad_lka), (near_at, near)):
            for r in range(rows):
                at = pl.ds(pl.multiple_of(offset + (16 + r * gap), 8), pitch)
                window[g, at, :] = source[0, r, :, start : start + lanes].astype(wide)
        for r in range(rows):
            middle[g, r * pitch : (r + 1) * pitch, :] = lka_mid[
                0, r, :, start : start + lanes
            ].astype(wide)
    for g, (start, which) in enumerate(pair_groups(width)):

        def step(block, carry, g=g, start=start, which=which):
            base = pl.multiple_of(block * 8, 8)

            def add_tap(t, value):
                tap_sums[which, t] += value

            total = window_sums(
                lambda r, s: window[g, pl.ds(base + (16 + r * gap + s), 8), :],
                lambda t: weights[which, t],
                7,
                3,
                rows,
                True,
                [middle[g, pl.ds(base + p * pitch, 8), :] for p in range(rows)],
                add_tap,
            )
            for o in range(rows):
                out[pl.ds(base + o * pitch, 8), start : start + lanes] = total[o]
            return carry

        lax.fori_loop(0, pitch // 8, step, 0, unroll=True)
    for r in range(rows):
        at = r * pitch
        grad_mid[0, r] = (
            out[at : at + pitch, :] * inside(1, pitch, breadth, 2 * width)
        ).astype(low)

    @pl.when(pl.program_id(0) == pl.num_programs(0) - 1)
    def _():
        store_pair_taps(grad_taps, tap_sums, width)
        grad_taps[...] += taps_before[...]


def five_kernel(
    counts,
    images,
    grad_mid,
    far,
    near,
    gelu_low,
    pre_gelu,
    grad_direct,
    grad_first,
    params,
    stats,
    proj_in,
    taps,
    lka_sum,
    out_sum,
    seven_sum,
    three_sum,
    scale_one,
    scale_two,
    grad_partial,
    packed,
    grad_proj_in,
    grad_taps,
    sums,
    pack,
    window,
    middle,
    out,
    weights,
    tap_sums,
    values,
    mask,
    *,
    rows,
    breadth,
    pitch,
):
    width = images.shape[3]
    alive = alive_lanes(counts, 0, width)
    pixels = pixels_of(counts, rows * breadth)
    mean, rstd = norm_of(stats, pixels)
    mean, rstd = paired(mean), paired(rstd)
    gain, shift, scale = (paired(params[k : k + 1, :]) for k in range(3))

    @pl.when(pl.program_id(0) == 0)
    def _():
        window[...] = jnp.zeros_like(window)
        tap_sums[...] = jnp.zeros_like(tap_sums)
        values[...] = jnp.zeros_like(values)
        sums[...] = jnp.zeros_like(sums)
        grad_proj_in[...] = jnp.zeros_like(grad_proj_in)
        mask[...] = inside(rows, pitch, breadth, 2 * width)
        fill_pair_weights(weights, taps, width)

    for g, (start, _) in enumerate(pair_groups(width)):
        for source, offset in zip((far, near), sides((rows + 2) * pitch)):
            for r in range(2):
                at = pl.ds(pl.multiple_of(offset + (8 + r * pitch), 8), pitch)
                window[g, at, :] = source[0, r, :, start : start + lanes].astype(wide)
        for r in range(rows):
            at = 8 + (r + 2) * pitch
            window[g, at : at + pitch, :] = grad_mid[0, r, :, start : start + lanes].astype(wide)
        middle[g] = gelu_low[0, :, start : start + lanes].astype(wide)
    for g, (start, which) in enumerate(pair_groups(width)):

        def step(block, carry, g=g, start=start, which=which):
            base = pl.multiple_of(block * 8, 8)

            def add_tap(t, value):
                tap_sums[which, t] += value

            total = window_sums(
                lambda r, s: window[g, pl.ds(base + (8 + r * pitch + s), 8), :],
                lambda t: weights[which, t],
                5,
                1,
                rows,
                True,
                [middle[g, pl.ds(base + p * pitch, 8), :] for p in range(rows)],
                add_tap,
            )
            for o in range(rows):
                out[pl.ds(base + o * pitch, 8), start : start + lanes] = total[o]
            return carry

        lax.fori_loop(0, pitch // 8, step, 0, unroll=True)
    for r in range(rows):
        values[r * pitch : r * pitch + breadth, :] = pair_lanes(
            images[0, r].astype(wide), images[1, r].astype(wide)
        )
    pre = pre_gelu[0].astype(wide)
    cdf, density = normal_parts(pre)
    grad_pre = ((grad_direct[0].astype(wide) + out[...]) * (cdf + pre * density)).astype(low)
    xhat = (values[...] - mean) * rstd
    normed = (xhat * gain + shift) * mask[...]
    grad_proj_in[...] += folded_square(
        jnp.dot(normed.T.astype(low), grad_pre, preferred_element_type=wide)
    )
    back = lax.dot_general(
        grad_pre, proj_in[...], (((1,), (1,)), ((), ())), preferred_element_type=wide
    )
    first = grad_first[0]
    grad_normed = (first * scale + back) * mask[...]
    sums[0:1, :] += folded(jnp.sum(grad_normed, axis=0, keepdims=True))
    sums[1:2, :] += folded(jnp.sum(grad_normed * xhat, axis=0, keepdims=True))
    grad_partial[0], grad_partial[1] = split_lanes(first + alive * rstd * gain * grad_normed)

    @pl.when(pl.program_id(0) == pl.num_programs(0) - 1)
    def _():
        store_pair_taps(grad_taps, tap_sums, width)
        pack[...] = jnp.zeros_like(pack)
        at = 0
        for part in (grad_proj_in, lka_sum, out_sum, grad_taps, seven_sum):
            pack[at : at + part.shape[0], :] = part[...]
            at += -(-part.shape[0] // 8) * 8
        for k in range(three_sum.shape[1] // width):
            pack[at : at + 9, :] = three_sum[:, k * width : (k + 1) * width]
            at += 9
        at = pack.shape[0] - 8
        pack[at : at + 2, :] = sums[...]
        pack[at + 2 : at + 3, :] = scale_one[...]
        pack[at + 3 : at + 4, :] = scale_two[...]
        packed[...] = pack[...].astype(low)


def pack_rows(width, deep):
    return -(-(3 * width + 32 + 56 + 9 * (deep // width)) // 64) * 64


def spread_kernel(packed, grad_in, grad_lka, grad_out, grad_five, grad_seven, grad_three):
    width = packed.shape[1]
    at = 0
    for part in (grad_in, grad_lka, grad_out, grad_five, grad_seven):
        size = -(-part.shape[0] // 8) * 8
        part[...] = packed[at : at + size, :].astype(wide)[: part.shape[0]]
        at += size
    rest = packed[at:, :].astype(wide)
    for k in range(grad_three.shape[1] // width):
        grad_three[:, k * width : (k + 1) * width] = rest[9 * k : 9 * k + 9]


def last_kernel(
    counts, images, grad_partial, params, stats, grad_stats, grad_images, *, rows, breadth, pitch
):
    alive = (pl.program_id(0) < live_here(counts)).astype(wide)
    pixels = pixels_of(counts, rows * breadth)
    mean, rstd = norm_of(stats, pixels)
    factor = alive * rstd * params[0:1, :] / pixels
    grad_sums = grad_stats[...].astype(wide)
    shift_sum, gain_sum = grad_sums[0:1, :], grad_sums[1:2, :]
    for r in range(rows):
        xhat = (images[0, r].astype(wide) - mean) * rstd
        part = grad_partial[0, r * pitch : r * pitch + breadth, :]
        grad_images[0, r] = part - factor * (shift_sum + xhat * gain_sum)


def mlp_kernel(
    counts,
    first_sum,
    far,
    near,
    cot,
    cot_far,
    cot_near,
    params,
    stats,
    fc_in,
    fc_out,
    taps,
    out_image,
    grad_normed,
    copies,
    scale_sum,
    grad_fc,
    grad_taps,
    sums,
    normed_wide,
    mlp_wide,
    normed_low,
    normed_turned,
    grads_low,
    grads_turned,
    hidden_even,
    hidden_odd,
    active_even,
    active_odd,
    grad_mixed,
    low_even,
    low_odd,
    back_even,
    back_odd,
    mlp_sum,
    normed_sum,
    weights,
    tap_sums,
    in_sum,
    out_sum,
    *,
    rows,
    breadth,
    pitch,
):
    image = pl.program_id(0)
    alive = (image < live_here(counts)).astype(jnp.float32)
    groups = fc_in.shape[1] // (2 * lanes)
    blocks = pitch // 8
    pixels = pixels_of(counts, rows * breadth)
    mean_two, rstd_two = norm_of(stats, pixels)
    gain_two, shift_two, scale_two = params[3:4, :], params[4:5, :], params[5:6, :]

    @pl.when(image == 0)
    def _():
        normed_wide[...] = jnp.zeros_like(normed_wide)
        mlp_wide[...] = jnp.zeros_like(mlp_wide)
        hidden_even[...] = jnp.zeros_like(hidden_even)
        hidden_odd[...] = jnp.zeros_like(hidden_odd)
        grad_mixed[...] = jnp.zeros_like(grad_mixed)
        tap_sums[...] = jnp.zeros_like(tap_sums)
        in_sum[...] = jnp.zeros_like(in_sum)
        out_sum[...] = jnp.zeros_like(out_sum)
        sums[...] = jnp.zeros_like(sums)
        scale_sum[...] = jnp.zeros_like(scale_sum)
        fill_weights(weights, taps, taps.shape[1])

    def normalized(value):
        return (value - mean_two) * rstd_two * gain_two + shift_two

    for source, offset, there in zip((far, near), sides((rows + 2) * pitch), present()):
        for r in range(2):
            at = pl.ds(pl.multiple_of(offset + r * pitch, 8), breadth)
            normed_wide[at, :] = there * normalized(source[0, r, 0:breadth, :])
    for r in range(rows):
        at = (r + 2) * pitch
        normed_wide[at : at + breadth, :] = normalized(first_sum[0, r, 0:breadth, :])
        at = (r + 1) * pitch
        mlp_wide[at : at + breadth, :] = cot[0, r].astype(jnp.float32) * alive * scale_two
    for source, offset in zip((cot_far, cot_near), sides((rows + 1) * pitch)):
        at = pl.ds(pl.multiple_of(offset, 8), breadth)
        mlp_wide[at, :] = source[0, 0].astype(wide) * alive * scale_two
    normed_low[...] = normed_wide[...].astype(jnp.bfloat16)
    grads_low[...] = mlp_wide[...].astype(jnp.bfloat16)
    inner = normed_wide[2 * pitch : (rows + 2) * pitch, :]
    normed_turned[...] = inner.T.astype(jnp.bfloat16)
    grads_turned[...] = mlp_wide[pitch : (rows + 1) * pitch, :].T.astype(jnp.bfloat16)
    mlp_sum[...] = jnp.zeros_like(mlp_sum)
    normed_sum[...] = jnp.zeros_like(normed_sum)

    hiddens, sources = (hidden_even, hidden_odd), (active_even, active_odd)
    actives, backs = (low_even, low_odd), (back_even, back_odd)

    def columns(group):
        return slice(group * 2 * lanes, (group + 1) * 2 * lanes)

    def enter(group):
        hid = jnp.dot(normed_low[...], fc_in[:, columns(group)], preferred_element_type=wide)
        hid = hid.astype(low).astype(wide)
        act = jnp.dot(grads_low[...], fc_out[:, columns(group)], preferred_element_type=wide)
        for half in range(2):
            lane = slice(half * lanes, (half + 1) * lanes)
            hiddens[group % 2][half, 8 : 8 + (rows + 4) * pitch, :] = hid[:, lane]
            sources[group % 2][half] = act[:, lane]

    def forward(group, half, block):
        hidden, source, active = (refs[group % 2] for refs in (hiddens, sources, actives))
        lane = slice(half * lanes, (half + 1) * lanes)
        place, base = group * 2 + half, block * 8
        mixed = window_sums(
            lambda r, s: hidden[half, pl.ds(base + (8 + r * pitch + s), 8), :],
            lambda t: weights[place, t],
            3,
            1,
            rows + 2,
            False,
        )
        for o in range(rows + 2):
            x = mixed[o]
            cdf, density = normal_parts(x)
            slope = cdf + x * density
            grad_mixed[half, pl.ds(base + (8 + o * pitch), 8), :] = (
                source[half, pl.ds(base + o * pitch, 8), :] * slope
            )
            if 1 <= o <= rows:
                active[pl.ds(base + (o - 1) * pitch, 8), lane] = x * cdf

    def backward(group, half, block):
        hidden, back = hiddens[group % 2], backs[group % 2]
        lane = slice(half * lanes, (half + 1) * lanes)
        place, base = group * 2 + half, block * 8

        def add_tap(t, value):
            tap_sums[place, t] += value

        total = window_sums(
            lambda r, s: grad_mixed[half, pl.ds(base + (8 + r * pitch + s), 8), :],
            lambda t: weights[place, t],
            3,
            1,
            rows,
            True,
            [hidden[half, pl.ds(base + (8 + (p + 2) * pitch), 8), :] for p in range(rows)],
            add_tap,
        )
        for p in range(rows):
            back[pl.ds(base + p * pitch, 8), lane] = total[p]

    def leave(group):
        act_low = actives[group % 2][...].astype(low)
        hid_low = backs[group % 2][...].astype(low)
        mlp_sum[...] += lax.dot_general(
            act_low,
            fc_out[:, columns(group)],
            (((1,), (1,)), ((), ())),
            preferred_element_type=wide,
        )
        normed_sum[...] += lax.dot_general(
            hid_low,
            fc_in[:, columns(group)],
            (((1,), (1,)), ((), ())),
            preferred_element_type=wide,
        )
        part_in = jnp.dot(normed_turned[...], hid_low, preferred_element_type=wide)
        part_out = jnp.dot(grads_turned[...], act_low, preferred_element_type=wide)
        for half in range(2):
            lane = slice(half * lanes, (half + 1) * lanes)
            in_sum[group * 2 + half] += part_in[:, lane]
            out_sum[group * 2 + half] += part_out[:, lane]

    enter(0)
    for group in range(groups):
        if group + 1 < groups:
            enter(group + 1)
        if group > 0:
            leave(group - 1)
        for half in range(2):
            for block in range(blocks):
                forward(group, half, block)
        for half in range(2):
            for block in range(blocks):
                backward(group, half, block)
    leave(groups - 1)

    scale_grad = jnp.zeros_like(scale_two)
    shift_grad = jnp.zeros_like(scale_two)
    gain_grad = jnp.zeros_like(scale_two)
    for r in range(rows):
        mlp = mlp_sum[r * pitch : r * pitch + breadth, :]
        back = normed_sum[r * pitch : r * pitch + breadth, :]
        first = first_sum[0, r, 0:breadth, :]
        out_image[0, r] = (alive * (first + scale_two * mlp)).astype(jnp.bfloat16)
        grad_normed[0, r * pitch : r * pitch + breadth, :] = back
        grad_normed[0, r * pitch + breadth : (r + 1) * pitch, :] = jnp.zeros(
            (pitch - breadth, back.shape[1]), wide
        )
        grad = cot[0, r].astype(jnp.float32) * alive
        scale_grad += jnp.sum(grad * mlp, axis=0, keepdims=True)
        shift_grad += jnp.sum(back, axis=0, keepdims=True)
        gain_grad += jnp.sum(back * (first - mean_two) * rstd_two, axis=0, keepdims=True)
    sums[0:1, :] += shift_grad
    sums[1:2, :] += gain_grad
    scale_sum[...] += scale_grad

    @pl.when(image == pl.num_programs(0) - 1)
    def _():
        copies[...] = jnp.broadcast_to(sums[...][None], copies.shape)
        grad_fc[0 : 2 * groups] = in_sum[...].astype(low)
        grad_fc[2 * groups :] = out_sum[...].astype(low)
        store_taps(grad_taps, tap_sums, taps.shape[1])


def unpack_kernel(packed, grad_in, grad_out):
    groups = packed.shape[0] // 2
    for g in range(groups):
        grad_in[:, g * lanes : (g + 1) * lanes] = packed[g].astype(wide)
        grad_out[:, g * lanes : (g + 1) * lanes] = packed[groups + g].astype(wide)


def mlp_block(
    counts, first_sum, far, near, cot, cot_far, cot_near, params, stats, fc_in, fc_out, taps
):
    images, rows, breadth, width = cot.shape
    pitch = first_sum.shape[2]
    deep = fc_in.shape[1]
    groups = deep // lanes
    return call(
        mlp_kernel,
        images,
        [
            (counts, smem),
            (first_sum, spec_image(rows, pitch, width)),
            (far, spec_image(2, pitch, width)),
            (near, spec_image(2, pitch, width)),
            (cot, spec_image(rows, breadth, width)),
            (cot_far, spec_image(1, breadth, width)),
            (cot_near, spec_image(1, breadth, width)),
            (params, spec_whole(8, width)),
            (stats, spec_whole(*stats.shape)),
            (fc_in, spec_whole(width, deep)),
            (fc_out.T, spec_whole(width, deep)),
            (taps, spec_whole(9, deep)),
        ],
        [
            (cot.shape, low, spec_image(rows, breadth, width)),
            ((images, rows * pitch, width), wide, spec_image(rows * pitch, width)),
            (stats.shape, wide, spec_whole(*stats.shape)),
            ((1, width), wide, spec_whole(1, width)),
            ((2 * groups, width, lanes), low, spec_whole(2 * groups, width, lanes)),
            ((9, deep), wide, spec_whole(9, deep)),
        ],
        [
            ((2, width), wide),
            (((rows + 4) * pitch, width), wide),
            (((rows + 2) * pitch, width), wide),
            (((rows + 4) * pitch, width), low),
            ((width, rows * pitch), low),
            (((rows + 2) * pitch, width), low),
            ((width, rows * pitch), low),
            ((2, (rows + 4) * pitch + 16, lanes), wide),
            ((2, (rows + 4) * pitch + 16, lanes), wide),
            ((2, (rows + 2) * pitch, lanes), wide),
            ((2, (rows + 2) * pitch, lanes), wide),
            ((2, (rows + 2) * pitch + 16, lanes), wide),
            ((rows * pitch, 2 * lanes), wide),
            ((rows * pitch, 2 * lanes), wide),
            ((rows * pitch, 2 * lanes), wide),
            ((rows * pitch, 2 * lanes), wide),
            ((rows * pitch, width), wide),
            ((rows * pitch, width), wide),
            ((groups, 9, 8, lanes), wide),
            ((groups, 9, 8, lanes), wide),
            ((groups, width, lanes), wide),
            ((groups, width, lanes), wide),
        ],
        53,
        "mlp",
        vmem=48,
        rows=rows,
        breadth=breadth,
        pitch=pitch,
    )


def body(
    images,
    counts,
    gain_one,
    shift_one,
    proj_in,
    kernel_five,
    kernel_seven,
    lka_proj,
    proj_out,
    scale_one,
    gain_two,
    shift_two,
    fc_in,
    kernel_three,
    fc_out,
    scale_two,
    cotangent,
):
    slots, rows, breadth, width = images.shape
    pitch = -(-(breadth + 2) // 8) * 8
    gap = -(-(breadth + 9) // 8) * 8
    flat = rows * pitch
    blank = jnp.zeros_like(gain_one)
    params = jnp.stack(
        [gain_one, shift_one, scale_one, gain_two, shift_two, scale_two, blank, blank]
    ).astype(wide)
    sizes = dict(rows=rows, breadth=breadth, pitch=pitch)
    vec = spec_whole(8, width)
    devices = device_count()
    blocks = (devices, 2, width)
    two = spec_whole(*blocks)
    square = spec_whole(width, width)
    image_spec = spec_image(rows, breadth, width)
    pairs = slots // 2
    chunks = [(0, pairs - 1), (pairs - 1, 1)]
    pair_width = 2 * width
    pair_square = spec_whole(pair_width, pair_width)
    pair_flat = (pairs, flat, pair_width)
    flat_spec = spec_image(flat, width)
    flat_shape = (slots, flat, width)
    row_shape = (slots, rows, pitch, width)
    groups = len(pair_groups(width))
    kinds = width // lanes + 1
    five_spec = spec_whole(*kernel_five.shape)
    seven_spec = spec_whole(*kernel_seven.shape)

    (first_part,) = call(
        stats_kernel,
        slots,
        [(counts, smem), (images, image_spec)],
        [(blocks, wide, two)],
        [((2, width), wide)],
        2,
        "input_sums",
    )
    pair_in, pair_lka, pair_out = (pair_matrix(m) for m in (proj_in, lka_proj, proj_out))
    first_part, images_after, cot_after = lax.optimization_barrier((first_part, images, cotangent))
    image_far, image_near = far_and_near(
        *(
            jnp.concatenate(parts, axis=1)
            for parts in zip(edge_rows(images_after, 2), edge_rows(cot_after, 1))
        )
    )
    first_stats = from_all(first_part)
    gelu_low = pre_gelu = cot_far = cot_near = None
    cot_shape = (slots, 1, breadth, width)
    mids, rims = [], []
    for start, count in chunks:
        gelu_low, pre_gelu, mid, cot_far, cot_near = call(
            front_kernel,
            count,
            [
                (counts, smem),
                (images, spec_two(start, rows, breadth, width)),
                (image_far, spec_two(start, 3, breadth, width)),
                (image_near, spec_two(start, 3, breadth, width)),
                (params, vec),
                (first_stats, two),
                (pair_in, pair_square),
                (kernel_five, five_spec),
            ],
            [
                (pair_flat, low, spec_from(start, flat, pair_width), gelu_low),
                (pair_flat, low, spec_from(start, flat, pair_width), pre_gelu),
                ((count, rows, pitch, pair_width), low, spec_image(rows, pitch, pair_width)),
                (cot_shape, low, spec_two(start, 1, breadth, width), cot_far),
                (cot_shape, low, spec_two(start, 1, breadth, width), cot_near),
            ],
            [
                (((rows + 4) * pitch, pair_width), wide),
                ((groups, (rows + 4) * pitch + 16, lanes), wide),
                ((kinds, 25, 8, lanes), wide),
                (((rows + 4) * pitch, lanes), wide),
                ((flat, pair_width), wide),
            ],
            4.3 * count,
            f"normed_to_five_{start}",
            **sizes,
        )
        mids.append(mid)
        rims.append(far_and_near(mid, mid))
    lka_low = attend = attn = first_sum = None
    second_part = jnp.zeros(blocks, wide)
    for (start, count), mid, (mid_far, mid_near) in zip(chunks, mids, rims):
        rim_spec = spec_image(rows, pitch, pair_width)
        pair_spec = spec_from(start, flat, pair_width)
        lka_low, attend, attn, first_sum, second_part = call(
            attend_kernel,
            count,
            [
                (counts, smem),
                (images, spec_two(start, rows, breadth, width)),
                (mid, rim_spec),
                (mid_far, rim_spec),
                (mid_near, rim_spec),
                (gelu_low, pair_spec),
                (params, vec),
                (first_stats, two),
                (second_part, two),
                (pair_lka, pair_square),
                (pair_out, pair_square),
                (kernel_seven, seven_spec),
            ],
            [
                (pair_flat, low, pair_spec, lka_low),
                (pair_flat, low, pair_spec, attend),
                (pair_flat, low, pair_spec, attn),
                (flat_shape, wide, spec_two(start, flat, width), first_sum),
                (blocks, wide, two),
            ],
            [
                ((2, width), wide),
                ((groups, 3 * rows * gap + 48, lanes), wide),
                ((kinds, 49, 8, lanes), wide),
                ((flat, pair_width), wide),
                ((flat, pair_width), wide),
                ((flat, pair_width), wide),
            ],
            6.2 * count,
            f"seven_to_first_sum_{start}",
            vmem=20,
            gap=gap,
            start_pair=start,
            **sizes,
        )
    first_rows = first_sum.reshape(row_shape)
    sum_far, sum_near = far_and_near(*edge_rows(first_rows, 2))
    second_stats = from_all(second_part)
    out_image, grad_normed_two, third_part, scale_two_part, grad_fc, grad_kernel_three = mlp_block(
        counts,
        first_rows,
        sum_far,
        sum_near,
        cotangent,
        cot_far,
        cot_near,
        params,
        second_stats,
        fc_in,
        fc_out,
        kernel_three,
    )
    grad_second = from_all(third_part)
    packed_shape = grad_fc.shape
    grad_fc = grad_fc.reshape(devices, -1, lanes)
    grad_fc, grad_second = lax.optimization_barrier((grad_fc, grad_second))
    fc_share = jnp.sum(from_all(grad_fc).astype(wide), axis=0).astype(low)
    grad_first = grad_direct = None
    gates, rims = [], []
    lka_sum = out_sum = jnp.zeros((width, width), wide)
    scale_sum = jnp.zeros((1, width), wide)
    for start, count in chunks:
        pair_spec = spec_from(start, flat, pair_width)
        grad_first, grad_direct, grad_lka, lka_sum, out_sum, scale_sum = call(
            gate_kernel,
            count,
            [
                (counts, smem),
                (first_sum, spec_two(start, flat, width)),
                (attn, pair_spec),
                (cotangent, spec_two(start, rows, breadth, width)),
                (grad_normed_two, spec_two(start, flat, width)),
                (lka_low, pair_spec),
                (attend, pair_spec),
                (gelu_low, pair_spec),
                (params, vec),
                (second_stats, two),
                (grad_second, two),
                (pair_lka, pair_square),
                (pair_out, pair_square),
                (lka_sum, square),
                (out_sum, square),
                (scale_sum, spec_whole(1, width)),
            ],
            [
                (pair_flat, wide, pair_spec, grad_first),
                (pair_flat, low, pair_spec, grad_direct),
                ((count, rows, pitch, pair_width), low, spec_image(rows, pitch, pair_width)),
                ((width, width), wide, square),
                ((width, width), wide, square),
                ((1, width), wide, spec_whole(1, width)),
            ],
            [
                ((flat, pair_width), wide),
                ((flat, pair_width), wide),
            ],
            3.2 * count,
            f"gate_backward_{start}",
            vmem=44,
            start_pair=start,
            **sizes,
        )
        gates.append(grad_lka)
        rims.append(far_and_near(grad_lka, grad_lka))
    grad_mid = None
    seven_sum = jnp.zeros(kernel_seven.shape, wide)
    for (start, count), grad_lka, mid, (lka_far, lka_near) in zip(chunks, gates, mids, rims):
        rim_spec = spec_image(rows, pitch, pair_width)
        grad_mid, seven_sum = call(
            seven_kernel,
            count,
            [
                (grad_lka, rim_spec),
                (lka_far, rim_spec),
                (lka_near, rim_spec),
                (mid, rim_spec),
                (kernel_seven, seven_spec),
                (seven_sum, seven_spec),
            ],
            [
                (
                    (pairs, rows, pitch, pair_width),
                    low,
                    spec_from(start, rows, pitch, pair_width),
                    grad_mid,
                ),
                (kernel_seven.shape, wide, seven_spec),
            ],
            [
                ((groups, 3 * rows * gap + 48, lanes), wide),
                ((groups, flat, lanes), wide),
                ((flat, pair_width), wide),
                ((kinds, 49, 8, lanes), wide),
                ((kinds, 49, 8, lanes), wide),
            ],
            7 * count,
            f"seven_backward_{start}",
            vmem=20,
            gap=gap,
            **sizes,
        )
    fc_share, grad_mid = lax.optimization_barrier((fc_share, grad_mid))
    five_far, five_near = far_and_near(*edge_rows(grad_mid, 2))
    fc_whole = lax.all_gather(fc_share, ("dp", "strip"), tiled=True)
    pair_spec = spec_image(flat, pair_width)
    deep = fc_in.shape[1]
    total_rows = pack_rows(width, deep)
    grad_partial, packed = call(
        five_kernel,
        pairs,
        [
            (counts, smem),
            (images, spec_two(0, rows, breadth, width)),
            (grad_mid, spec_image(rows, pitch, pair_width)),
            (five_far, spec_image(2, pitch, pair_width)),
            (five_near, spec_image(2, pitch, pair_width)),
            (gelu_low, pair_spec),
            (pre_gelu, pair_spec),
            (grad_direct, pair_spec),
            (grad_first, pair_spec),
            (params, vec),
            (first_stats, two),
            (pair_in, pair_square),
            (kernel_five, five_spec),
            (lka_sum, square),
            (out_sum, square),
            (seven_sum, seven_spec),
            (grad_kernel_three, spec_whole(*kernel_three.shape)),
            (scale_sum, spec_whole(1, width)),
            (scale_two_part, spec_whole(1, width)),
        ],
        [
            (flat_shape, wide, spec_two(0, flat, width)),
            ((total_rows + 8, width), low, spec_whole(total_rows + 8, width)),
        ],
        [
            ((width, width), wide),
            (kernel_five.shape, wide),
            ((2, width), wide),
            ((total_rows + 8, width), wide),
            ((groups, (rows + 4) * pitch + 16, lanes), wide),
            ((groups, flat, lanes), wide),
            ((flat, pair_width), wide),
            ((kinds, 25, 8, lanes), wide),
            ((kinds, 25, 8, lanes), wide),
            ((flat, pair_width), wide),
            ((flat, pair_width), wide),
        ],
        6 * pairs,
        "five_backward",
        vmem=52,
        **sizes,
    )
    share, vectors = split_sums(packed, 8)
    fc_whole, share = lax.optimization_barrier((fc_whole, share))
    matrices = joined(share)
    pieces = call(
        spread_kernel,
        1,
        [(matrices, spec_whole(total_rows, width))],
        [
            (shape, wide, spec_whole(*shape))
            for shape in [(width, width)] * 3
            + [kernel_five.shape, kernel_seven.shape, kernel_three.shape]
        ],
        [],
        2,
        "attention_gradients",
    )
    (grad_images,) = call(
        last_kernel,
        slots,
        [
            (counts, smem),
            (images, image_spec),
            (grad_partial, flat_spec),
            (params, vec),
            (first_stats, two),
            (vectors, spec_whole(8, width)),
        ],
        [(images.shape, wide, image_spec)],
        [],
        4,
        "input_gradient",
        **sizes,
    )
    grad_fc_in, grad_fc_out = call(
        unpack_kernel,
        1,
        [(fc_whole.reshape(packed_shape), spec_whole(*packed_shape))],
        [
            ((width, deep), wide, spec_whole(width, deep)),
            ((width, deep), wide, spec_whole(width, deep)),
        ],
        [],
        2,
        "weight_gradients",
    )
    vectors = vectors.astype(wide)
    grad_second = jnp.sum(grad_second, axis=0)
    return (
        out_image,
        grad_images,
        vectors[1],
        vectors[0],
        pieces[0],
        pieces[3],
        pieces[4],
        pieces[1],
        pieces[2],
        vectors[2],
        grad_second[1],
        grad_second[0],
        grad_fc_in,
        pieces[5],
        grad_fc_out.T,
        vectors[3],
    )


def solution(mesh):
    split = P("dp", "strip", None, None)
    return jax.shard_map(
        body,
        mesh=mesh,
        in_specs=(split,) + (P(),) * 15 + (split,),
        out_specs=(split, split) + (P(),) * 14,
        check_vma=False,
    )
```

```python
import functools

import jax
import jax.numpy as jnp
from jax import lax
from jax.experimental import pallas as pl
from jax.experimental.pallas import tpu as pltpu
from jax.sharding import PartitionSpec as P

epsilon = 1e-05
lanes = 128
smem = pl.BlockSpec(memory_space=pltpu.SMEM)
wide = jnp.float32
low = jnp.bfloat16


def exchange_steps():
    return [
        (axis, 1 << bit)
        for axis in ("strip", "dp")
        for bit in range(lax.axis_size(axis).bit_length() - 1)
    ]


def swapped(value, axis, bit):
    return lax.ppermute(value, axis, [(i, i ^ bit) for i in range(lax.axis_size(axis))])


def device_count():
    return lax.axis_size("dp") * lax.axis_size("strip")


def from_all(copies):
    return lax.all_to_all(copies, ("dp", "strip"), 0, 0)


def split_sums(part, size):
    for place, (axis, bit) in enumerate(exchange_steps()):
        length = part.shape[0] - size
        if place < 3:
            upper = (lax.axis_index(axis) // bit) % 2
            tail = part[length:]
            halves = part[:length].reshape((2, length // 2) + part.shape[1:])
            sent = lax.dynamic_index_in_dim(halves, 1 - upper, 0, False)
            kept = lax.dynamic_index_in_dim(halves, upper, 0, False)
            sent, part = jnp.concatenate([sent, tail]), jnp.concatenate([kept, tail])
        else:
            sent = part
        got = swapped(sent, axis, bit)
        part = (part.astype(wide) + got.astype(wide)).astype(low)
    return part[: part.shape[0] - size], part[part.shape[0] - size :]


def joined(part, beside):
    for place, (axis, bit) in enumerate(reversed(exchange_steps()[:3])):
        if place == 1:
            part, beside = lax.optimization_barrier((part, beside))
        upper = (lax.axis_index(axis) // bit) % 2
        got = swapped(part, axis, bit)
        part = jnp.where(
            upper == 0, jnp.concatenate([part, got]), jnp.concatenate([got, part])
        )
    return part, beside


def near_pairs():
    return [(i, i ^ 1) for i in range(lax.axis_size("strip"))]


def far_and_near(far, near):
    count = lax.axis_size("strip")
    pairs = [(i, i + 1) for i in range(1, count - 1, 2)]
    return (
        lax.ppermute(far, "strip", pairs + [(j, i) for i, j in pairs]),
        lax.ppermute(near, "strip", near_pairs()),
    )


def edge_rows(value, width):
    odd = lax.axis_index("strip") % 2
    length = value.shape[1] - width
    return (
        lax.dynamic_slice_in_dim(value, odd * length, width, 1),
        lax.dynamic_slice_in_dim(value, (1 - odd) * length, width, 1),
    )


def sides(length):
    odd = lax.axis_index("strip") % 2
    return odd * length, (1 - odd) * length


def present():
    strip, count = lax.axis_index("strip"), lax.axis_size("strip")
    above, below = (strip > 0).astype(wide), (strip < count - 1).astype(wide)
    odd = (strip % 2).astype(wide)
    return odd * below + (1 - odd) * above, odd * above + (1 - odd) * below


def normal_parts(x):
    density = jnp.exp2(x * x * -0.7213475204444817 - 1.3257480647361595)
    scale = 1.0 + 0.2316419 * jnp.abs(x)
    guess = pl.reciprocal(scale, approx=True)
    t = guess * (2.0 - scale * guess)
    poly = 1.781477937 + t * (-1.821255978 + t * 1.330274429)
    poly = t * (0.319381530 + t * (-0.356563782 + t * poly))
    tail = density * poly
    return jnp.where(x > 0, 1.0 - tail, tail), density


def window_sums(load, weight, across, spread, rows, back, center=None, add_tap=None):
    total = [None] * rows
    reach = spread * (across - 1)
    for j in range(across):
        shift = (j - across // 2) * spread * (-1 if back else 1)
        w = [weight(i * across + j) for i in range(across)]
        tap = [None] * across
        for r in range(rows + reach):
            v = load(r, shift)
            for i in range(across):
                o = r - reach + spread * i if back else r - spread * i
                if 0 <= o < rows:
                    term = v * w[i]
                    total[o] = term if total[o] is None else total[o] + term
                    if center is not None:
                        term = v * center[o]
                        tap[i] = term if tap[i] is None else tap[i] + term
        if center is not None:
            for i in range(across):
                add_tap(i * across + j, tap[i])
    return total


def lane_groups(width):
    return [(start, min(lanes, width - start)) for start in range(0, width, lanes)]


def fill_weights(weights, taps, width):
    weights[...] = jnp.zeros_like(weights)
    for g, (start, size) in enumerate(lane_groups(width)):
        for t in range(taps.shape[0]):
            weights[g, t, :, 0:size] = jnp.broadcast_to(
                taps[t : t + 1, start : start + size].astype(wide), (8, size)
            )


def store_taps(grad_taps, tap_sums, width):
    for g, (start, size) in enumerate(lane_groups(width)):
        for t in range(grad_taps.shape[0]):
            grad_taps[t : t + 1, start : start + size] = jnp.sum(
                tap_sums[g, t, :, 0:size], axis=0, keepdims=True
            )


def inside(rows, pitch, breadth, width):
    place = lax.broadcasted_iota(jnp.int32, (rows, pitch, width), 1)
    return jnp.where(place < breadth, 1.0, 0.0).reshape(rows * pitch, width)


def live_here(counts):
    return counts[lax.axis_index("dp")]


def pixels_of(counts, area):
    total = counts[0]
    for k in range(1, counts.shape[0]):
        total += counts[k]
    return total.astype(wide) * (area * lax.axis_size("strip"))


def norm_of(blocks, pixels):
    stats = jnp.sum(blocks[...], axis=0) / pixels
    mean = stats[0:1, :]
    return mean, lax.rsqrt(stats[1:2, :] - mean * mean + epsilon)


def spec_image(*shape):
    return pl.BlockSpec((1,) + shape, lambda i: (i,) + (0,) * len(shape))


def spec_from(start, *shape):
    return pl.BlockSpec((1,) + shape, lambda i: (i + start,) + (0,) * len(shape))


def spec_two(start, *shape):
    return pl.BlockSpec((2,) + shape, lambda i: (i + start,) + (0,) * len(shape))


def spec_whole(*shape):
    return pl.BlockSpec(shape, lambda i: (0,) * len(shape))


def call(kernel, steps, ins, outs, scratch, cost, name, vmem=44, **sizes):
    earlier = [out[3] for out in outs if len(out) > 3 and out[3] is not None]
    aliases, at = {}, len(ins)
    for place, out in enumerate(outs):
        if len(out) > 3 and out[3] is not None:
            aliases[at] = place
            at += 1

    def run(*refs):
        kernel(*refs[: len(ins)], *refs[at:], **sizes)

    return pl.pallas_call(
        run,
        grid=(steps,),
        in_specs=[spec for _, spec in ins] + [pl.BlockSpec(memory_space=pl.ANY)] * len(earlier),
        out_specs=[out[2] for out in outs],
        out_shape=[jax.ShapeDtypeStruct(out[0], out[1]) for out in outs],
        scratch_shapes=[pltpu.VMEM(shape, dtype) for shape, dtype in scratch],
        input_output_aliases=aliases,
        compiler_params=pltpu.CompilerParams(vmem_limit_bytes=vmem * 1024 * 1024),
        cost_estimate=pl.CostEstimate(
            flops=0, bytes_accessed=int(cost * 3.5e6), transcendentals=0
        ),
        name=name,
    )(*[array for array, _ in ins], *earlier)


def paired(value):
    return pair_lanes(value, value)


def pair_lanes(left, right):
    main = left.shape[-1] // lanes * lanes
    tails = jnp.concatenate([left[..., main:], right[..., main:]], axis=-1)
    return jnp.concatenate([left[..., :main], right[..., :main], tails], axis=-1)


def split_lanes(value):
    width = value.shape[-1] // 2
    main = width // lanes * lanes
    left = jnp.concatenate([value[..., :main], value[..., 2 * main : main + width]], axis=-1)
    right = jnp.concatenate([value[..., main : 2 * main], value[..., main + width :]], axis=-1)
    return left, right


def folded(value):
    left, right = split_lanes(value)
    return left + right


def folded_square(value):
    width = value.shape[0] // 2
    main = width // lanes * lanes
    left = split_lanes(jnp.concatenate([value[:main], value[2 * main : main + width]], axis=0))[0]
    right = split_lanes(jnp.concatenate([value[main : 2 * main], value[main + width :]], axis=0))[1]
    return left + right


def pair_matrix(matrix):
    blank = jnp.zeros_like(matrix)
    left = jnp.concatenate([matrix, blank], axis=1)
    right = jnp.concatenate([blank, matrix], axis=1)
    width = matrix.shape[0]
    main = width // lanes * lanes

    def columns(value):
        return jnp.concatenate(
            [
                value[:, :main],
                value[:, width : width + main],
                value[:, main:width],
                value[:, width + main :],
            ],
            axis=1,
        )

    left, right = columns(left), columns(right)
    return jnp.concatenate([left[:main], right[:main], left[main:], right[main:]])


def pair_groups(width):
    main = width // lanes
    return [(g * lanes, g % main) for g in range(2 * main)] + [(2 * main * lanes, main)]


def fill_pair_weights(weights, taps, width):
    main = width // lanes * lanes
    for t in range(taps.shape[0]):
        row = taps[t : t + 1, :].astype(wide)
        tail = row[:, main:]
        for g in range(main // lanes):
            weights[g, t] = jnp.broadcast_to(row[:, g * lanes : (g + 1) * lanes], (8, lanes))
        weights[main // lanes, t] = jnp.broadcast_to(
            jnp.concatenate([tail, tail], axis=1), (8, lanes)
        )


def store_pair_taps(grad_taps, tap_sums, width):
    main = width // lanes * lanes
    for t in range(grad_taps.shape[0]):
        for g in range(main // lanes):
            grad_taps[t : t + 1, g * lanes : (g + 1) * lanes] = jnp.sum(
                tap_sums[g, t], axis=0, keepdims=True
            )
        tail = jnp.sum(tap_sums[main // lanes, t], axis=0, keepdims=True)
        grad_taps[t : t + 1, main:width] = tail[:, : width - main] + tail[:, width - main :]


def alive_lanes(counts, start, width):
    main = width // lanes * lanes
    image = 2 * (pl.program_id(0) + start)
    at = lax.broadcasted_iota(jnp.int32, (1, 2 * width), 1)
    second = ((at >= main) & (at < 2 * main)) | (at >= main + width)
    return jnp.where(image + second.astype(jnp.int32) < live_here(counts), 1.0, 0.0)


def stats_kernel(counts, images, copies, sums):
    image = pl.program_id(0)

    @pl.when(image == 0)
    def _():
        sums[...] = jnp.zeros_like(sums)

    alive = (image < live_here(counts)).astype(wide)
    total = jnp.zeros((images.shape[2], images.shape[3]), wide)
    square = total
    for r in range(images.shape[1]):
        value = images[0, r].astype(wide)
        total += value
        square += value * value
    sums[0:1, :] += jnp.sum(total, axis=0, keepdims=True) * alive
    sums[1:2, :] += jnp.sum(square, axis=0, keepdims=True) * alive

    @pl.when(image == pl.num_programs(0) - 1)
    def _():
        copies[...] = jnp.broadcast_to(sums[...][None], copies.shape)


def front_kernel(
    counts,
    images,
    far,
    near,
    params,
    stats,
    proj_in,
    taps,
    gelu_low,
    pre_gelu,
    lka_mid,
    cot_far,
    cot_near,
    values,
    gelu,
    weights,
    mask,
    mid,
    *,
    rows,
    breadth,
    pitch,
):
    width = images.shape[3]
    pixels = pixels_of(counts, rows * breadth)
    mean, rstd = norm_of(stats, pixels)
    mean, rstd = paired(mean), paired(rstd)
    gain, shift = paired(params[0:1, :]), paired(params[1:2, :])

    @pl.when(pl.program_id(0) == 0)
    def _():
        values[...] = jnp.zeros_like(values)
        gelu[...] = jnp.zeros_like(gelu)
        fill_pair_weights(weights, taps, width)
        mask[...] = inside(rows + 4, pitch, breadth, lanes)
        for offset, there in zip(sides((rows + 2) * pitch), present()):
            at = pl.ds(pl.multiple_of(offset, 8), 2 * pitch)
            mask[at, :] = mask[at, :] * there

    def place(at, source, r):
        value = pair_lanes(source[0, r].astype(wide), source[1, r].astype(wide))
        values[pl.ds(at, breadth), :] = (value - mean) * rstd * gain + shift

    for k in range(2):
        cot_far[k, 0] = far[k, 2]
        cot_near[k, 0] = near[k, 2]
    for source, offset in zip((far, near), sides((rows + 2) * pitch)):
        for r in range(2):
            place(pl.multiple_of(offset + r * pitch, 8), source, r)
    for r in range(rows):
        place((r + 2) * pitch, images, r)
    pre = jnp.dot(values[...].astype(low), proj_in[...], preferred_element_type=wide)
    pre_gelu[0] = pre[2 * pitch : (rows + 2) * pitch, :].astype(low)
    for g, (start, _) in enumerate(pair_groups(width)):
        part = pre[:, start : start + lanes]
        cdf, _ = normal_parts(part)
        rounded = (part * cdf * mask[...]).astype(low).astype(wide)
        gelu_low[0, :, start : start + lanes] = rounded[2 * pitch : (rows + 2) * pitch].astype(low)
        gelu[g, 8 : 8 + (rows + 4) * pitch, :] = rounded
    for g, (start, which) in enumerate(pair_groups(width)):

        def step(block, carry, g=g, start=start, which=which):
            base = pl.multiple_of(block * 8, 8)
            total = window_sums(
                lambda r, s: gelu[g, pl.ds(base + (8 + r * pitch + s), 8), :],
                lambda t: weights[which, t],
                5,
                1,
                rows,
                False,
            )
            for o in range(rows):
                mid[pl.ds(base + o * pitch, 8), start : start + lanes] = total[o]
            return carry

        lax.fori_loop(0, pitch // 8, step, 0)
    for r in range(rows):
        at = r * pitch
        lka_mid[0, r] = (
            mid[at : at + pitch, :] * inside(1, pitch, breadth, 2 * width)
        ).astype(low)


def attend_kernel(
    counts,
    images,
    lka_mid,
    far,
    near,
    gelu_low,
    params,
    stats,
    earlier_sums,
    lka_proj,
    proj_out,
    taps,
    lka_low,
    attend_out,
    first_sum,
    copies,
    sums,
    window,
    weights,
    lka,
    values,
    mask,
    *,
    rows,
    breadth,
    pitch,
    gap,
    start_pair,
):
    width = images.shape[3]
    alive = alive_lanes(counts, start_pair, width)
    pixels = pixels_of(counts, rows * breadth)
    mean, rstd = norm_of(stats, pixels)
    mean, rstd = paired(mean), paired(rstd)
    gain, shift, scale = (paired(params[k : k + 1, :]) for k in range(3))

    @pl.when(pl.program_id(0) == 0)
    def _():
        window[...] = jnp.zeros_like(window)
        values[...] = jnp.zeros_like(values)
        sums[...] = earlier_sums[0]
        fill_pair_weights(weights, taps, width)
        mask[...] = inside(rows, pitch, breadth, 2 * width)

    far_at, near_at = sides(2 * rows * gap)
    for offset, source in ((far_at, far), (rows * gap, lka_mid), (near_at, near)):
        for r in range(rows):
            at = pl.ds(pl.multiple_of(offset + (16 + r * gap), 8), pitch)
            for g, (start, _) in enumerate(pair_groups(width)):
                window[g, at, :] = source[0, r, :, start : start + lanes].astype(wide)
    for g, (start, which) in enumerate(pair_groups(width)):

        def step(block, carry, g=g, start=start, which=which):
            base = pl.multiple_of(block * 8, 8)
            total = window_sums(
                lambda r, s: window[g, pl.ds(base + (16 + r * gap + s), 8), :],
                lambda t: weights[which, t],
                7,
                3,
                rows,
                False,
            )
            for o in range(rows):
                lka[pl.ds(base + o * pitch, 8), start : start + lanes] = total[o]
            return carry

        lax.fori_loop(0, pitch // 8, step, 0)
    for r in range(rows):
        values[r * pitch : r * pitch + breadth, :] = pair_lanes(
            images[0, r].astype(wide), images[1, r].astype(wide)
        )
    low_lka = lka[...].astype(low)
    lka_low[0] = low_lka
    attend = jnp.dot(low_lka, lka_proj[...], preferred_element_type=wide)
    attend_out[0] = attend.astype(low)
    gated = (gelu_low[0].astype(wide) * attend).astype(low)
    branch = jnp.dot(gated, proj_out[...], preferred_element_type=wide)
    attn = (branch + ((values[...] - mean) * rstd * gain + shift)) * mask[...]
    first = values[...] + scale * attn
    first_sum[0], first_sum[1] = split_lanes(first)
    sums[0:1, :] += folded(jnp.sum(first, axis=0, keepdims=True) * alive)
    sums[1:2, :] += folded(jnp.sum(first * first, axis=0, keepdims=True) * alive)

    @pl.when(pl.program_id(0) == pl.num_programs(0) - 1)
    def _():
        copies[...] = jnp.broadcast_to(sums[...][None], copies.shape)


def gate_kernel(
    counts,
    first_sum,
    images,
    cot,
    grad_normed,
    lka_low,
    attend,
    gelu_low,
    params,
    stats,
    grad_stats,
    lka_proj,
    proj_out,
    lka_before,
    out_before,
    scale_before,
    grad_first,
    grad_direct,
    grad_lka,
    grad_lka_proj,
    grad_proj_out,
    sums,
    values,
    pixels_in,
    mask,
    *,
    rows,
    breadth,
    pitch,
    start_pair,
):
    width = cot.shape[3]
    alive = alive_lanes(counts, start_pair, width)
    pixels = pixels_of(counts, rows * breadth)
    mean, rstd = norm_of(stats, pixels)
    mean, rstd = paired(mean), paired(rstd)
    scale, gain = paired(params[2:3, :]), paired(params[3:4, :])
    grad_sums = jnp.sum(grad_stats[...], axis=0)
    shift_sum, gain_sum = paired(grad_sums[0:1, :]), paired(grad_sums[1:2, :])

    @pl.when(pl.program_id(0) == 0)
    def _():
        values[...] = jnp.zeros_like(values)
        pixels_in[...] = jnp.zeros_like(pixels_in)
        mask[...] = inside(rows, pitch, breadth, 2 * width)
        sums[...] = scale_before[...]
        grad_lka_proj[...] = lka_before[...]
        grad_proj_out[...] = out_before[...]

    for r in range(rows):
        values[r * pitch : r * pitch + breadth, :] = pair_lanes(
            cot[0, r].astype(wide), cot[1, r].astype(wide)
        )
        pixels_in[r * pitch : r * pitch + breadth, :] = pair_lanes(
            images[0, r].astype(wide), images[1, r].astype(wide)
        )
    summed = pair_lanes(first_sum[0], first_sum[1])
    yhat = (summed - mean) * rstd
    inner = pair_lanes(grad_normed[0], grad_normed[1]) - (shift_sum + yhat * gain_sum) / pixels
    first = alive * (values[...] + rstd * gain * inner) * mask[...]
    grad_first[0] = first
    sums[...] += folded(
        jnp.sum(first * (summed - pixels_in[...]), axis=0, keepdims=True) / scale
    )
    branch = (first * scale).astype(low)
    gated_back = lax.dot_general(
        branch, proj_out[...], (((1,), (1,)), ((), ())), preferred_element_type=wide
    )
    gelu = gelu_low[0].astype(wide)
    attended = attend[0].astype(wide)
    gated = gelu * attended
    grad_proj_out[...] += folded_square(
        jnp.dot(gated.T.astype(low), branch, preferred_element_type=wide)
    )
    grad_direct[0] = (gated_back * attended).astype(low)
    back = (gated_back * gelu).astype(low)
    lka = lax.dot_general(
        back, lka_proj[...], (((1,), (1,)), ((), ())), preferred_element_type=wide
    )
    grad_lka_proj[...] += folded_square(
        jnp.dot(lka_low[0].astype(wide).T.astype(low), back, preferred_element_type=wide)
    )
    for r in range(rows):
        grad_lka[0, r] = lka[r * pitch : (r + 1) * pitch, :].astype(low)


def seven_kernel(
    grad_lka,
    far,
    near,
    lka_mid,
    taps,
    taps_before,
    grad_mid,
    grad_taps,
    window,
    middle,
    out,
    weights,
    tap_sums,
    *,
    rows,
    breadth,
    pitch,
    gap,
):
    width = taps.shape[1]

    @pl.when(pl.program_id(0) == 0)
    def _():
        window[...] = jnp.zeros_like(window)
        tap_sums[...] = jnp.zeros_like(tap_sums)
        fill_pair_weights(weights, taps, width)

    far_at, near_at = sides(2 * rows * gap)
    for g, (start, _) in enumerate(pair_groups(width)):
        for offset, source in ((far_at, far), (rows * gap, grad_lka), (near_at, near)):
            for r in range(rows):
                at = pl.ds(pl.multiple_of(offset + (16 + r * gap), 8), pitch)
                window[g, at, :] = source[0, r, :, start : start + lanes].astype(wide)
        for r in range(rows):
            middle[g, r * pitch : (r + 1) * pitch, :] = lka_mid[
                0, r, :, start : start + lanes
            ].astype(wide)
    for g, (start, which) in enumerate(pair_groups(width)):

        def step(block, carry, g=g, start=start, which=which):
            base = pl.multiple_of(block * 8, 8)

            def add_tap(t, value):
                tap_sums[which, t] += value

            total = window_sums(
                lambda r, s: window[g, pl.ds(base + (16 + r * gap + s), 8), :],
                lambda t: weights[which, t],
                7,
                3,
                rows,
                True,
                [middle[g, pl.ds(base + p * pitch, 8), :] for p in range(rows)],
                add_tap,
            )
            for o in range(rows):
                out[pl.ds(base + o * pitch, 8), start : start + lanes] = total[o]
            return carry

        lax.fori_loop(0, pitch // 8, step, 0, unroll=True)
    for r in range(rows):
        at = r * pitch
        grad_mid[0, r] = (
            out[at : at + pitch, :] * inside(1, pitch, breadth, 2 * width)
        ).astype(low)

    @pl.when(pl.program_id(0) == pl.num_programs(0) - 1)
    def _():
        store_pair_taps(grad_taps, tap_sums, width)
        grad_taps[...] += taps_before[...]


def five_kernel(
    counts,
    images,
    grad_mid,
    far,
    near,
    gelu_low,
    pre_gelu,
    grad_direct,
    grad_first,
    params,
    stats,
    proj_in,
    taps,
    lka_sum,
    out_sum,
    seven_sum,
    three_sum,
    scale_one,
    scale_two,
    grad_partial,
    packed,
    grad_proj_in,
    grad_taps,
    sums,
    pack,
    window,
    middle,
    out,
    weights,
    tap_sums,
    values,
    mask,
    *,
    rows,
    breadth,
    pitch,
):
    width = images.shape[3]
    alive = alive_lanes(counts, 0, width)
    pixels = pixels_of(counts, rows * breadth)
    mean, rstd = norm_of(stats, pixels)
    mean, rstd = paired(mean), paired(rstd)
    gain, shift, scale = (paired(params[k : k + 1, :]) for k in range(3))

    @pl.when(pl.program_id(0) == 0)
    def _():
        window[...] = jnp.zeros_like(window)
        tap_sums[...] = jnp.zeros_like(tap_sums)
        values[...] = jnp.zeros_like(values)
        sums[...] = jnp.zeros_like(sums)
        grad_proj_in[...] = jnp.zeros_like(grad_proj_in)
        mask[...] = inside(rows, pitch, breadth, 2 * width)
        fill_pair_weights(weights, taps, width)

    for g, (start, _) in enumerate(pair_groups(width)):
        for source, offset in zip((far, near), sides((rows + 2) * pitch)):
            for r in range(2):
                at = pl.ds(pl.multiple_of(offset + (8 + r * pitch), 8), pitch)
                window[g, at, :] = source[0, r, :, start : start + lanes].astype(wide)
        for r in range(rows):
            at = 8 + (r + 2) * pitch
            window[g, at : at + pitch, :] = grad_mid[0, r, :, start : start + lanes].astype(wide)
        middle[g] = gelu_low[0, :, start : start + lanes].astype(wide)
    for g, (start, which) in enumerate(pair_groups(width)):

        def step(block, carry, g=g, start=start, which=which):
            base = pl.multiple_of(block * 8, 8)

            def add_tap(t, value):
                tap_sums[which, t] += value

            total = window_sums(
                lambda r, s: window[g, pl.ds(base + (8 + r * pitch + s), 8), :],
                lambda t: weights[which, t],
                5,
                1,
                rows,
                True,
                [middle[g, pl.ds(base + p * pitch, 8), :] for p in range(rows)],
                add_tap,
            )
            for o in range(rows):
                out[pl.ds(base + o * pitch, 8), start : start + lanes] = total[o]
            return carry

        lax.fori_loop(0, pitch // 8, step, 0, unroll=True)
    for r in range(rows):
        values[r * pitch : r * pitch + breadth, :] = pair_lanes(
            images[0, r].astype(wide), images[1, r].astype(wide)
        )
    pre = pre_gelu[0].astype(wide)
    cdf, density = normal_parts(pre)
    grad_pre = ((grad_direct[0].astype(wide) + out[...]) * (cdf + pre * density)).astype(low)
    xhat = (values[...] - mean) * rstd
    normed = (xhat * gain + shift) * mask[...]
    grad_proj_in[...] += folded_square(
        jnp.dot(normed.T.astype(low), grad_pre, preferred_element_type=wide)
    )
    back = lax.dot_general(
        grad_pre, proj_in[...], (((1,), (1,)), ((), ())), preferred_element_type=wide
    )
    first = grad_first[0]
    grad_normed = (first * scale + back) * mask[...]
    sums[0:1, :] += folded(jnp.sum(grad_normed, axis=0, keepdims=True))
    sums[1:2, :] += folded(jnp.sum(grad_normed * xhat, axis=0, keepdims=True))
    grad_partial[0], grad_partial[1] = split_lanes(first + alive * rstd * gain * grad_normed)

    @pl.when(pl.program_id(0) == pl.num_programs(0) - 1)
    def _():
        store_pair_taps(grad_taps, tap_sums, width)
        pack[...] = jnp.zeros_like(pack)
        at = 0
        for part in (grad_proj_in, lka_sum, out_sum, grad_taps, seven_sum):
            pack[at : at + part.shape[0], :] = part[...]
            at += -(-part.shape[0] // 8) * 8
        for k in range(three_sum.shape[1] // width):
            pack[at : at + 9, :] = three_sum[:, k * width : (k + 1) * width]
            at += 9
        at = pack.shape[0] - 8
        pack[at : at + 2, :] = sums[...]
        pack[at + 2 : at + 3, :] = scale_one[...]
        pack[at + 3 : at + 4, :] = scale_two[...]
        packed[...] = pack[...].astype(low)


def pack_rows(width, deep):
    return -(-(3 * width + 32 + 56 + 9 * (deep // width)) // 64) * 64


def spread_kernel(packed, grad_in, grad_lka, grad_out, grad_five, grad_seven, grad_three):
    width = packed.shape[1]
    at = 0
    for part in (grad_in, grad_lka, grad_out, grad_five, grad_seven):
        size = -(-part.shape[0] // 8) * 8
        part[...] = packed[at : at + size, :].astype(wide)[: part.shape[0]]
        at += size
    rest = packed[at:, :].astype(wide)
    for k in range(grad_three.shape[1] // width):
        grad_three[:, k * width : (k + 1) * width] = rest[9 * k : 9 * k + 9]


def last_kernel(
    counts, images, grad_partial, params, stats, grad_stats, grad_images, *, rows, breadth, pitch
):
    alive = (pl.program_id(0) < live_here(counts)).astype(wide)
    pixels = pixels_of(counts, rows * breadth)
    mean, rstd = norm_of(stats, pixels)
    factor = alive * rstd * params[0:1, :] / pixels
    grad_sums = grad_stats[...].astype(wide)
    shift_sum, gain_sum = grad_sums[0:1, :], grad_sums[1:2, :]
    for r in range(rows):
        xhat = (images[0, r].astype(wide) - mean) * rstd
        part = grad_partial[0, r * pitch : r * pitch + breadth, :]
        grad_images[0, r] = part - factor * (shift_sum + xhat * gain_sum)


def mlp_kernel(
    counts,
    first_sum,
    far,
    near,
    cot,
    cot_far,
    cot_near,
    params,
    stats,
    fc_in,
    fc_out,
    taps,
    out_image,
    grad_normed,
    copies,
    scale_sum,
    fc_kept,
    fc_sent,
    grad_taps,
    sums,
    normed_wide,
    mlp_wide,
    normed_low,
    normed_turned,
    grads_low,
    grads_turned,
    hidden_even,
    hidden_odd,
    active_even,
    active_odd,
    grad_mixed,
    low_even,
    low_odd,
    back_even,
    back_odd,
    mlp_sum,
    normed_sum,
    weights,
    tap_sums,
    in_sum,
    out_sum,
    *,
    rows,
    breadth,
    pitch,
):
    image = pl.program_id(0)
    alive = (image < live_here(counts)).astype(jnp.float32)
    groups = fc_in.shape[1] // (2 * lanes)
    blocks = pitch // 8
    pixels = pixels_of(counts, rows * breadth)
    mean_two, rstd_two = norm_of(stats, pixels)
    gain_two, shift_two, scale_two = params[3:4, :], params[4:5, :], params[5:6, :]

    @pl.when(image == 0)
    def _():
        normed_wide[...] = jnp.zeros_like(normed_wide)
        mlp_wide[...] = jnp.zeros_like(mlp_wide)
        hidden_even[...] = jnp.zeros_like(hidden_even)
        hidden_odd[...] = jnp.zeros_like(hidden_odd)
        grad_mixed[...] = jnp.zeros_like(grad_mixed)
        tap_sums[...] = jnp.zeros_like(tap_sums)
        in_sum[...] = jnp.zeros_like(in_sum)
        out_sum[...] = jnp.zeros_like(out_sum)
        sums[...] = jnp.zeros_like(sums)
        scale_sum[...] = jnp.zeros_like(scale_sum)
        fill_weights(weights, taps, taps.shape[1])

    def normalized(value):
        return (value - mean_two) * rstd_two * gain_two + shift_two

    for source, offset, there in zip((far, near), sides((rows + 2) * pitch), present()):
        for r in range(2):
            at = pl.ds(pl.multiple_of(offset + r * pitch, 8), breadth)
            normed_wide[at, :] = there * normalized(source[0, r, 0:breadth, :])
    for r in range(rows):
        at = (r + 2) * pitch
        normed_wide[at : at + breadth, :] = normalized(first_sum[0, r, 0:breadth, :])
        at = (r + 1) * pitch
        mlp_wide[at : at + breadth, :] = cot[0, r].astype(jnp.float32) * alive * scale_two
    for source, offset in zip((cot_far, cot_near), sides((rows + 1) * pitch)):
        at = pl.ds(pl.multiple_of(offset, 8), breadth)
        mlp_wide[at, :] = source[0, 0].astype(wide) * alive * scale_two
    normed_low[...] = normed_wide[...].astype(jnp.bfloat16)
    grads_low[...] = mlp_wide[...].astype(jnp.bfloat16)
    inner = normed_wide[2 * pitch : (rows + 2) * pitch, :]
    normed_turned[...] = inner.T.astype(jnp.bfloat16)
    grads_turned[...] = mlp_wide[pitch : (rows + 1) * pitch, :].T.astype(jnp.bfloat16)
    mlp_sum[...] = jnp.zeros_like(mlp_sum)
    normed_sum[...] = jnp.zeros_like(normed_sum)

    hiddens, sources = (hidden_even, hidden_odd), (active_even, active_odd)
    actives, backs = (low_even, low_odd), (back_even, back_odd)

    def columns(group):
        return slice(group * 2 * lanes, (group + 1) * 2 * lanes)

    def enter(group):
        hid = jnp.dot(normed_low[...], fc_in[:, columns(group)], preferred_element_type=wide)
        hid = hid.astype(low).astype(wide)
        act = jnp.dot(grads_low[...], fc_out[:, columns(group)], preferred_element_type=wide)
        for half in range(2):
            lane = slice(half * lanes, (half + 1) * lanes)
            hiddens[group % 2][half, 8 : 8 + (rows + 4) * pitch, :] = hid[:, lane]
            sources[group % 2][half] = act[:, lane]

    def forward(group, half, block):
        hidden, source, active = (refs[group % 2] for refs in (hiddens, sources, actives))
        lane = slice(half * lanes, (half + 1) * lanes)
        place, base = group * 2 + half, block * 8
        mixed = window_sums(
            lambda r, s: hidden[half, pl.ds(base + (8 + r * pitch + s), 8), :],
            lambda t: weights[place, t],
            3,
            1,
            rows + 2,
            False,
        )
        for o in range(rows + 2):
            x = mixed[o]
            cdf, density = normal_parts(x)
            slope = cdf + x * density
            grad_mixed[half, pl.ds(base + (8 + o * pitch), 8), :] = (
                source[half, pl.ds(base + o * pitch, 8), :] * slope
            )
            if 1 <= o <= rows:
                active[pl.ds(base + (o - 1) * pitch, 8), lane] = x * cdf

    def backward(group, half, block):
        hidden, back = hiddens[group % 2], backs[group % 2]
        lane = slice(half * lanes, (half + 1) * lanes)
        place, base = group * 2 + half, block * 8

        def add_tap(t, value):
            tap_sums[place, t] += value

        total = window_sums(
            lambda r, s: grad_mixed[half, pl.ds(base + (8 + r * pitch + s), 8), :],
            lambda t: weights[place, t],
            3,
            1,
            rows,
            True,
            [hidden[half, pl.ds(base + (8 + (p + 2) * pitch), 8), :] for p in range(rows)],
            add_tap,
        )
        for p in range(rows):
            back[pl.ds(base + p * pitch, 8), lane] = total[p]

    def leave(group):
        act_low = actives[group % 2][...].astype(low)
        hid_low = backs[group % 2][...].astype(low)
        mlp_sum[...] += lax.dot_general(
            act_low,
            fc_out[:, columns(group)],
            (((1,), (1,)), ((), ())),
            preferred_element_type=wide,
        )
        normed_sum[...] += lax.dot_general(
            hid_low,
            fc_in[:, columns(group)],
            (((1,), (1,)), ((), ())),
            preferred_element_type=wide,
        )
        part_in = jnp.dot(normed_turned[...], hid_low, preferred_element_type=wide)
        part_out = jnp.dot(grads_turned[...], act_low, preferred_element_type=wide)
        for half in range(2):
            lane = slice(half * lanes, (half + 1) * lanes)
            in_sum[group * 2 + half] += part_in[:, lane]
            out_sum[group * 2 + half] += part_out[:, lane]

    enter(0)
    for group in range(groups):
        if group + 1 < groups:
            enter(group + 1)
        if group > 0:
            leave(group - 1)
        for half in range(2):
            for block in range(blocks):
                forward(group, half, block)
        for half in range(2):
            for block in range(blocks):
                backward(group, half, block)
    leave(groups - 1)

    scale_grad = jnp.zeros_like(scale_two)
    shift_grad = jnp.zeros_like(scale_two)
    gain_grad = jnp.zeros_like(scale_two)
    for r in range(rows):
        mlp = mlp_sum[r * pitch : r * pitch + breadth, :]
        back = normed_sum[r * pitch : r * pitch + breadth, :]
        first = first_sum[0, r, 0:breadth, :]
        out_image[0, r] = (alive * (first + scale_two * mlp)).astype(jnp.bfloat16)
        grad_normed[0, r * pitch : r * pitch + breadth, :] = back
        grad_normed[0, r * pitch + breadth : (r + 1) * pitch, :] = jnp.zeros(
            (pitch - breadth, back.shape[1]), wide
        )
        grad = cot[0, r].astype(jnp.float32) * alive
        scale_grad += jnp.sum(grad * mlp, axis=0, keepdims=True)
        shift_grad += jnp.sum(back, axis=0, keepdims=True)
        gain_grad += jnp.sum(back * (first - mean_two) * rstd_two, axis=0, keepdims=True)
    sums[0:1, :] += shift_grad
    sums[1:2, :] += gain_grad
    scale_sum[...] += scale_grad

    @pl.when(image == pl.num_programs(0) - 1)
    def _():
        copies[...] = jnp.broadcast_to(sums[...][None], copies.shape)
        odd = lax.axis_index("strip") % 2

        @pl.when(odd == 0)
        def _():
            fc_kept[...] = in_sum[...].astype(low)
            fc_sent[...] = out_sum[...].astype(low)

        @pl.when(odd == 1)
        def _():
            fc_kept[...] = out_sum[...].astype(low)
            fc_sent[...] = in_sum[...].astype(low)

        store_taps(grad_taps, tap_sums, taps.shape[1])


def unpack_kernel(own, other, grad_in, grad_out):
    def spread(source, target):
        for g in range(source.shape[0]):
            target[:, g * lanes : (g + 1) * lanes] = source[g].astype(wide)

    odd = lax.axis_index("strip") % 2

    @pl.when(odd == 0)
    def _():
        spread(own, grad_in)
        spread(other, grad_out)

    @pl.when(odd == 1)
    def _():
        spread(other, grad_in)
        spread(own, grad_out)


def mlp_block(
    counts, first_sum, far, near, cot, cot_far, cot_near, params, stats, fc_in, fc_out, taps
):
    images, rows, breadth, width = cot.shape
    pitch = first_sum.shape[2]
    deep = fc_in.shape[1]
    groups = deep // lanes
    return call(
        mlp_kernel,
        images,
        [
            (counts, smem),
            (first_sum, spec_image(rows, pitch, width)),
            (far, spec_image(2, pitch, width)),
            (near, spec_image(2, pitch, width)),
            (cot, spec_image(rows, breadth, width)),
            (cot_far, spec_image(1, breadth, width)),
            (cot_near, spec_image(1, breadth, width)),
            (params, spec_whole(8, width)),
            (stats, spec_whole(*stats.shape)),
            (fc_in, spec_whole(width, deep)),
            (fc_out.T, spec_whole(width, deep)),
            (taps, spec_whole(9, deep)),
        ],
        [
            (cot.shape, low, spec_image(rows, breadth, width)),
            ((images, rows * pitch, width), wide, spec_image(rows * pitch, width)),
            (stats.shape, wide, spec_whole(*stats.shape)),
            ((1, width), wide, spec_whole(1, width)),
            ((groups, width, lanes), low, spec_whole(groups, width, lanes)),
            ((groups, width, lanes), low, spec_whole(groups, width, lanes)),
            ((9, deep), wide, spec_whole(9, deep)),
        ],
        [
            ((2, width), wide),
            (((rows + 4) * pitch, width), wide),
            (((rows + 2) * pitch, width), wide),
            (((rows + 4) * pitch, width), low),
            ((width, rows * pitch), low),
            (((rows + 2) * pitch, width), low),
            ((width, rows * pitch), low),
            ((2, (rows + 4) * pitch + 16, lanes), wide),
            ((2, (rows + 4) * pitch + 16, lanes), wide),
            ((2, (rows + 2) * pitch, lanes), wide),
            ((2, (rows + 2) * pitch, lanes), wide),
            ((2, (rows + 2) * pitch + 16, lanes), wide),
            ((rows * pitch, 2 * lanes), wide),
            ((rows * pitch, 2 * lanes), wide),
            ((rows * pitch, 2 * lanes), wide),
            ((rows * pitch, 2 * lanes), wide),
            ((rows * pitch, width), wide),
            ((rows * pitch, width), wide),
            ((groups, 9, 8, lanes), wide),
            ((groups, 9, 8, lanes), wide),
            ((groups, width, lanes), wide),
            ((groups, width, lanes), wide),
        ],
        53,
        "mlp",
        vmem=28,
        rows=rows,
        breadth=breadth,
        pitch=pitch,
    )


def body(
    images,
    counts,
    gain_one,
    shift_one,
    proj_in,
    kernel_five,
    kernel_seven,
    lka_proj,
    proj_out,
    scale_one,
    gain_two,
    shift_two,
    fc_in,
    kernel_three,
    fc_out,
    scale_two,
    cotangent,
):
    slots, rows, breadth, width = images.shape
    pitch = -(-(breadth + 2) // 8) * 8
    gap = -(-(breadth + 9) // 8) * 8
    flat = rows * pitch
    blank = jnp.zeros_like(gain_one)
    params = jnp.stack(
        [gain_one, shift_one, scale_one, gain_two, shift_two, scale_two, blank, blank]
    ).astype(wide)
    sizes = dict(rows=rows, breadth=breadth, pitch=pitch)
    vec = spec_whole(8, width)
    devices = device_count()
    blocks = (devices, 2, width)
    two = spec_whole(*blocks)
    square = spec_whole(width, width)
    image_spec = spec_image(rows, breadth, width)
    pairs = slots // 2
    chunks = [(0, pairs - 1), (pairs - 1, 1)]
    pair_width = 2 * width
    pair_square = spec_whole(pair_width, pair_width)
    pair_flat = (pairs, flat, pair_width)
    flat_spec = spec_image(flat, width)
    flat_shape = (slots, flat, width)
    row_shape = (slots, rows, pitch, width)
    groups = len(pair_groups(width))
    kinds = width // lanes + 1
    five_spec = spec_whole(*kernel_five.shape)
    seven_spec = spec_whole(*kernel_seven.shape)

    (first_part,) = call(
        stats_kernel,
        slots,
        [(counts, smem), (images, image_spec)],
        [(blocks, wide, two)],
        [((2, width), wide)],
        2,
        "input_sums",
    )
    pair_in, pair_lka, pair_out = (pair_matrix(m) for m in (proj_in, lka_proj, proj_out))
    first_part, images_after, cot_after = lax.optimization_barrier((first_part, images, cotangent))
    image_far, image_near = far_and_near(
        *(
            jnp.concatenate(parts, axis=1)
            for parts in zip(edge_rows(images_after, 2), edge_rows(cot_after, 1))
        )
    )
    first_stats = from_all(first_part)
    gelu_low = pre_gelu = cot_far = cot_near = None
    cot_shape = (slots, 1, breadth, width)
    mids, rims = [], []
    for start, count in chunks:
        gelu_low, pre_gelu, mid, cot_far, cot_near = call(
            front_kernel,
            count,
            [
                (counts, smem),
                (images, spec_two(start, rows, breadth, width)),
                (image_far, spec_two(start, 3, breadth, width)),
                (image_near, spec_two(start, 3, breadth, width)),
                (params, vec),
                (first_stats, two),
                (pair_in, pair_square),
                (kernel_five, five_spec),
            ],
            [
                (pair_flat, low, spec_from(start, flat, pair_width), gelu_low),
                (pair_flat, low, spec_from(start, flat, pair_width), pre_gelu),
                ((count, rows, pitch, pair_width), low, spec_image(rows, pitch, pair_width)),
                (cot_shape, low, spec_two(start, 1, breadth, width), cot_far),
                (cot_shape, low, spec_two(start, 1, breadth, width), cot_near),
            ],
            [
                (((rows + 4) * pitch, pair_width), wide),
                ((groups, (rows + 4) * pitch + 16, lanes), wide),
                ((kinds, 25, 8, lanes), wide),
                (((rows + 4) * pitch, lanes), wide),
                ((flat, pair_width), wide),
            ],
            4.3 * count,
            f"normed_to_five_{start}",
            **sizes,
        )
        mids.append(mid)
        rims.append(far_and_near(mid, mid))
    lka_low = attend = first_sum = None
    second_part = jnp.zeros(blocks, wide)
    for (start, count), mid, (mid_far, mid_near) in zip(chunks, mids, rims):
        rim_spec = spec_image(rows, pitch, pair_width)
        pair_spec = spec_from(start, flat, pair_width)
        lka_low, attend, first_sum, second_part = call(
            attend_kernel,
            count,
            [
                (counts, smem),
                (images, spec_two(start, rows, breadth, width)),
                (mid, rim_spec),
                (mid_far, rim_spec),
                (mid_near, rim_spec),
                (gelu_low, pair_spec),
                (params, vec),
                (first_stats, two),
                (second_part, two),
                (pair_lka, pair_square),
                (pair_out, pair_square),
                (kernel_seven, seven_spec),
            ],
            [
                (pair_flat, low, pair_spec, lka_low),
                (pair_flat, low, pair_spec, attend),
                (flat_shape, wide, spec_two(start, flat, width), first_sum),
                (blocks, wide, two),
            ],
            [
                ((2, width), wide),
                ((groups, 3 * rows * gap + 48, lanes), wide),
                ((kinds, 49, 8, lanes), wide),
                ((flat, pair_width), wide),
                ((flat, pair_width), wide),
                ((flat, pair_width), wide),
            ],
            6.2 * count,
            f"seven_to_first_sum_{start}",
            vmem=20,
            gap=gap,
            start_pair=start,
            **sizes,
        )
    first_rows = first_sum.reshape(row_shape)
    sum_far, sum_near = far_and_near(*edge_rows(first_rows, 2))
    second_stats = from_all(second_part)
    out_image, grad_normed_two, third_part, scale_two_part, fc_kept, fc_sent, grad_kernel_three = mlp_block(
        counts,
        first_rows,
        sum_far,
        sum_near,
        cotangent,
        cot_far,
        cot_near,
        params,
        second_stats,
        fc_in,
        fc_out,
        kernel_three,
    )
    grad_second = from_all(third_part)
    fc_kept, fc_sent, grad_second = lax.optimization_barrier((fc_kept, fc_sent, grad_second))
    got = lax.ppermute(fc_sent, "strip", near_pairs())
    half = (fc_kept.astype(wide) + got.astype(wide)).astype(low)
    sides_of = [[d for d in range(devices) if d % 2 == k] for k in range(2)]
    fc_share = jnp.sum(
        lax.all_to_all(
            half.reshape(devices // 2, -1, lanes),
            ("dp", "strip"),
            0,
            0,
            axis_index_groups=sides_of,
        ).astype(wide),
        axis=0,
    ).astype(low)
    grad_first = grad_direct = None
    gates, rims = [], []
    lka_sum = out_sum = jnp.zeros((width, width), wide)
    scale_sum = jnp.zeros((1, width), wide)
    for start, count in chunks:
        pair_spec = spec_from(start, flat, pair_width)
        grad_first, grad_direct, grad_lka, lka_sum, out_sum, scale_sum = call(
            gate_kernel,
            count,
            [
                (counts, smem),
                (first_sum, spec_two(start, flat, width)),
                (images, spec_two(start, rows, breadth, width)),
                (cotangent, spec_two(start, rows, breadth, width)),
                (grad_normed_two, spec_two(start, flat, width)),
                (lka_low, pair_spec),
                (attend, pair_spec),
                (gelu_low, pair_spec),
                (params, vec),
                (second_stats, two),
                (grad_second, two),
                (pair_lka, pair_square),
                (pair_out, pair_square),
                (lka_sum, square),
                (out_sum, square),
                (scale_sum, spec_whole(1, width)),
            ],
            [
                (pair_flat, wide, pair_spec, grad_first),
                (pair_flat, low, pair_spec, grad_direct),
                ((count, rows, pitch, pair_width), low, spec_image(rows, pitch, pair_width)),
                ((width, width), wide, square),
                ((width, width), wide, square),
                ((1, width), wide, spec_whole(1, width)),
            ],
            [
                ((flat, pair_width), wide),
                ((flat, pair_width), wide),
                ((flat, pair_width), wide),
            ],
            3.2 * count,
            f"gate_backward_{start}",
            vmem=52,
            start_pair=start,
            **sizes,
        )
        gates.append(grad_lka)
        rims.append(far_and_near(grad_lka, grad_lka))
    grad_mid = None
    seven_sum = jnp.zeros(kernel_seven.shape, wide)
    for (start, count), grad_lka, mid, (lka_far, lka_near) in zip(chunks, gates, mids, rims):
        rim_spec = spec_image(rows, pitch, pair_width)
        grad_mid, seven_sum = call(
            seven_kernel,
            count,
            [
                (grad_lka, rim_spec),
                (lka_far, rim_spec),
                (lka_near, rim_spec),
                (mid, rim_spec),
                (kernel_seven, seven_spec),
                (seven_sum, seven_spec),
            ],
            [
                (
                    (pairs, rows, pitch, pair_width),
                    low,
                    spec_from(start, rows, pitch, pair_width),
                    grad_mid,
                ),
                (kernel_seven.shape, wide, seven_spec),
            ],
            [
                ((groups, 3 * rows * gap + 48, lanes), wide),
                ((groups, flat, lanes), wide),
                ((flat, pair_width), wide),
                ((kinds, 49, 8, lanes), wide),
                ((kinds, 49, 8, lanes), wide),
            ],
            7 * count,
            f"seven_backward_{start}",
            vmem=20,
            gap=gap,
            **sizes,
        )
    five_far, five_near = far_and_near(*edge_rows(grad_mid, 2))
    fc_share, five_far, five_near = lax.optimization_barrier((fc_share, five_far, five_near))
    fc_own = lax.all_to_all(
        jnp.broadcast_to(fc_share[None], (devices // 2,) + fc_share.shape),
        ("dp", "strip"),
        0,
        0,
        axis_index_groups=sides_of,
    ).reshape(fc_kept.shape)
    pair_spec = spec_image(flat, pair_width)
    deep = fc_in.shape[1]
    total_rows = pack_rows(width, deep)
    grad_partial, packed = call(
        five_kernel,
        pairs,
        [
            (counts, smem),
            (images, spec_two(0, rows, breadth, width)),
            (grad_mid, spec_image(rows, pitch, pair_width)),
            (five_far, spec_image(2, pitch, pair_width)),
            (five_near, spec_image(2, pitch, pair_width)),
            (gelu_low, pair_spec),
            (pre_gelu, pair_spec),
            (grad_direct, pair_spec),
            (grad_first, pair_spec),
            (params, vec),
            (first_stats, two),
            (pair_in, pair_square),
            (kernel_five, five_spec),
            (lka_sum, square),
            (out_sum, square),
            (seven_sum, seven_spec),
            (grad_kernel_three, spec_whole(*kernel_three.shape)),
            (scale_sum, spec_whole(1, width)),
            (scale_two_part, spec_whole(1, width)),
        ],
        [
            (flat_shape, wide, spec_two(0, flat, width)),
            ((total_rows + 8, width), low, spec_whole(total_rows + 8, width)),
        ],
        [
            ((width, width), wide),
            (kernel_five.shape, wide),
            ((2, width), wide),
            ((total_rows + 8, width), wide),
            ((groups, (rows + 4) * pitch + 16, lanes), wide),
            ((groups, flat, lanes), wide),
            ((flat, pair_width), wide),
            ((kinds, 25, 8, lanes), wide),
            ((kinds, 25, 8, lanes), wide),
            ((flat, pair_width), wide),
            ((flat, pair_width), wide),
        ],
        6 * pairs,
        "five_backward",
        vmem=52,
        **sizes,
    )
    fc_own, packed = lax.optimization_barrier((fc_own, packed))
    share, vectors = split_sums(packed, 8)
    fc_other = lax.ppermute(fc_own, "strip", near_pairs())
    (grad_images,) = call(
        last_kernel,
        slots,
        [
            (counts, smem),
            (images, image_spec),
            (grad_partial, flat_spec),
            (params, vec),
            (first_stats, two),
            (vectors, spec_whole(8, width)),
        ],
        [(images.shape, wide, image_spec)],
        [],
        4,
        "input_gradient",
        **sizes,
    )
    matrices, grad_images = joined(share, grad_images)
    pieces = call(
        spread_kernel,
        1,
        [(matrices, spec_whole(total_rows, width))],
        [
            (shape, wide, spec_whole(*shape))
            for shape in [(width, width)] * 3
            + [kernel_five.shape, kernel_seven.shape, kernel_three.shape]
        ],
        [],
        2,
        "attention_gradients",
    )
    grad_fc_in, grad_fc_out = call(
        unpack_kernel,
        1,
        [(half, spec_whole(*half.shape)) for half in (fc_own, fc_other)],
        [
            ((width, deep), wide, spec_whole(width, deep)),
            ((width, deep), wide, spec_whole(width, deep)),
        ],
        [],
        2,
        "weight_gradients",
    )
    vectors = vectors.astype(wide)
    grad_second = jnp.sum(grad_second, axis=0)
    return (
        out_image,
        grad_images,
        vectors[1],
        vectors[0],
        pieces[0],
        pieces[3],
        pieces[4],
        pieces[1],
        pieces[2],
        vectors[2],
        grad_second[1],
        grad_second[0],
        grad_fc_in,
        pieces[5],
        grad_fc_out.T,
        vectors[3],
    )


def solution(mesh):
    split = P("dp", "strip", None, None)
    return jax.shard_map(
        body,
        mesh=mesh,
        in_specs=(split,) + (P(),) * 15 + (split,),
        out_specs=(split, split) + (P(),) * 14,
        check_vma=False,
    )
```

```python
import functools

import jax
import jax.numpy as jnp
from jax import lax
from jax.experimental import pallas as pl
from jax.experimental.pallas import tpu as pltpu
from jax.sharding import PartitionSpec as P

epsilon = 1e-05
lanes = 128
smem = pl.BlockSpec(memory_space=pltpu.SMEM)
wide = jnp.float32
low = jnp.bfloat16


def exchange_steps():
    return [
        (axis, 1 << bit)
        for axis in ("strip", "dp")
        for bit in range(lax.axis_size(axis).bit_length() - 1)
    ]


def swapped(value, axis, bit):
    return lax.ppermute(value, axis, [(i, i ^ bit) for i in range(lax.axis_size(axis))])


def device_count():
    return lax.axis_size("dp") * lax.axis_size("strip")


def from_all(copies):
    return lax.all_to_all(copies, ("dp", "strip"), 0, 0)


def split_sums(part, sent, size):
    for place, (axis, bit) in enumerate(exchange_steps()):
        length = part.shape[0] - size
        if 0 < place < 3:
            upper = (lax.axis_index(axis) // bit) % 2
            tail = part[length:]
            halves = part[:length].reshape((2, length // 2) + part.shape[1:])
            sent = lax.dynamic_index_in_dim(halves, 1 - upper, 0, False)
            kept = lax.dynamic_index_in_dim(halves, upper, 0, False)
            sent, part = jnp.concatenate([sent, tail]), jnp.concatenate([kept, tail])
        elif place > 0:
            sent = part
        got = swapped(sent, axis, bit)
        part = (part.astype(wide) + got.astype(wide)).astype(low)
    return part[: part.shape[0] - size], part[part.shape[0] - size :]


def joined(part, beside):
    for place, (axis, bit) in enumerate(reversed(exchange_steps()[:3])):
        if place > 0:
            part, beside[place - 1] = lax.optimization_barrier((part, beside[place - 1]))
        upper = (lax.axis_index(axis) // bit) % 2
        got = swapped(part, axis, bit)
        part = jnp.where(
            upper == 0, jnp.concatenate([part, got]), jnp.concatenate([got, part])
        )
    return part, beside


def near_pairs():
    return [(i, i ^ 1) for i in range(lax.axis_size("strip"))]


def far_and_near(far, near):
    count = lax.axis_size("strip")
    pairs = [(i, i + 1) for i in range(1, count - 1, 2)]
    return (
        lax.ppermute(far, "strip", pairs + [(j, i) for i, j in pairs]),
        lax.ppermute(near, "strip", near_pairs()),
    )


def edge_rows(value, width):
    odd = lax.axis_index("strip") % 2
    length = value.shape[1] - width
    return (
        lax.dynamic_slice_in_dim(value, odd * length, width, 1),
        lax.dynamic_slice_in_dim(value, (1 - odd) * length, width, 1),
    )


def sides(length):
    odd = lax.axis_index("strip") % 2
    return odd * length, (1 - odd) * length


def present():
    strip, count = lax.axis_index("strip"), lax.axis_size("strip")
    above, below = (strip > 0).astype(wide), (strip < count - 1).astype(wide)
    odd = (strip % 2).astype(wide)
    return odd * below + (1 - odd) * above, odd * above + (1 - odd) * below


def normal_parts(x):
    density = jnp.exp2(x * x * -0.7213475204444817 - 1.3257480647361595)
    scale = 1.0 + 0.2316419 * jnp.abs(x)
    guess = pl.reciprocal(scale, approx=True)
    t = guess * (2.0 - scale * guess)
    poly = 1.781477937 + t * (-1.821255978 + t * 1.330274429)
    poly = t * (0.319381530 + t * (-0.356563782 + t * poly))
    tail = density * poly
    return jnp.where(x > 0, 1.0 - tail, tail), density


def window_sums(load, weight, across, spread, rows, back, center=None, add_tap=None):
    total = [None] * rows
    reach = spread * (across - 1)
    for j in range(across):
        shift = (j - across // 2) * spread * (-1 if back else 1)
        w = [weight(i * across + j) for i in range(across)]
        tap = [None] * across
        for r in range(rows + reach):
            v = load(r, shift)
            for i in range(across):
                o = r - reach + spread * i if back else r - spread * i
                if 0 <= o < rows:
                    term = v * w[i]
                    total[o] = term if total[o] is None else total[o] + term
                    if center is not None:
                        term = v * center[o]
                        tap[i] = term if tap[i] is None else tap[i] + term
        if center is not None:
            for i in range(across):
                add_tap(i * across + j, tap[i])
    return total


def lane_groups(width):
    return [(start, min(lanes, width - start)) for start in range(0, width, lanes)]


def fill_weights(weights, taps, width):
    weights[...] = jnp.zeros_like(weights)
    for g, (start, size) in enumerate(lane_groups(width)):
        for t in range(taps.shape[0]):
            weights[g, t, :, 0:size] = jnp.broadcast_to(
                taps[t : t + 1, start : start + size].astype(wide), (8, size)
            )


def store_taps(grad_taps, tap_sums, width):
    for g, (start, size) in enumerate(lane_groups(width)):
        for t in range(grad_taps.shape[0]):
            grad_taps[t : t + 1, start : start + size] = jnp.sum(
                tap_sums[g, t, :, 0:size], axis=0, keepdims=True
            )


def inside(rows, pitch, breadth, width):
    place = lax.broadcasted_iota(jnp.int32, (rows, pitch, width), 1)
    return jnp.where(place < breadth, 1.0, 0.0).reshape(rows * pitch, width)


def live_here(counts):
    return counts[lax.axis_index("dp")]


def pixels_of(counts, area):
    total = counts[0]
    for k in range(1, counts.shape[0]):
        total += counts[k]
    return total.astype(wide) * (area * lax.axis_size("strip"))


def norm_of(blocks, pixels):
    stats = jnp.sum(blocks[...], axis=0) / pixels
    mean = stats[0:1, :]
    return mean, lax.rsqrt(stats[1:2, :] - mean * mean + epsilon)


def spec_image(*shape):
    return pl.BlockSpec((1,) + shape, lambda i: (i,) + (0,) * len(shape))


def spec_from(start, *shape):
    return pl.BlockSpec((1,) + shape, lambda i: (i + start,) + (0,) * len(shape))


def spec_two(start, *shape):
    return pl.BlockSpec((2,) + shape, lambda i: (i + start,) + (0,) * len(shape))


def spec_whole(*shape):
    return pl.BlockSpec(shape, lambda i: (0,) * len(shape))


def call(kernel, steps, ins, outs, scratch, cost, name, vmem=44, **sizes):
    earlier = [out[3] for out in outs if len(out) > 3 and out[3] is not None]
    aliases, at = {}, len(ins)
    for place, out in enumerate(outs):
        if len(out) > 3 and out[3] is not None:
            aliases[at] = place
            at += 1

    def run(*refs):
        kernel(*refs[: len(ins)], *refs[at:], **sizes)

    return pl.pallas_call(
        run,
        grid=(steps,),
        in_specs=[spec for _, spec in ins] + [pl.BlockSpec(memory_space=pl.ANY)] * len(earlier),
        out_specs=[out[2] for out in outs],
        out_shape=[jax.ShapeDtypeStruct(out[0], out[1]) for out in outs],
        scratch_shapes=[pltpu.VMEM(shape, dtype) for shape, dtype in scratch],
        input_output_aliases=aliases,
        compiler_params=pltpu.CompilerParams(vmem_limit_bytes=vmem * 1024 * 1024),
        cost_estimate=pl.CostEstimate(
            flops=0, bytes_accessed=int(cost * 3.5e6), transcendentals=0
        ),
        name=name,
    )(*[array for array, _ in ins], *earlier)


def paired(value):
    return pair_lanes(value, value)


def pair_lanes(left, right):
    main = left.shape[-1] // lanes * lanes
    tails = jnp.concatenate([left[..., main:], right[..., main:]], axis=-1)
    return jnp.concatenate([left[..., :main], right[..., :main], tails], axis=-1)


def split_lanes(value):
    width = value.shape[-1] // 2
    main = width // lanes * lanes
    left = jnp.concatenate([value[..., :main], value[..., 2 * main : main + width]], axis=-1)
    right = jnp.concatenate([value[..., main : 2 * main], value[..., main + width :]], axis=-1)
    return left, right


def folded(value):
    left, right = split_lanes(value)
    return left + right


def folded_square(value):
    width = value.shape[0] // 2
    main = width // lanes * lanes
    left = split_lanes(jnp.concatenate([value[:main], value[2 * main : main + width]], axis=0))[0]
    right = split_lanes(jnp.concatenate([value[main : 2 * main], value[main + width :]], axis=0))[1]
    return left + right


def pair_matrix(matrix):
    blank = jnp.zeros_like(matrix)
    left = jnp.concatenate([matrix, blank], axis=1)
    right = jnp.concatenate([blank, matrix], axis=1)
    width = matrix.shape[0]
    main = width // lanes * lanes

    def columns(value):
        return jnp.concatenate(
            [
                value[:, :main],
                value[:, width : width + main],
                value[:, main:width],
                value[:, width + main :],
            ],
            axis=1,
        )

    left, right = columns(left), columns(right)
    return jnp.concatenate([left[:main], right[:main], left[main:], right[main:]])


def pair_groups(width):
    main = width // lanes
    return [(g * lanes, g % main) for g in range(2 * main)] + [(2 * main * lanes, main)]


def fill_pair_weights(weights, taps, width):
    main = width // lanes * lanes
    for t in range(taps.shape[0]):
        row = taps[t : t + 1, :].astype(wide)
        tail = row[:, main:]
        for g in range(main // lanes):
            weights[g, t] = jnp.broadcast_to(row[:, g * lanes : (g + 1) * lanes], (8, lanes))
        weights[main // lanes, t] = jnp.broadcast_to(
            jnp.concatenate([tail, tail], axis=1), (8, lanes)
        )


def store_pair_taps(grad_taps, tap_sums, width):
    main = width // lanes * lanes
    for t in range(grad_taps.shape[0]):
        for g in range(main // lanes):
            grad_taps[t : t + 1, g * lanes : (g + 1) * lanes] = jnp.sum(
                tap_sums[g, t], axis=0, keepdims=True
            )
        tail = jnp.sum(tap_sums[main // lanes, t], axis=0, keepdims=True)
        grad_taps[t : t + 1, main:width] = tail[:, : width - main] + tail[:, width - main :]


def alive_lanes(counts, start, width):
    main = width // lanes * lanes
    image = 2 * (pl.program_id(0) + start)
    at = lax.broadcasted_iota(jnp.int32, (1, 2 * width), 1)
    second = ((at >= main) & (at < 2 * main)) | (at >= main + width)
    return jnp.where(image + second.astype(jnp.int32) < live_here(counts), 1.0, 0.0)


def stats_kernel(counts, images, copies, sums):
    image = pl.program_id(0)

    @pl.when(image == 0)
    def _():
        sums[...] = jnp.zeros_like(sums)

    alive = (image < live_here(counts)).astype(wide)
    total = jnp.zeros((images.shape[2], images.shape[3]), wide)
    square = total
    for r in range(images.shape[1]):
        value = images[0, r].astype(wide)
        total += value
        square += value * value
    sums[0:1, :] += jnp.sum(total, axis=0, keepdims=True) * alive
    sums[1:2, :] += jnp.sum(square, axis=0, keepdims=True) * alive

    @pl.when(image == pl.num_programs(0) - 1)
    def _():
        copies[...] = jnp.broadcast_to(sums[...][None], copies.shape)


def front_kernel(
    counts,
    images,
    far,
    near,
    params,
    stats,
    proj_in,
    taps,
    gelu_low,
    pre_gelu,
    lka_mid,
    cot_far,
    cot_near,
    values,
    gelu,
    weights,
    mask,
    mid,
    *,
    rows,
    breadth,
    pitch,
):
    width = images.shape[3]
    pixels = pixels_of(counts, rows * breadth)
    mean, rstd = norm_of(stats, pixels)
    mean, rstd = paired(mean), paired(rstd)
    gain, shift = paired(params[0:1, :]), paired(params[1:2, :])

    @pl.when(pl.program_id(0) == 0)
    def _():
        values[...] = jnp.zeros_like(values)
        gelu[...] = jnp.zeros_like(gelu)
        fill_pair_weights(weights, taps, width)
        mask[...] = inside(rows + 4, pitch, breadth, lanes)
        for offset, there in zip(sides((rows + 2) * pitch), present()):
            at = pl.ds(pl.multiple_of(offset, 8), 2 * pitch)
            mask[at, :] = mask[at, :] * there

    def place(at, source, r):
        value = pair_lanes(source[0, r].astype(wide), source[1, r].astype(wide))
        values[pl.ds(at, breadth), :] = (value - mean) * rstd * gain + shift

    for k in range(2):
        cot_far[k, 0] = far[k, 2]
        cot_near[k, 0] = near[k, 2]
    for source, offset in zip((far, near), sides((rows + 2) * pitch)):
        for r in range(2):
            place(pl.multiple_of(offset + r * pitch, 8), source, r)
    for r in range(rows):
        place((r + 2) * pitch, images, r)
    pre = jnp.dot(values[...].astype(low), proj_in[...], preferred_element_type=wide)
    pre_gelu[0] = pre[2 * pitch : (rows + 2) * pitch, :].astype(low)
    for g, (start, _) in enumerate(pair_groups(width)):
        part = pre[:, start : start + lanes]
        cdf, _ = normal_parts(part)
        rounded = (part * cdf * mask[...]).astype(low).astype(wide)
        gelu_low[0, :, start : start + lanes] = rounded[2 * pitch : (rows + 2) * pitch].astype(low)
        gelu[g, 8 : 8 + (rows + 4) * pitch, :] = rounded
    for g, (start, which) in enumerate(pair_groups(width)):

        def step(block, carry, g=g, start=start, which=which):
            base = pl.multiple_of(block * 8, 8)
            total = window_sums(
                lambda r, s: gelu[g, pl.ds(base + (8 + r * pitch + s), 8), :],
                lambda t: weights[which, t],
                5,
                1,
                rows,
                False,
            )
            for o in range(rows):
                mid[pl.ds(base + o * pitch, 8), start : start + lanes] = total[o]
            return carry

        lax.fori_loop(0, pitch // 8, step, 0)
    for r in range(rows):
        at = r * pitch
        lka_mid[0, r] = (
            mid[at : at + pitch, :] * inside(1, pitch, breadth, 2 * width)
        ).astype(low)


def attend_kernel(
    counts,
    images,
    lka_mid,
    far,
    near,
    gelu_low,
    params,
    stats,
    earlier_sums,
    lka_proj,
    proj_out,
    taps,
    lka_low,
    attend_out,
    first_sum,
    copies,
    sums,
    window,
    weights,
    lka,
    values,
    mask,
    *,
    rows,
    breadth,
    pitch,
    gap,
    start_pair,
):
    width = images.shape[3]
    alive = alive_lanes(counts, start_pair, width)
    pixels = pixels_of(counts, rows * breadth)
    mean, rstd = norm_of(stats, pixels)
    mean, rstd = paired(mean), paired(rstd)
    gain, shift, scale = (paired(params[k : k + 1, :]) for k in range(3))

    @pl.when(pl.program_id(0) == 0)
    def _():
        window[...] = jnp.zeros_like(window)
        values[...] = jnp.zeros_like(values)
        sums[...] = earlier_sums[0]
        fill_pair_weights(weights, taps, width)
        mask[...] = inside(rows, pitch, breadth, 2 * width)

    far_at, near_at = sides(2 * rows * gap)
    for offset, source in ((far_at, far), (rows * gap, lka_mid), (near_at, near)):
        for r in range(rows):
            at = pl.ds(pl.multiple_of(offset + (16 + r * gap), 8), pitch)
            for g, (start, _) in enumerate(pair_groups(width)):
                window[g, at, :] = source[0, r, :, start : start + lanes].astype(wide)
    for g, (start, which) in enumerate(pair_groups(width)):

        def step(block, carry, g=g, start=start, which=which):
            base = pl.multiple_of(block * 8, 8)
            total = window_sums(
                lambda r, s: window[g, pl.ds(base + (16 + r * gap + s), 8), :],
                lambda t: weights[which, t],
                7,
                3,
                rows,
                False,
            )
            for o in range(rows):
                lka[pl.ds(base + o * pitch, 8), start : start + lanes] = total[o]
            return carry

        lax.fori_loop(0, pitch // 8, step, 0)
    for r in range(rows):
        values[r * pitch : r * pitch + breadth, :] = pair_lanes(
            images[0, r].astype(wide), images[1, r].astype(wide)
        )
    low_lka = lka[...].astype(low)
    lka_low[0] = low_lka
    attend = jnp.dot(low_lka, lka_proj[...], preferred_element_type=wide)
    attend_out[0] = attend.astype(low)
    gated = (gelu_low[0].astype(wide) * attend).astype(low)
    branch = jnp.dot(gated, proj_out[...], preferred_element_type=wide)
    attn = (branch + ((values[...] - mean) * rstd * gain + shift)) * mask[...]
    first = values[...] + scale * attn
    first_sum[0], first_sum[1] = split_lanes(first)
    sums[0:1, :] += folded(jnp.sum(first, axis=0, keepdims=True) * alive)
    sums[1:2, :] += folded(jnp.sum(first * first, axis=0, keepdims=True) * alive)

    @pl.when(pl.program_id(0) == pl.num_programs(0) - 1)
    def _():
        copies[...] = jnp.broadcast_to(sums[...][None], copies.shape)


def gate_kernel(
    counts,
    first_sum,
    images,
    cot,
    grad_normed,
    lka_low,
    attend,
    gelu_low,
    params,
    stats,
    grad_stats,
    lka_proj,
    proj_out,
    lka_before,
    out_before,
    scale_before,
    grad_first,
    grad_direct,
    grad_lka,
    grad_lka_proj,
    grad_proj_out,
    sums,
    values,
    pixels_in,
    mask,
    *,
    rows,
    breadth,
    pitch,
    start_pair,
):
    width = cot.shape[3]
    alive = alive_lanes(counts, start_pair, width)
    pixels = pixels_of(counts, rows * breadth)
    mean, rstd = norm_of(stats, pixels)
    mean, rstd = paired(mean), paired(rstd)
    scale, gain = paired(params[2:3, :]), paired(params[3:4, :])
    grad_sums = jnp.sum(grad_stats[...], axis=0)
    shift_sum, gain_sum = paired(grad_sums[0:1, :]), paired(grad_sums[1:2, :])

    @pl.when(pl.program_id(0) == 0)
    def _():
        values[...] = jnp.zeros_like(values)
        pixels_in[...] = jnp.zeros_like(pixels_in)
        mask[...] = inside(rows, pitch, breadth, 2 * width)
        sums[...] = scale_before[...]
        grad_lka_proj[...] = lka_before[...]
        grad_proj_out[...] = out_before[...]

    for r in range(rows):
        values[r * pitch : r * pitch + breadth, :] = pair_lanes(
            cot[0, r].astype(wide), cot[1, r].astype(wide)
        )
        pixels_in[r * pitch : r * pitch + breadth, :] = pair_lanes(
            images[0, r].astype(wide), images[1, r].astype(wide)
        )
    summed = pair_lanes(first_sum[0], first_sum[1])
    yhat = (summed - mean) * rstd
    inner = pair_lanes(grad_normed[0], grad_normed[1]) - (shift_sum + yhat * gain_sum) / pixels
    first = alive * (values[...] + rstd * gain * inner) * mask[...]
    grad_first[0] = first
    sums[...] += folded(
        jnp.sum(first * (summed - pixels_in[...]), axis=0, keepdims=True) / scale
    )
    branch = (first * scale).astype(low)
    gated_back = lax.dot_general(
        branch, proj_out[...], (((1,), (1,)), ((), ())), preferred_element_type=wide
    )
    gelu = gelu_low[0].astype(wide)
    attended = attend[0].astype(wide)
    gated = gelu * attended
    grad_proj_out[...] += folded_square(
        jnp.dot(gated.T.astype(low), branch, preferred_element_type=wide)
    )
    grad_direct[0] = (gated_back * attended).astype(low)
    back = (gated_back * gelu).astype(low)
    lka = lax.dot_general(
        back, lka_proj[...], (((1,), (1,)), ((), ())), preferred_element_type=wide
    )
    grad_lka_proj[...] += folded_square(
        jnp.dot(lka_low[0].astype(wide).T.astype(low), back, preferred_element_type=wide)
    )
    for r in range(rows):
        grad_lka[0, r] = lka[r * pitch : (r + 1) * pitch, :].astype(low)


def seven_kernel(
    grad_lka,
    far,
    near,
    lka_mid,
    taps,
    taps_before,
    grad_mid,
    grad_taps,
    window,
    middle,
    out,
    weights,
    tap_sums,
    *,
    rows,
    breadth,
    pitch,
    gap,
):
    width = taps.shape[1]

    @pl.when(pl.program_id(0) == 0)
    def _():
        window[...] = jnp.zeros_like(window)
        tap_sums[...] = jnp.zeros_like(tap_sums)
        fill_pair_weights(weights, taps, width)

    far_at, near_at = sides(2 * rows * gap)
    for g, (start, _) in enumerate(pair_groups(width)):
        for offset, source in ((far_at, far), (rows * gap, grad_lka), (near_at, near)):
            for r in range(rows):
                at = pl.ds(pl.multiple_of(offset + (16 + r * gap), 8), pitch)
                window[g, at, :] = source[0, r, :, start : start + lanes].astype(wide)
        for r in range(rows):
            middle[g, r * pitch : (r + 1) * pitch, :] = lka_mid[
                0, r, :, start : start + lanes
            ].astype(wide)
    for g, (start, which) in enumerate(pair_groups(width)):

        def step(block, carry, g=g, start=start, which=which):
            base = pl.multiple_of(block * 8, 8)

            def add_tap(t, value):
                tap_sums[which, t] += value

            total = window_sums(
                lambda r, s: window[g, pl.ds(base + (16 + r * gap + s), 8), :],
                lambda t: weights[which, t],
                7,
                3,
                rows,
                True,
                [middle[g, pl.ds(base + p * pitch, 8), :] for p in range(rows)],
                add_tap,
            )
            for o in range(rows):
                out[pl.ds(base + o * pitch, 8), start : start + lanes] = total[o]
            return carry

        lax.fori_loop(0, pitch // 8, step, 0, unroll=True)
    for r in range(rows):
        at = r * pitch
        grad_mid[0, r] = (
            out[at : at + pitch, :] * inside(1, pitch, breadth, 2 * width)
        ).astype(low)

    @pl.when(pl.program_id(0) == pl.num_programs(0) - 1)
    def _():
        store_pair_taps(grad_taps, tap_sums, width)
        grad_taps[...] += taps_before[...]


def five_kernel(
    counts,
    images,
    grad_mid,
    far,
    near,
    gelu_low,
    pre_gelu,
    grad_direct,
    grad_first,
    params,
    stats,
    proj_in,
    taps,
    lka_sum,
    out_sum,
    seven_sum,
    three_sum,
    scale_one,
    scale_two,
    grad_partial,
    packed_kept,
    packed_sent,
    grad_proj_in,
    grad_taps,
    sums,
    pack,
    window,
    middle,
    out,
    weights,
    tap_sums,
    values,
    mask,
    *,
    rows,
    breadth,
    pitch,
):
    width = images.shape[3]
    alive = alive_lanes(counts, 0, width)
    pixels = pixels_of(counts, rows * breadth)
    mean, rstd = norm_of(stats, pixels)
    mean, rstd = paired(mean), paired(rstd)
    gain, shift, scale = (paired(params[k : k + 1, :]) for k in range(3))

    @pl.when(pl.program_id(0) == 0)
    def _():
        window[...] = jnp.zeros_like(window)
        tap_sums[...] = jnp.zeros_like(tap_sums)
        values[...] = jnp.zeros_like(values)
        sums[...] = jnp.zeros_like(sums)
        grad_proj_in[...] = jnp.zeros_like(grad_proj_in)
        mask[...] = inside(rows, pitch, breadth, 2 * width)
        fill_pair_weights(weights, taps, width)

    for g, (start, _) in enumerate(pair_groups(width)):
        for source, offset in zip((far, near), sides((rows + 2) * pitch)):
            for r in range(2):
                at = pl.ds(pl.multiple_of(offset + (8 + r * pitch), 8), pitch)
                window[g, at, :] = source[0, r, :, start : start + lanes].astype(wide)
        for r in range(rows):
            at = 8 + (r + 2) * pitch
            window[g, at : at + pitch, :] = grad_mid[0, r, :, start : start + lanes].astype(wide)
        middle[g] = gelu_low[0, :, start : start + lanes].astype(wide)
    for g, (start, which) in enumerate(pair_groups(width)):

        def step(block, carry, g=g, start=start, which=which):
            base = pl.multiple_of(block * 8, 8)

            def add_tap(t, value):
                tap_sums[which, t] += value

            total = window_sums(
                lambda r, s: window[g, pl.ds(base + (8 + r * pitch + s), 8), :],
                lambda t: weights[which, t],
                5,
                1,
                rows,
                True,
                [middle[g, pl.ds(base + p * pitch, 8), :] for p in range(rows)],
                add_tap,
            )
            for o in range(rows):
                out[pl.ds(base + o * pitch, 8), start : start + lanes] = total[o]
            return carry

        lax.fori_loop(0, pitch // 8, step, 0, unroll=True)
    for r in range(rows):
        values[r * pitch : r * pitch + breadth, :] = pair_lanes(
            images[0, r].astype(wide), images[1, r].astype(wide)
        )
    pre = pre_gelu[0].astype(wide)
    cdf, density = normal_parts(pre)
    grad_pre = ((grad_direct[0].astype(wide) + out[...]) * (cdf + pre * density)).astype(low)
    xhat = (values[...] - mean) * rstd
    normed = (xhat * gain + shift) * mask[...]
    grad_proj_in[...] += folded_square(
        jnp.dot(normed.T.astype(low), grad_pre, preferred_element_type=wide)
    )
    back = lax.dot_general(
        grad_pre, proj_in[...], (((1,), (1,)), ((), ())), preferred_element_type=wide
    )
    first = grad_first[0]
    grad_normed = (first * scale + back) * mask[...]
    sums[0:1, :] += folded(jnp.sum(grad_normed, axis=0, keepdims=True))
    sums[1:2, :] += folded(jnp.sum(grad_normed * xhat, axis=0, keepdims=True))
    grad_partial[0], grad_partial[1] = split_lanes(first + alive * rstd * gain * grad_normed)

    @pl.when(pl.program_id(0) == pl.num_programs(0) - 1)
    def _():
        store_pair_taps(grad_taps, tap_sums, width)
        pack[...] = jnp.zeros_like(pack)
        at = 0
        for part in (grad_proj_in, lka_sum, out_sum, grad_taps, seven_sum):
            pack[at : at + part.shape[0], :] = part[...]
            at += -(-part.shape[0] // 8) * 8
        for k in range(three_sum.shape[1] // width):
            pack[at : at + 9, :] = three_sum[:, k * width : (k + 1) * width]
            at += 9
        at = pack.shape[0] - 8
        pack[at : at + 2, :] = sums[...]
        pack[at + 2 : at + 3, :] = scale_one[...]
        pack[at + 3 : at + 4, :] = scale_two[...]
        half = (pack.shape[0] - 8) // 2
        for target, offset in zip((packed_kept, packed_sent), sides(half)):
            target[0:half, :] = pack[pl.ds(pl.multiple_of(offset, 8), half), :].astype(low)
            target[half:, :] = pack[at:, :].astype(low)


def pack_rows(width, deep):
    return -(-(3 * width + 32 + 56 + 9 * (deep // width)) // 64) * 64


def spread_kernel(packed, grad_in, grad_lka, grad_out, grad_five, grad_seven, grad_three):
    width = packed.shape[1]
    at = 0
    for part in (grad_in, grad_lka, grad_out, grad_five, grad_seven):
        size = -(-part.shape[0] // 8) * 8
        part[...] = packed[at : at + size, :].astype(wide)[: part.shape[0]]
        at += size
    rest = packed[at:, :].astype(wide)
    for k in range(grad_three.shape[1] // width):
        grad_three[:, k * width : (k + 1) * width] = rest[9 * k : 9 * k + 9]


def last_kernel(
    counts, images, grad_partial, params, stats, grad_stats, grad_images, *, rows, breadth, pitch
):
    alive = (pl.program_id(0) < live_here(counts)).astype(wide)
    pixels = pixels_of(counts, rows * breadth)
    mean, rstd = norm_of(stats, pixels)
    factor = alive * rstd * params[0:1, :] / pixels
    grad_sums = grad_stats[...].astype(wide)
    shift_sum, gain_sum = grad_sums[0:1, :], grad_sums[1:2, :]
    for r in range(rows):
        xhat = (images[0, r].astype(wide) - mean) * rstd
        part = grad_partial[0, r * pitch : r * pitch + breadth, :]
        grad_images[0, r] = part - factor * (shift_sum + xhat * gain_sum)


def mlp_kernel(
    counts,
    first_sum,
    far,
    near,
    cot,
    cot_far,
    cot_near,
    params,
    stats,
    fc_in,
    fc_out,
    taps,
    out_image,
    grad_normed,
    copies,
    scale_sum,
    fc_kept,
    fc_sent,
    grad_taps,
    sums,
    normed_wide,
    mlp_wide,
    normed_low,
    normed_turned,
    grads_low,
    grads_turned,
    hidden_even,
    hidden_odd,
    active_even,
    active_odd,
    grad_mixed,
    low_even,
    low_odd,
    back_even,
    back_odd,
    mlp_sum,
    normed_sum,
    weights,
    tap_sums,
    in_sum,
    out_sum,
    *,
    rows,
    breadth,
    pitch,
):
    image = pl.program_id(0)
    alive = (image < live_here(counts)).astype(jnp.float32)
    groups = fc_in.shape[1] // (2 * lanes)
    blocks = pitch // 8
    pixels = pixels_of(counts, rows * breadth)
    mean_two, rstd_two = norm_of(stats, pixels)
    gain_two, shift_two, scale_two = params[3:4, :], params[4:5, :], params[5:6, :]

    @pl.when(image == 0)
    def _():
        normed_wide[...] = jnp.zeros_like(normed_wide)
        mlp_wide[...] = jnp.zeros_like(mlp_wide)
        hidden_even[...] = jnp.zeros_like(hidden_even)
        hidden_odd[...] = jnp.zeros_like(hidden_odd)
        grad_mixed[...] = jnp.zeros_like(grad_mixed)
        tap_sums[...] = jnp.zeros_like(tap_sums)
        in_sum[...] = jnp.zeros_like(in_sum)
        out_sum[...] = jnp.zeros_like(out_sum)
        sums[...] = jnp.zeros_like(sums)
        scale_sum[...] = jnp.zeros_like(scale_sum)
        fill_weights(weights, taps, taps.shape[1])

    def normalized(value):
        return (value - mean_two) * rstd_two * gain_two + shift_two

    for source, offset, there in zip((far, near), sides((rows + 2) * pitch), present()):
        for r in range(2):
            at = pl.ds(pl.multiple_of(offset + r * pitch, 8), breadth)
            normed_wide[at, :] = there * normalized(source[0, r, 0:breadth, :])
    for r in range(rows):
        at = (r + 2) * pitch
        normed_wide[at : at + breadth, :] = normalized(first_sum[0, r, 0:breadth, :])
        at = (r + 1) * pitch
        mlp_wide[at : at + breadth, :] = cot[0, r].astype(jnp.float32) * alive * scale_two
    for source, offset in zip((cot_far, cot_near), sides((rows + 1) * pitch)):
        at = pl.ds(pl.multiple_of(offset, 8), breadth)
        mlp_wide[at, :] = source[0, 0].astype(wide) * alive * scale_two
    normed_low[...] = normed_wide[...].astype(jnp.bfloat16)
    grads_low[...] = mlp_wide[...].astype(jnp.bfloat16)
    inner = normed_wide[2 * pitch : (rows + 2) * pitch, :]
    normed_turned[...] = inner.T.astype(jnp.bfloat16)
    grads_turned[...] = mlp_wide[pitch : (rows + 1) * pitch, :].T.astype(jnp.bfloat16)
    mlp_sum[...] = jnp.zeros_like(mlp_sum)
    normed_sum[...] = jnp.zeros_like(normed_sum)

    hiddens, sources = (hidden_even, hidden_odd), (active_even, active_odd)
    actives, backs = (low_even, low_odd), (back_even, back_odd)

    def columns(group):
        return slice(group * 2 * lanes, (group + 1) * 2 * lanes)

    def enter(group):
        hid = jnp.dot(normed_low[...], fc_in[:, columns(group)], preferred_element_type=wide)
        hid = hid.astype(low).astype(wide)
        act = jnp.dot(grads_low[...], fc_out[:, columns(group)], preferred_element_type=wide)
        for half in range(2):
            lane = slice(half * lanes, (half + 1) * lanes)
            hiddens[group % 2][half, 8 : 8 + (rows + 4) * pitch, :] = hid[:, lane]
            sources[group % 2][half] = act[:, lane]

    def forward(group, half, block):
        hidden, source, active = (refs[group % 2] for refs in (hiddens, sources, actives))
        lane = slice(half * lanes, (half + 1) * lanes)
        place, base = group * 2 + half, block * 8
        mixed = window_sums(
            lambda r, s: hidden[half, pl.ds(base + (8 + r * pitch + s), 8), :],
            lambda t: weights[place, t],
            3,
            1,
            rows + 2,
            False,
        )
        for o in range(rows + 2):
            x = mixed[o]
            cdf, density = normal_parts(x)
            slope = cdf + x * density
            grad_mixed[half, pl.ds(base + (8 + o * pitch), 8), :] = (
                source[half, pl.ds(base + o * pitch, 8), :] * slope
            )
            if 1 <= o <= rows:
                active[pl.ds(base + (o - 1) * pitch, 8), lane] = x * cdf

    def backward(group, half, block):
        hidden, back = hiddens[group % 2], backs[group % 2]
        lane = slice(half * lanes, (half + 1) * lanes)
        place, base = group * 2 + half, block * 8

        def add_tap(t, value):
            tap_sums[place, t] += value

        total = window_sums(
            lambda r, s: grad_mixed[half, pl.ds(base + (8 + r * pitch + s), 8), :],
            lambda t: weights[place, t],
            3,
            1,
            rows,
            True,
            [hidden[half, pl.ds(base + (8 + (p + 2) * pitch), 8), :] for p in range(rows)],
            add_tap,
        )
        for p in range(rows):
            back[pl.ds(base + p * pitch, 8), lane] = total[p]

    def leave(group):
        act_low = actives[group % 2][...].astype(low)
        hid_low = backs[group % 2][...].astype(low)
        mlp_sum[...] += lax.dot_general(
            act_low,
            fc_out[:, columns(group)],
            (((1,), (1,)), ((), ())),
            preferred_element_type=wide,
        )
        normed_sum[...] += lax.dot_general(
            hid_low,
            fc_in[:, columns(group)],
            (((1,), (1,)), ((), ())),
            preferred_element_type=wide,
        )
        part_in = jnp.dot(normed_turned[...], hid_low, preferred_element_type=wide)
        part_out = jnp.dot(grads_turned[...], act_low, preferred_element_type=wide)
        for half in range(2):
            lane = slice(half * lanes, (half + 1) * lanes)
            in_sum[group * 2 + half] += part_in[:, lane]
            out_sum[group * 2 + half] += part_out[:, lane]

    enter(0)
    for group in range(groups):
        if group + 1 < groups:
            enter(group + 1)
        if group > 0:
            leave(group - 1)
        for half in range(2):
            for block in range(blocks):
                forward(group, half, block)
        for half in range(2):
            for block in range(blocks):
                backward(group, half, block)
    leave(groups - 1)

    scale_grad = jnp.zeros_like(scale_two)
    shift_grad = jnp.zeros_like(scale_two)
    gain_grad = jnp.zeros_like(scale_two)
    for r in range(rows):
        mlp = mlp_sum[r * pitch : r * pitch + breadth, :]
        back = normed_sum[r * pitch : r * pitch + breadth, :]
        first = first_sum[0, r, 0:breadth, :]
        out_image[0, r] = (alive * (first + scale_two * mlp)).astype(jnp.bfloat16)
        grad_normed[0, r * pitch : r * pitch + breadth, :] = back
        grad_normed[0, r * pitch + breadth : (r + 1) * pitch, :] = jnp.zeros(
            (pitch - breadth, back.shape[1]), wide
        )
        grad = cot[0, r].astype(jnp.float32) * alive
        scale_grad += jnp.sum(grad * mlp, axis=0, keepdims=True)
        shift_grad += jnp.sum(back, axis=0, keepdims=True)
        gain_grad += jnp.sum(back * (first - mean_two) * rstd_two, axis=0, keepdims=True)
    sums[0:1, :] += shift_grad
    sums[1:2, :] += gain_grad
    scale_sum[...] += scale_grad

    @pl.when(image == pl.num_programs(0) - 1)
    def _():
        copies[...] = jnp.broadcast_to(sums[...][None], copies.shape)
        odd = lax.axis_index("strip") % 2

        @pl.when(odd == 0)
        def _():
            fc_kept[...] = in_sum[...].astype(low)
            fc_sent[...] = out_sum[...].astype(low)

        @pl.when(odd == 1)
        def _():
            fc_kept[...] = out_sum[...].astype(low)
            fc_sent[...] = in_sum[...].astype(low)

        store_taps(grad_taps, tap_sums, taps.shape[1])


def unpack_kernel(own, other, grad_in, grad_out):
    def spread(source, target):
        for g in range(source.shape[0]):
            target[:, g * lanes : (g + 1) * lanes] = source[g].astype(wide)

    odd = lax.axis_index("strip") % 2

    @pl.when(odd == 0)
    def _():
        spread(own, grad_in)
        spread(other, grad_out)

    @pl.when(odd == 1)
    def _():
        spread(other, grad_in)
        spread(own, grad_out)


def mlp_block(
    counts, first_sum, far, near, cot, cot_far, cot_near, params, stats, fc_in, fc_out, taps
):
    images, rows, breadth, width = cot.shape
    pitch = first_sum.shape[2]
    deep = fc_in.shape[1]
    groups = deep // lanes
    return call(
        mlp_kernel,
        images,
        [
            (counts, smem),
            (first_sum, spec_image(rows, pitch, width)),
            (far, spec_image(2, pitch, width)),
            (near, spec_image(2, pitch, width)),
            (cot, spec_image(rows, breadth, width)),
            (cot_far, spec_image(1, breadth, width)),
            (cot_near, spec_image(1, breadth, width)),
            (params, spec_whole(8, width)),
            (stats, spec_whole(*stats.shape)),
            (fc_in, spec_whole(width, deep)),
            (fc_out.T, spec_whole(width, deep)),
            (taps, spec_whole(9, deep)),
        ],
        [
            (cot.shape, low, spec_image(rows, breadth, width)),
            ((images, rows * pitch, width), wide, spec_image(rows * pitch, width)),
            (stats.shape, wide, spec_whole(*stats.shape)),
            ((1, width), wide, spec_whole(1, width)),
            ((groups, width, lanes), low, spec_whole(groups, width, lanes)),
            ((groups, width, lanes), low, spec_whole(groups, width, lanes)),
            ((9, deep), wide, spec_whole(9, deep)),
        ],
        [
            ((2, width), wide),
            (((rows + 4) * pitch, width), wide),
            (((rows + 2) * pitch, width), wide),
            (((rows + 4) * pitch, width), low),
            ((width, rows * pitch), low),
            (((rows + 2) * pitch, width), low),
            ((width, rows * pitch), low),
            ((2, (rows + 4) * pitch + 16, lanes), wide),
            ((2, (rows + 4) * pitch + 16, lanes), wide),
            ((2, (rows + 2) * pitch, lanes), wide),
            ((2, (rows + 2) * pitch, lanes), wide),
            ((2, (rows + 2) * pitch + 16, lanes), wide),
            ((rows * pitch, 2 * lanes), wide),
            ((rows * pitch, 2 * lanes), wide),
            ((rows * pitch, 2 * lanes), wide),
            ((rows * pitch, 2 * lanes), wide),
            ((rows * pitch, width), wide),
            ((rows * pitch, width), wide),
            ((groups, 9, 8, lanes), wide),
            ((groups, 9, 8, lanes), wide),
            ((groups, width, lanes), wide),
            ((groups, width, lanes), wide),
        ],
        53,
        "mlp",
        vmem=28,
        rows=rows,
        breadth=breadth,
        pitch=pitch,
    )


def body(
    images,
    counts,
    gain_one,
    shift_one,
    proj_in,
    kernel_five,
    kernel_seven,
    lka_proj,
    proj_out,
    scale_one,
    gain_two,
    shift_two,
    fc_in,
    kernel_three,
    fc_out,
    scale_two,
    cotangent,
):
    slots, rows, breadth, width = images.shape
    pitch = -(-(breadth + 2) // 8) * 8
    gap = -(-(breadth + 9) // 8) * 8
    flat = rows * pitch
    blank = jnp.zeros_like(gain_one)
    params = jnp.stack(
        [gain_one, shift_one, scale_one, gain_two, shift_two, scale_two, blank, blank]
    ).astype(wide)
    sizes = dict(rows=rows, breadth=breadth, pitch=pitch)
    vec = spec_whole(8, width)
    devices = device_count()
    blocks = (devices, 2, width)
    two = spec_whole(*blocks)
    square = spec_whole(width, width)
    image_spec = spec_image(rows, breadth, width)
    pairs = slots // 2
    chunks = [(0, pairs - 1), (pairs - 1, 1)]
    pair_width = 2 * width
    pair_square = spec_whole(pair_width, pair_width)
    pair_flat = (pairs, flat, pair_width)
    flat_spec = spec_image(flat, width)
    flat_shape = (slots, flat, width)
    row_shape = (slots, rows, pitch, width)
    groups = len(pair_groups(width))
    kinds = width // lanes + 1
    five_spec = spec_whole(*kernel_five.shape)
    seven_spec = spec_whole(*kernel_seven.shape)

    (first_part,) = call(
        stats_kernel,
        slots,
        [(counts, smem), (images, image_spec)],
        [(blocks, wide, two)],
        [((2, width), wide)],
        2,
        "input_sums",
    )
    pair_in, pair_lka, pair_out = (pair_matrix(m) for m in (proj_in, lka_proj, proj_out))
    first_part, images_after, cot_after = lax.optimization_barrier((first_part, images, cotangent))
    image_far, image_near = far_and_near(
        *(
            jnp.concatenate(parts, axis=1)
            for parts in zip(edge_rows(images_after, 2), edge_rows(cot_after, 1))
        )
    )
    first_stats = from_all(first_part)
    gelu_low = pre_gelu = cot_far = cot_near = None
    cot_shape = (slots, 1, breadth, width)
    mids, rims = [], []
    for start, count in chunks:
        gelu_low, pre_gelu, mid, cot_far, cot_near = call(
            front_kernel,
            count,
            [
                (counts, smem),
                (images, spec_two(start, rows, breadth, width)),
                (image_far, spec_two(start, 3, breadth, width)),
                (image_near, spec_two(start, 3, breadth, width)),
                (params, vec),
                (first_stats, two),
                (pair_in, pair_square),
                (kernel_five, five_spec),
            ],
            [
                (pair_flat, low, spec_from(start, flat, pair_width), gelu_low),
                (pair_flat, low, spec_from(start, flat, pair_width), pre_gelu),
                ((count, rows, pitch, pair_width), low, spec_image(rows, pitch, pair_width)),
                (cot_shape, low, spec_two(start, 1, breadth, width), cot_far),
                (cot_shape, low, spec_two(start, 1, breadth, width), cot_near),
            ],
            [
                (((rows + 4) * pitch, pair_width), wide),
                ((groups, (rows + 4) * pitch + 16, lanes), wide),
                ((kinds, 25, 8, lanes), wide),
                (((rows + 4) * pitch, lanes), wide),
                ((flat, pair_width), wide),
            ],
            4.3 * count,
            f"normed_to_five_{start}",
            vmem=50,
            **sizes,
        )
        mids.append(mid)
        rims.append(far_and_near(mid, mid))
    lka_low = attend = first_sum = None
    second_part = jnp.zeros(blocks, wide)
    for (start, count), mid, (mid_far, mid_near) in zip(chunks, mids, rims):
        rim_spec = spec_image(rows, pitch, pair_width)
        pair_spec = spec_from(start, flat, pair_width)
        lka_low, attend, first_sum, second_part = call(
            attend_kernel,
            count,
            [
                (counts, smem),
                (images, spec_two(start, rows, breadth, width)),
                (mid, rim_spec),
                (mid_far, rim_spec),
                (mid_near, rim_spec),
                (gelu_low, pair_spec),
                (params, vec),
                (first_stats, two),
                (second_part, two),
                (pair_lka, pair_square),
                (pair_out, pair_square),
                (kernel_seven, seven_spec),
            ],
            [
                (pair_flat, low, pair_spec, lka_low),
                (pair_flat, low, pair_spec, attend),
                (flat_shape, wide, spec_two(start, flat, width), first_sum),
                (blocks, wide, two),
            ],
            [
                ((2, width), wide),
                ((groups, 3 * rows * gap + 48, lanes), wide),
                ((kinds, 49, 8, lanes), wide),
                ((flat, pair_width), wide),
                ((flat, pair_width), wide),
                ((flat, pair_width), wide),
            ],
            6.2 * count,
            f"seven_to_first_sum_{start}",
            vmem=20,
            gap=gap,
            start_pair=start,
            **sizes,
        )
    first_rows = first_sum.reshape(row_shape)
    sum_far, sum_near = far_and_near(*edge_rows(first_rows, 2))
    second_stats = from_all(second_part)
    out_image, grad_normed_two, third_part, scale_two_part, fc_kept, fc_sent, grad_kernel_three = mlp_block(
        counts,
        first_rows,
        sum_far,
        sum_near,
        cotangent,
        cot_far,
        cot_near,
        params,
        second_stats,
        fc_in,
        fc_out,
        kernel_three,
    )
    grad_second = from_all(third_part)
    fc_kept, fc_sent, grad_second = lax.optimization_barrier((fc_kept, fc_sent, grad_second))
    got = lax.ppermute(fc_sent, "strip", near_pairs())
    half = (fc_kept.astype(wide) + got.astype(wide)).astype(low)
    sides_of = [[d for d in range(devices) if d % 2 == k] for k in range(2)]
    fc_share = jnp.sum(
        lax.all_to_all(
            half.reshape(devices // 2, -1, lanes),
            ("dp", "strip"),
            0,
            0,
            axis_index_groups=sides_of,
        ).astype(wide),
        axis=0,
    ).astype(low)
    grad_first = grad_direct = None
    gates, rims = [], []
    lka_sum = out_sum = jnp.zeros((width, width), wide)
    scale_sum = jnp.zeros((1, width), wide)
    for start, count in chunks:
        pair_spec = spec_from(start, flat, pair_width)
        grad_first, grad_direct, grad_lka, lka_sum, out_sum, scale_sum = call(
            gate_kernel,
            count,
            [
                (counts, smem),
                (first_sum, spec_two(start, flat, width)),
                (images, spec_two(start, rows, breadth, width)),
                (cotangent, spec_two(start, rows, breadth, width)),
                (grad_normed_two, spec_two(start, flat, width)),
                (lka_low, pair_spec),
                (attend, pair_spec),
                (gelu_low, pair_spec),
                (params, vec),
                (second_stats, two),
                (grad_second, two),
                (pair_lka, pair_square),
                (pair_out, pair_square),
                (lka_sum, square),
                (out_sum, square),
                (scale_sum, spec_whole(1, width)),
            ],
            [
                (pair_flat, wide, pair_spec, grad_first),
                (pair_flat, low, pair_spec, grad_direct),
                ((count, rows, pitch, pair_width), low, spec_image(rows, pitch, pair_width)),
                ((width, width), wide, square),
                ((width, width), wide, square),
                ((1, width), wide, spec_whole(1, width)),
            ],
            [
                ((flat, pair_width), wide),
                ((flat, pair_width), wide),
                ((flat, pair_width), wide),
            ],
            3.2 * count,
            f"gate_backward_{start}",
            vmem=52,
            start_pair=start,
            **sizes,
        )
        gates.append(grad_lka)
        rims.append(far_and_near(grad_lka, grad_lka))
    grad_mid = None
    seven_sum = jnp.zeros(kernel_seven.shape, wide)
    for (start, count), grad_lka, mid, (lka_far, lka_near) in zip(chunks, gates, mids, rims):
        rim_spec = spec_image(rows, pitch, pair_width)
        grad_mid, seven_sum = call(
            seven_kernel,
            count,
            [
                (grad_lka, rim_spec),
                (lka_far, rim_spec),
                (lka_near, rim_spec),
                (mid, rim_spec),
                (kernel_seven, seven_spec),
                (seven_sum, seven_spec),
            ],
            [
                (
                    (pairs, rows, pitch, pair_width),
                    low,
                    spec_from(start, rows, pitch, pair_width),
                    grad_mid,
                ),
                (kernel_seven.shape, wide, seven_spec),
            ],
            [
                ((groups, 3 * rows * gap + 48, lanes), wide),
                ((groups, flat, lanes), wide),
                ((flat, pair_width), wide),
                ((kinds, 49, 8, lanes), wide),
                ((kinds, 49, 8, lanes), wide),
            ],
            7 * count,
            f"seven_backward_{start}",
            vmem=20,
            gap=gap,
            **sizes,
        )
    five_far, five_near = far_and_near(*edge_rows(grad_mid, 2))
    fc_share, five_far, five_near = lax.optimization_barrier((fc_share, five_far, five_near))
    fc_own = lax.all_to_all(
        jnp.broadcast_to(fc_share[None], (devices // 2,) + fc_share.shape),
        ("dp", "strip"),
        0,
        0,
        axis_index_groups=sides_of,
    ).reshape(fc_kept.shape)
    pair_spec = spec_image(flat, pair_width)
    deep = fc_in.shape[1]
    total_rows = pack_rows(width, deep)
    grad_partial, packed_kept, packed_sent = call(
        five_kernel,
        pairs,
        [
            (counts, smem),
            (images, spec_two(0, rows, breadth, width)),
            (grad_mid, spec_image(rows, pitch, pair_width)),
            (five_far, spec_image(2, pitch, pair_width)),
            (five_near, spec_image(2, pitch, pair_width)),
            (gelu_low, pair_spec),
            (pre_gelu, pair_spec),
            (grad_direct, pair_spec),
            (grad_first, pair_spec),
            (params, vec),
            (first_stats, two),
            (pair_in, pair_square),
            (kernel_five, five_spec),
            (lka_sum, square),
            (out_sum, square),
            (seven_sum, seven_spec),
            (grad_kernel_three, spec_whole(*kernel_three.shape)),
            (scale_sum, spec_whole(1, width)),
            (scale_two_part, spec_whole(1, width)),
        ],
        [
            (flat_shape, wide, spec_two(0, flat, width)),
            ((total_rows // 2 + 8, width), low, spec_whole(total_rows // 2 + 8, width)),
            ((total_rows // 2 + 8, width), low, spec_whole(total_rows // 2 + 8, width)),
        ],
        [
            ((width, width), wide),
            (kernel_five.shape, wide),
            ((2, width), wide),
            ((total_rows + 8, width), wide),
            ((groups, (rows + 4) * pitch + 16, lanes), wide),
            ((groups, flat, lanes), wide),
            ((flat, pair_width), wide),
            ((kinds, 25, 8, lanes), wide),
            ((kinds, 25, 8, lanes), wide),
            ((flat, pair_width), wide),
            ((flat, pair_width), wide),
        ],
        6 * pairs,
        "five_backward",
        vmem=52,
        **sizes,
    )
    fc_own, packed_sent = lax.optimization_barrier((fc_own, packed_sent))
    share, vectors = split_sums(packed_kept, packed_sent, 8)
    fc_other = lax.ppermute(fc_own, "strip", near_pairs())
    (grad_images,) = call(
        last_kernel,
        slots,
        [
            (counts, smem),
            (images, image_spec),
            (grad_partial, flat_spec),
            (params, vec),
            (first_stats, two),
            (vectors, spec_whole(8, width)),
        ],
        [(images.shape, wide, image_spec)],
        [],
        4,
        "input_gradient",
        vmem=56,
        **sizes,
    )
    grad_fc_in, grad_fc_out = call(
        unpack_kernel,
        1,
        [(half, spec_whole(*half.shape)) for half in (fc_own, fc_other)],
        [
            ((width, deep), wide, spec_whole(width, deep)),
            ((width, deep), wide, spec_whole(width, deep)),
        ],
        [],
        2,
        "weight_gradients",
    )
    matrices, (grad_images, (grad_fc_in, grad_fc_out)) = joined(
        share, [grad_images, (grad_fc_in, grad_fc_out)]
    )
    pieces = call(
        spread_kernel,
        1,
        [(matrices, spec_whole(total_rows, width))],
        [
            (shape, wide, spec_whole(*shape))
            for shape in [(width, width)] * 3
            + [kernel_five.shape, kernel_seven.shape, kernel_three.shape]
        ],
        [],
        2,
        "attention_gradients",
    )
    vectors = vectors.astype(wide)
    grad_second = jnp.sum(grad_second, axis=0)
    return (
        out_image,
        grad_images,
        vectors[1],
        vectors[0],
        pieces[0],
        pieces[3],
        pieces[4],
        pieces[1],
        pieces[2],
        vectors[2],
        grad_second[1],
        grad_second[0],
        grad_fc_in,
        pieces[5],
        grad_fc_out.T,
        vectors[3],
    )


def solution(mesh):
    split = P("dp", "strip", None, None)
    return jax.shard_map(
        body,
        mesh=mesh,
        in_specs=(split,) + (P(),) * 15 + (split,),
        out_specs=(split, split) + (P(),) * 14,
        check_vma=False,
    )
```

```python
import functools

import jax
import jax.numpy as jnp
from jax import lax
from jax.experimental import pallas as pl
from jax.experimental.pallas import tpu as pltpu
from jax.sharding import PartitionSpec as P

epsilon = 1e-05
lanes = 128
smem = pl.BlockSpec(memory_space=pltpu.SMEM)
wide = jnp.float32
low = jnp.bfloat16


def exchange_steps():
    return [
        (axis, 1 << bit)
        for axis in ("strip", "dp")
        for bit in range(lax.axis_size(axis).bit_length() - 1)
    ]


def swapped(value, axis, bit):
    return lax.ppermute(value, axis, [(i, i ^ bit) for i in range(lax.axis_size(axis))])


def device_count():
    return lax.axis_size("dp") * lax.axis_size("strip")


def from_all(copies):
    return lax.all_to_all(copies, ("dp", "strip"), 0, 0)


def split_sums(part, sent, size):
    for place, (axis, bit) in enumerate(exchange_steps()):
        length = part.shape[0] - size
        if 0 < place < 3:
            upper = (lax.axis_index(axis) // bit) % 2
            tail = part[length:]
            halves = part[:length].reshape((2, length // 2) + part.shape[1:])
            sent = lax.dynamic_index_in_dim(halves, 1 - upper, 0, False)
            kept = lax.dynamic_index_in_dim(halves, upper, 0, False)
            sent, part = jnp.concatenate([sent, tail]), jnp.concatenate([kept, tail])
        elif place > 0:
            sent = part
        got = swapped(sent, axis, bit)
        part = (part.astype(wide) + got.astype(wide)).astype(low)
    return part[: part.shape[0] - size], part[part.shape[0] - size :]


def joined(part, beside):
    for place, (axis, bit) in enumerate(reversed(exchange_steps()[:3])):
        if place > 0:
            part, beside[place - 1] = lax.optimization_barrier((part, beside[place - 1]))
        upper = (lax.axis_index(axis) // bit) % 2
        got = swapped(part, axis, bit)
        part = jnp.where(
            upper == 0, jnp.concatenate([part, got]), jnp.concatenate([got, part])
        )
    return part, beside


def near_pairs():
    return [(i, i ^ 1) for i in range(lax.axis_size("strip"))]


def far_and_near(far, near):
    count = lax.axis_size("strip")
    pairs = [(i, i + 1) for i in range(1, count - 1, 2)]
    return (
        lax.ppermute(far, "strip", pairs + [(j, i) for i, j in pairs]),
        lax.ppermute(near, "strip", near_pairs()),
    )


def edge_rows(value, width):
    odd = lax.axis_index("strip") % 2
    length = value.shape[1] - width
    return (
        lax.dynamic_slice_in_dim(value, odd * length, width, 1),
        lax.dynamic_slice_in_dim(value, (1 - odd) * length, width, 1),
    )


def sides(length):
    odd = lax.axis_index("strip") % 2
    return odd * length, (1 - odd) * length


def present():
    strip, count = lax.axis_index("strip"), lax.axis_size("strip")
    above, below = (strip > 0).astype(wide), (strip < count - 1).astype(wide)
    odd = (strip % 2).astype(wide)
    return odd * below + (1 - odd) * above, odd * above + (1 - odd) * below


def normal_parts(x):
    density = jnp.exp2(x * x * -0.7213475204444817 - 1.3257480647361595)
    scale = 1.0 + 0.2316419 * jnp.abs(x)
    guess = pl.reciprocal(scale, approx=True)
    t = guess * (2.0 - scale * guess)
    poly = 1.781477937 + t * (-1.821255978 + t * 1.330274429)
    poly = t * (0.319381530 + t * (-0.356563782 + t * poly))
    tail = density * poly
    return jnp.where(x > 0, 1.0 - tail, tail), density


def window_sums(load, weight, across, spread, rows, back, center=None, add_tap=None):
    total = [None] * rows
    reach = spread * (across - 1)
    for j in range(across):
        shift = (j - across // 2) * spread * (-1 if back else 1)
        w = [weight(i * across + j) for i in range(across)]
        tap = [None] * across
        for r in range(rows + reach):
            v = load(r, shift)
            for i in range(across):
                o = r - reach + spread * i if back else r - spread * i
                if 0 <= o < rows:
                    term = v * w[i]
                    total[o] = term if total[o] is None else total[o] + term
                    if center is not None:
                        term = v * center[o]
                        tap[i] = term if tap[i] is None else tap[i] + term
        if center is not None:
            for i in range(across):
                add_tap(i * across + j, tap[i])
    return total


def lane_groups(width):
    return [(start, min(lanes, width - start)) for start in range(0, width, lanes)]


def fill_weights(weights, taps, width):
    weights[...] = jnp.zeros_like(weights)
    for g, (start, size) in enumerate(lane_groups(width)):
        for t in range(taps.shape[0]):
            weights[g, t, :, 0:size] = jnp.broadcast_to(
                taps[t : t + 1, start : start + size].astype(wide), (8, size)
            )


def store_taps(grad_taps, tap_sums, width):
    for g, (start, size) in enumerate(lane_groups(width)):
        for t in range(grad_taps.shape[0]):
            grad_taps[t : t + 1, start : start + size] = jnp.sum(
                tap_sums[g, t, :, 0:size], axis=0, keepdims=True
            )


def inside(rows, pitch, breadth, width):
    place = lax.broadcasted_iota(jnp.int32, (rows, pitch, width), 1)
    return jnp.where(place < breadth, 1.0, 0.0).reshape(rows * pitch, width)


def live_here(counts):
    return counts[lax.axis_index("dp")]


def pixels_of(counts, area):
    total = counts[0]
    for k in range(1, counts.shape[0]):
        total += counts[k]
    return total.astype(wide) * (area * lax.axis_size("strip"))


def norm_of(blocks, pixels):
    stats = jnp.sum(blocks[...], axis=0) / pixels
    mean = stats[0:1, :]
    return mean, lax.rsqrt(stats[1:2, :] - mean * mean + epsilon)


def spec_image(*shape):
    return pl.BlockSpec((1,) + shape, lambda i: (i,) + (0,) * len(shape))


def spec_from(start, *shape):
    return pl.BlockSpec((1,) + shape, lambda i: (i + start,) + (0,) * len(shape))


def spec_two(start, *shape):
    return pl.BlockSpec((2,) + shape, lambda i: (i + start,) + (0,) * len(shape))


def spec_whole(*shape):
    return pl.BlockSpec(shape, lambda i: (0,) * len(shape))


def call(kernel, steps, ins, outs, scratch, cost, name, vmem=44, **sizes):
    earlier = [out[3] for out in outs if len(out) > 3 and out[3] is not None]
    aliases, at = {}, len(ins)
    for place, out in enumerate(outs):
        if len(out) > 3 and out[3] is not None:
            aliases[at] = place
            at += 1

    def run(*refs):
        kernel(*refs[: len(ins)], *refs[at:], **sizes)

    return pl.pallas_call(
        run,
        grid=(steps,),
        in_specs=[spec for _, spec in ins] + [pl.BlockSpec(memory_space=pl.ANY)] * len(earlier),
        out_specs=[out[2] for out in outs],
        out_shape=[jax.ShapeDtypeStruct(out[0], out[1]) for out in outs],
        scratch_shapes=[pltpu.VMEM(shape, dtype) for shape, dtype in scratch],
        input_output_aliases=aliases,
        compiler_params=pltpu.CompilerParams(vmem_limit_bytes=vmem * 1024 * 1024),
        cost_estimate=pl.CostEstimate(
            flops=0, bytes_accessed=int(cost * 3.5e6), transcendentals=0
        ),
        name=name,
    )(*[array for array, _ in ins], *earlier)


def paired(value):
    return pair_lanes(value, value)


def pair_lanes(left, right):
    main = left.shape[-1] // lanes * lanes
    tails = jnp.concatenate([left[..., main:], right[..., main:]], axis=-1)
    return jnp.concatenate([left[..., :main], right[..., :main], tails], axis=-1)


def split_lanes(value):
    width = value.shape[-1] // 2
    main = width // lanes * lanes
    left = jnp.concatenate([value[..., :main], value[..., 2 * main : main + width]], axis=-1)
    right = jnp.concatenate([value[..., main : 2 * main], value[..., main + width :]], axis=-1)
    return left, right


def folded(value):
    left, right = split_lanes(value)
    return left + right


def folded_square(value):
    width = value.shape[0] // 2
    main = width // lanes * lanes
    left = split_lanes(jnp.concatenate([value[:main], value[2 * main : main + width]], axis=0))[0]
    right = split_lanes(jnp.concatenate([value[main : 2 * main], value[main + width :]], axis=0))[1]
    return left + right


def pair_matrix(matrix):
    blank = jnp.zeros_like(matrix)
    left = jnp.concatenate([matrix, blank], axis=1)
    right = jnp.concatenate([blank, matrix], axis=1)
    width = matrix.shape[0]
    main = width // lanes * lanes

    def columns(value):
        return jnp.concatenate(
            [
                value[:, :main],
                value[:, width : width + main],
                value[:, main:width],
                value[:, width + main :],
            ],
            axis=1,
        )

    left, right = columns(left), columns(right)
    return jnp.concatenate([left[:main], right[:main], left[main:], right[main:]])


def pair_groups(width):
    main = width // lanes
    return [(g * lanes, g % main) for g in range(2 * main)] + [(2 * main * lanes, main)]


def fill_pair_weights(weights, taps, width):
    main = width // lanes * lanes
    for t in range(taps.shape[0]):
        row = taps[t : t + 1, :].astype(wide)
        tail = row[:, main:]
        for g in range(main // lanes):
            weights[g, t] = jnp.broadcast_to(row[:, g * lanes : (g + 1) * lanes], (8, lanes))
        weights[main // lanes, t] = jnp.broadcast_to(
            jnp.concatenate([tail, tail], axis=1), (8, lanes)
        )


def store_pair_taps(grad_taps, tap_sums, width):
    main = width // lanes * lanes
    for t in range(grad_taps.shape[0]):
        for g in range(main // lanes):
            grad_taps[t : t + 1, g * lanes : (g + 1) * lanes] = jnp.sum(
                tap_sums[g, t], axis=0, keepdims=True
            )
        tail = jnp.sum(tap_sums[main // lanes, t], axis=0, keepdims=True)
        grad_taps[t : t + 1, main:width] = tail[:, : width - main] + tail[:, width - main :]


def alive_lanes(counts, start, width):
    main = width // lanes * lanes
    image = 2 * (pl.program_id(0) + start)
    at = lax.broadcasted_iota(jnp.int32, (1, 2 * width), 1)
    second = ((at >= main) & (at < 2 * main)) | (at >= main + width)
    return jnp.where(image + second.astype(jnp.int32) < live_here(counts), 1.0, 0.0)


def stats_kernel(counts, images, copies, sums):
    image = pl.program_id(0)

    @pl.when(image == 0)
    def _():
        sums[...] = jnp.zeros_like(sums)

    alive = (image < live_here(counts)).astype(wide)
    total = jnp.zeros((images.shape[2], images.shape[3]), wide)
    square = total
    for r in range(images.shape[1]):
        value = images[0, r].astype(wide)
        total += value
        square += value * value
    sums[0:1, :] += jnp.sum(total, axis=0, keepdims=True) * alive
    sums[1:2, :] += jnp.sum(square, axis=0, keepdims=True) * alive

    @pl.when(image == pl.num_programs(0) - 1)
    def _():
        copies[...] = jnp.broadcast_to(sums[...][None], copies.shape)


def front_kernel(
    counts,
    images,
    far,
    near,
    params,
    stats,
    proj_in,
    taps,
    gelu_low,
    pre_gelu,
    lka_mid,
    cot_far,
    cot_near,
    values,
    gelu,
    weights,
    mask,
    mid,
    *,
    rows,
    breadth,
    pitch,
):
    width = images.shape[3]
    pixels = pixels_of(counts, rows * breadth)
    mean, rstd = norm_of(stats, pixels)
    mean, rstd = paired(mean), paired(rstd)
    gain, shift = paired(params[0:1, :]), paired(params[1:2, :])

    @pl.when(pl.program_id(0) == 0)
    def _():
        values[...] = jnp.zeros_like(values)
        gelu[...] = jnp.zeros_like(gelu)
        fill_pair_weights(weights, taps, width)
        mask[...] = inside(rows + 4, pitch, breadth, lanes)
        for offset, there in zip(sides((rows + 2) * pitch), present()):
            at = pl.ds(pl.multiple_of(offset, 8), 2 * pitch)
            mask[at, :] = mask[at, :] * there

    def place(at, source, r):
        value = pair_lanes(source[0, r].astype(wide), source[1, r].astype(wide))
        values[pl.ds(at, breadth), :] = (value - mean) * rstd * gain + shift

    for k in range(2):
        cot_far[k, 0] = far[k, 2]
        cot_near[k, 0] = near[k, 2]
    for source, offset in zip((far, near), sides((rows + 2) * pitch)):
        for r in range(2):
            place(pl.multiple_of(offset + r * pitch, 8), source, r)
    for r in range(rows):
        place((r + 2) * pitch, images, r)
    pre = jnp.dot(values[...].astype(low), proj_in[...], preferred_element_type=wide)
    pre_gelu[0] = pre[2 * pitch : (rows + 2) * pitch, :].astype(low)
    for g, (start, _) in enumerate(pair_groups(width)):
        part = pre[:, start : start + lanes]
        cdf, _ = normal_parts(part)
        rounded = (part * cdf * mask[...]).astype(low).astype(wide)
        gelu_low[0, :, start : start + lanes] = rounded[2 * pitch : (rows + 2) * pitch].astype(low)
        gelu[g, 8 : 8 + (rows + 4) * pitch, :] = rounded
    for g, (start, which) in enumerate(pair_groups(width)):

        def step(block, carry, g=g, start=start, which=which):
            base = pl.multiple_of(block * 8, 8)
            total = window_sums(
                lambda r, s: gelu[g, pl.ds(base + (8 + r * pitch + s), 8), :],
                lambda t: weights[which, t],
                5,
                1,
                rows,
                False,
            )
            for o in range(rows):
                mid[pl.ds(base + o * pitch, 8), start : start + lanes] = total[o]
            return carry

        lax.fori_loop(0, pitch // 8, step, 0)
    for r in range(rows):
        at = r * pitch
        lka_mid[0, r] = (
            mid[at : at + pitch, :] * inside(1, pitch, breadth, 2 * width)
        ).astype(low)


def attend_kernel(
    counts,
    images,
    lka_mid,
    far,
    near,
    gelu_low,
    params,
    stats,
    earlier_sums,
    lka_proj,
    proj_out,
    taps,
    lka_low,
    attend_out,
    first_sum,
    copies,
    sums,
    window,
    weights,
    lka,
    values,
    mask,
    *,
    rows,
    breadth,
    pitch,
    gap,
    start_pair,
):
    width = images.shape[3]
    alive = alive_lanes(counts, start_pair, width)
    pixels = pixels_of(counts, rows * breadth)
    mean, rstd = norm_of(stats, pixels)
    mean, rstd = paired(mean), paired(rstd)
    gain, shift, scale = (paired(params[k : k + 1, :]) for k in range(3))

    @pl.when(pl.program_id(0) == 0)
    def _():
        window[...] = jnp.zeros_like(window)
        values[...] = jnp.zeros_like(values)
        sums[...] = earlier_sums[0]
        fill_pair_weights(weights, taps, width)
        mask[...] = inside(rows, pitch, breadth, 2 * width)

    far_at, near_at = sides(2 * rows * gap)
    for offset, source in ((far_at, far), (rows * gap, lka_mid), (near_at, near)):
        for r in range(rows):
            at = pl.ds(pl.multiple_of(offset + (16 + r * gap), 8), pitch)
            for g, (start, _) in enumerate(pair_groups(width)):
                window[g, at, :] = source[0, r, :, start : start + lanes].astype(wide)
    for g, (start, which) in enumerate(pair_groups(width)):

        def step(block, carry, g=g, start=start, which=which):
            base = pl.multiple_of(block * 8, 8)
            total = window_sums(
                lambda r, s: window[g, pl.ds(base + (16 + r * gap + s), 8), :],
                lambda t: weights[which, t],
                7,
                3,
                rows,
                False,
            )
            for o in range(rows):
                lka[pl.ds(base + o * pitch, 8), start : start + lanes] = total[o]
            return carry

        lax.fori_loop(0, pitch // 8, step, 0)
    for r in range(rows):
        values[r * pitch : r * pitch + breadth, :] = pair_lanes(
            images[0, r].astype(wide), images[1, r].astype(wide)
        )
    low_lka = lka[...].astype(low)
    lka_low[0] = low_lka
    attend = jnp.dot(low_lka, lka_proj[...], preferred_element_type=wide)
    attend_out[0] = attend.astype(low)
    gated = (gelu_low[0].astype(wide) * attend).astype(low)
    branch = jnp.dot(gated, proj_out[...], preferred_element_type=wide)
    attn = (branch + ((values[...] - mean) * rstd * gain + shift)) * mask[...]
    first = values[...] + scale * attn
    first_sum[0], first_sum[1] = split_lanes(first)
    sums[0:1, :] += folded(jnp.sum(first, axis=0, keepdims=True) * alive)
    sums[1:2, :] += folded(jnp.sum(first * first, axis=0, keepdims=True) * alive)

    @pl.when(pl.program_id(0) == pl.num_programs(0) - 1)
    def _():
        copies[...] = jnp.broadcast_to(sums[...][None], copies.shape)


def gate_kernel(
    counts,
    first_sum,
    images,
    cot,
    grad_normed,
    lka_low,
    attend,
    gelu_low,
    params,
    stats,
    grad_stats,
    lka_proj,
    proj_out,
    lka_before,
    out_before,
    scale_before,
    grad_first,
    grad_direct,
    grad_lka,
    grad_lka_proj,
    grad_proj_out,
    sums,
    values,
    pixels_in,
    mask,
    *,
    rows,
    breadth,
    pitch,
    start_pair,
):
    width = cot.shape[3]
    alive = alive_lanes(counts, start_pair, width)
    pixels = pixels_of(counts, rows * breadth)
    mean, rstd = norm_of(stats, pixels)
    mean, rstd = paired(mean), paired(rstd)
    scale, gain = paired(params[2:3, :]), paired(params[3:4, :])
    grad_sums = jnp.sum(grad_stats[...], axis=0)
    shift_sum, gain_sum = paired(grad_sums[0:1, :]), paired(grad_sums[1:2, :])

    @pl.when(pl.program_id(0) == 0)
    def _():
        values[...] = jnp.zeros_like(values)
        pixels_in[...] = jnp.zeros_like(pixels_in)
        mask[...] = inside(rows, pitch, breadth, 2 * width)
        sums[...] = scale_before[...]
        grad_lka_proj[...] = lka_before[...]
        grad_proj_out[...] = out_before[...]

    for r in range(rows):
        values[r * pitch : r * pitch + breadth, :] = pair_lanes(
            cot[0, r].astype(wide), cot[1, r].astype(wide)
        )
        pixels_in[r * pitch : r * pitch + breadth, :] = pair_lanes(
            images[0, r].astype(wide), images[1, r].astype(wide)
        )
    summed = pair_lanes(first_sum[0], first_sum[1])
    yhat = (summed - mean) * rstd
    inner = pair_lanes(grad_normed[0], grad_normed[1]) - (shift_sum + yhat * gain_sum) / pixels
    first = alive * (values[...] + rstd * gain * inner) * mask[...]
    grad_first[0] = first
    sums[...] += folded(
        jnp.sum(first * (summed - pixels_in[...]), axis=0, keepdims=True) / scale
    )
    branch = (first * scale).astype(low)
    gated_back = lax.dot_general(
        branch, proj_out[...], (((1,), (1,)), ((), ())), preferred_element_type=wide
    )
    gelu = gelu_low[0].astype(wide)
    attended = attend[0].astype(wide)
    gated = gelu * attended
    grad_proj_out[...] += folded_square(
        jnp.dot(gated.T.astype(low), branch, preferred_element_type=wide)
    )
    grad_direct[0] = (gated_back * attended).astype(low)
    back = (gated_back * gelu).astype(low)
    lka = lax.dot_general(
        back, lka_proj[...], (((1,), (1,)), ((), ())), preferred_element_type=wide
    )
    grad_lka_proj[...] += folded_square(
        jnp.dot(lka_low[0].astype(wide).T.astype(low), back, preferred_element_type=wide)
    )
    for r in range(rows):
        grad_lka[0, r] = lka[r * pitch : (r + 1) * pitch, :].astype(low)


def seven_kernel(
    grad_lka,
    far,
    near,
    lka_mid,
    taps,
    taps_before,
    grad_mid,
    grad_taps,
    window,
    middle,
    out,
    weights,
    tap_sums,
    *,
    rows,
    breadth,
    pitch,
    gap,
):
    width = taps.shape[1]

    @pl.when(pl.program_id(0) == 0)
    def _():
        window[...] = jnp.zeros_like(window)
        tap_sums[...] = jnp.zeros_like(tap_sums)
        fill_pair_weights(weights, taps, width)

    far_at, near_at = sides(2 * rows * gap)
    for g, (start, _) in enumerate(pair_groups(width)):
        for offset, source in ((far_at, far), (rows * gap, grad_lka), (near_at, near)):
            for r in range(rows):
                at = pl.ds(pl.multiple_of(offset + (16 + r * gap), 8), pitch)
                window[g, at, :] = source[0, r, :, start : start + lanes].astype(wide)
        for r in range(rows):
            middle[g, r * pitch : (r + 1) * pitch, :] = lka_mid[
                0, r, :, start : start + lanes
            ].astype(wide)
    for g, (start, which) in enumerate(pair_groups(width)):

        def step(block, carry, g=g, start=start, which=which):
            base = pl.multiple_of(block * 8, 8)

            def add_tap(t, value):
                tap_sums[which, t] += value

            total = window_sums(
                lambda r, s: window[g, pl.ds(base + (16 + r * gap + s), 8), :],
                lambda t: weights[which, t],
                7,
                3,
                rows,
                True,
                [middle[g, pl.ds(base + p * pitch, 8), :] for p in range(rows)],
                add_tap,
            )
            for o in range(rows):
                out[pl.ds(base + o * pitch, 8), start : start + lanes] = total[o]
            return carry

        lax.fori_loop(0, pitch // 8, step, 0, unroll=True)
    for r in range(rows):
        at = r * pitch
        grad_mid[0, r] = (
            out[at : at + pitch, :] * inside(1, pitch, breadth, 2 * width)
        ).astype(low)

    @pl.when(pl.program_id(0) == pl.num_programs(0) - 1)
    def _():
        store_pair_taps(grad_taps, tap_sums, width)
        grad_taps[...] += taps_before[...]


def five_kernel(
    counts,
    images,
    grad_mid,
    far,
    near,
    gelu_low,
    pre_gelu,
    grad_direct,
    grad_first,
    params,
    stats,
    proj_in,
    taps,
    lka_sum,
    out_sum,
    seven_sum,
    three_sum,
    scale_one,
    scale_two,
    grad_partial,
    packed_kept,
    packed_sent,
    grad_proj_in,
    grad_taps,
    sums,
    pack,
    window,
    middle,
    out,
    weights,
    tap_sums,
    values,
    mask,
    *,
    rows,
    breadth,
    pitch,
):
    width = images.shape[3]
    alive = alive_lanes(counts, 0, width)
    pixels = pixels_of(counts, rows * breadth)
    mean, rstd = norm_of(stats, pixels)
    mean, rstd = paired(mean), paired(rstd)
    gain, shift, scale = (paired(params[k : k + 1, :]) for k in range(3))

    @pl.when(pl.program_id(0) == 0)
    def _():
        window[...] = jnp.zeros_like(window)
        tap_sums[...] = jnp.zeros_like(tap_sums)
        values[...] = jnp.zeros_like(values)
        sums[...] = jnp.zeros_like(sums)
        grad_proj_in[...] = jnp.zeros_like(grad_proj_in)
        mask[...] = inside(rows, pitch, breadth, 2 * width)
        fill_pair_weights(weights, taps, width)

    for g, (start, _) in enumerate(pair_groups(width)):
        for source, offset in zip((far, near), sides((rows + 2) * pitch)):
            for r in range(2):
                at = pl.ds(pl.multiple_of(offset + (8 + r * pitch), 8), pitch)
                window[g, at, :] = source[0, r, :, start : start + lanes].astype(wide)
        for r in range(rows):
            at = 8 + (r + 2) * pitch
            window[g, at : at + pitch, :] = grad_mid[0, r, :, start : start + lanes].astype(wide)
        middle[g] = gelu_low[0, :, start : start + lanes].astype(wide)
    for g, (start, which) in enumerate(pair_groups(width)):

        def step(block, carry, g=g, start=start, which=which):
            base = pl.multiple_of(block * 8, 8)

            def add_tap(t, value):
                tap_sums[which, t] += value

            total = window_sums(
                lambda r, s: window[g, pl.ds(base + (8 + r * pitch + s), 8), :],
                lambda t: weights[which, t],
                5,
                1,
                rows,
                True,
                [middle[g, pl.ds(base + p * pitch, 8), :] for p in range(rows)],
                add_tap,
            )
            for o in range(rows):
                out[pl.ds(base + o * pitch, 8), start : start + lanes] = total[o]
            return carry

        lax.fori_loop(0, pitch // 8, step, 0, unroll=True)
    for r in range(rows):
        values[r * pitch : r * pitch + breadth, :] = pair_lanes(
            images[0, r].astype(wide), images[1, r].astype(wide)
        )
    pre = pre_gelu[0].astype(wide)
    cdf, density = normal_parts(pre)
    grad_pre = ((grad_direct[0].astype(wide) + out[...]) * (cdf + pre * density)).astype(low)
    xhat = (values[...] - mean) * rstd
    normed = (xhat * gain + shift) * mask[...]
    grad_proj_in[...] += folded_square(
        jnp.dot(normed.T.astype(low), grad_pre, preferred_element_type=wide)
    )
    back = lax.dot_general(
        grad_pre, proj_in[...], (((1,), (1,)), ((), ())), preferred_element_type=wide
    )
    first = grad_first[0]
    grad_normed = (first * scale + back) * mask[...]
    sums[0:1, :] += folded(jnp.sum(grad_normed, axis=0, keepdims=True))
    sums[1:2, :] += folded(jnp.sum(grad_normed * xhat, axis=0, keepdims=True))
    grad_partial[0], grad_partial[1] = split_lanes(first + alive * rstd * gain * grad_normed)

    @pl.when(pl.program_id(0) == pl.num_programs(0) - 1)
    def _():
        store_pair_taps(grad_taps, tap_sums, width)
        pack[...] = jnp.zeros_like(pack)
        at = 0
        for part in (grad_proj_in, lka_sum, out_sum, grad_taps, seven_sum):
            pack[at : at + part.shape[0], :] = part[...]
            at += -(-part.shape[0] // 8) * 8
        for k in range(three_sum.shape[1] // width):
            pack[at : at + 9, :] = three_sum[:, k * width : (k + 1) * width]
            at += 9
        at = pack.shape[0] - 8
        pack[at : at + 2, :] = sums[...]
        pack[at + 2 : at + 3, :] = scale_one[...]
        pack[at + 3 : at + 4, :] = scale_two[...]
        half = (pack.shape[0] - 8) // 2
        for target, offset in zip((packed_kept, packed_sent), sides(half)):
            target[0:half, :] = pack[pl.ds(pl.multiple_of(offset, 8), half), :].astype(low)
            target[half:, :] = pack[at:, :].astype(low)


def pack_rows(width, deep):
    return -(-(3 * width + 32 + 56 + 9 * (deep // width)) // 64) * 64


def spread_kernel(packed, grad_in, grad_lka, grad_out, grad_five, grad_seven, grad_three):
    width = packed.shape[1]
    at = 0
    for part in (grad_in, grad_lka, grad_out, grad_five, grad_seven):
        size = -(-part.shape[0] // 8) * 8
        part[...] = packed[at : at + size, :].astype(wide)[: part.shape[0]]
        at += size
    rest = packed[at:, :].astype(wide)
    for k in range(grad_three.shape[1] // width):
        grad_three[:, k * width : (k + 1) * width] = rest[9 * k : 9 * k + 9]


def last_kernel(
    counts, images, grad_partial, params, stats, grad_stats, grad_images, *, rows, breadth, pitch
):
    alive = (pl.program_id(0) < live_here(counts)).astype(wide)
    pixels = pixels_of(counts, rows * breadth)
    mean, rstd = norm_of(stats, pixels)
    factor = alive * rstd * params[0:1, :] / pixels
    grad_sums = grad_stats[...].astype(wide)
    shift_sum, gain_sum = grad_sums[0:1, :], grad_sums[1:2, :]
    for r in range(rows):
        xhat = (images[0, r].astype(wide) - mean) * rstd
        part = grad_partial[0, r * pitch : r * pitch + breadth, :]
        grad_images[0, r] = part - factor * (shift_sum + xhat * gain_sum)


def mlp_kernel(
    counts,
    first_sum,
    far,
    near,
    cot,
    cot_far,
    cot_near,
    params,
    stats,
    fc_in,
    fc_out,
    taps,
    out_image,
    grad_normed,
    copies,
    scale_sum,
    fc_kept,
    fc_sent,
    grad_taps,
    sums,
    normed_wide,
    mlp_wide,
    normed_low,
    normed_turned,
    grads_low,
    grads_turned,
    hidden_even,
    hidden_odd,
    active_even,
    active_odd,
    grad_mixed,
    low_even,
    low_odd,
    back_even,
    back_odd,
    mlp_sum,
    normed_sum,
    weights,
    tap_sums,
    in_sum,
    out_sum,
    *,
    rows,
    breadth,
    pitch,
):
    image = pl.program_id(0)
    alive = (image < live_here(counts)).astype(jnp.float32)
    groups = fc_in.shape[1] // (2 * lanes)
    blocks = pitch // 8
    pixels = pixels_of(counts, rows * breadth)
    mean_two, rstd_two = norm_of(stats, pixels)
    gain_two, shift_two, scale_two = params[3:4, :], params[4:5, :], params[5:6, :]

    @pl.when(image == 0)
    def _():
        normed_wide[...] = jnp.zeros_like(normed_wide)
        mlp_wide[...] = jnp.zeros_like(mlp_wide)
        hidden_even[...] = jnp.zeros_like(hidden_even)
        hidden_odd[...] = jnp.zeros_like(hidden_odd)
        grad_mixed[...] = jnp.zeros_like(grad_mixed)
        tap_sums[...] = jnp.zeros_like(tap_sums)
        in_sum[...] = jnp.zeros_like(in_sum)
        out_sum[...] = jnp.zeros_like(out_sum)
        sums[...] = jnp.zeros_like(sums)
        scale_sum[...] = jnp.zeros_like(scale_sum)
        fill_weights(weights, taps, taps.shape[1])

    def normalized(value):
        return (value - mean_two) * rstd_two * gain_two + shift_two

    for source, offset, there in zip((far, near), sides((rows + 2) * pitch), present()):
        for r in range(2):
            at = pl.ds(pl.multiple_of(offset + r * pitch, 8), breadth)
            normed_wide[at, :] = there * normalized(source[0, r, 0:breadth, :])
    for r in range(rows):
        at = (r + 2) * pitch
        normed_wide[at : at + breadth, :] = normalized(first_sum[0, r, 0:breadth, :])
        at = (r + 1) * pitch
        mlp_wide[at : at + breadth, :] = cot[0, r].astype(jnp.float32) * alive * scale_two
    for source, offset in zip((cot_far, cot_near), sides((rows + 1) * pitch)):
        at = pl.ds(pl.multiple_of(offset, 8), breadth)
        mlp_wide[at, :] = source[0, 0].astype(wide) * alive * scale_two
    normed_low[...] = normed_wide[...].astype(jnp.bfloat16)
    grads_low[...] = mlp_wide[...].astype(jnp.bfloat16)
    inner = normed_wide[2 * pitch : (rows + 2) * pitch, :]
    normed_turned[...] = inner.T.astype(jnp.bfloat16)
    grads_turned[...] = mlp_wide[pitch : (rows + 1) * pitch, :].T.astype(jnp.bfloat16)
    mlp_sum[...] = jnp.zeros_like(mlp_sum)
    normed_sum[...] = jnp.zeros_like(normed_sum)

    hiddens, sources = (hidden_even, hidden_odd), (active_even, active_odd)
    actives, backs = (low_even, low_odd), (back_even, back_odd)

    def columns(group):
        return slice(group * 2 * lanes, (group + 1) * 2 * lanes)

    def enter(group):
        hid = jnp.dot(normed_low[...], fc_in[:, columns(group)], preferred_element_type=wide)
        hid = hid.astype(low).astype(wide)
        act = jnp.dot(grads_low[...], fc_out[:, columns(group)], preferred_element_type=wide)
        for half in range(2):
            lane = slice(half * lanes, (half + 1) * lanes)
            hiddens[group % 2][half, 8 : 8 + (rows + 4) * pitch, :] = hid[:, lane]
            sources[group % 2][half] = act[:, lane]

    def forward(group, half, block):
        hidden, source, active = (refs[group % 2] for refs in (hiddens, sources, actives))
        lane = slice(half * lanes, (half + 1) * lanes)
        place, base = group * 2 + half, block * 8
        mixed = window_sums(
            lambda r, s: hidden[half, pl.ds(base + (8 + r * pitch + s), 8), :],
            lambda t: weights[place, t],
            3,
            1,
            rows + 2,
            False,
        )
        for o in range(rows + 2):
            x = mixed[o]
            cdf, density = normal_parts(x)
            slope = cdf + x * density
            grad_mixed[half, pl.ds(base + (8 + o * pitch), 8), :] = (
                source[half, pl.ds(base + o * pitch, 8), :] * slope
            )
            if 1 <= o <= rows:
                active[pl.ds(base + (o - 1) * pitch, 8), lane] = x * cdf

    def backward(group, half, block):
        hidden, back = hiddens[group % 2], backs[group % 2]
        lane = slice(half * lanes, (half + 1) * lanes)
        place, base = group * 2 + half, block * 8

        def add_tap(t, value):
            tap_sums[place, t] += value

        total = window_sums(
            lambda r, s: grad_mixed[half, pl.ds(base + (8 + r * pitch + s), 8), :],
            lambda t: weights[place, t],
            3,
            1,
            rows,
            True,
            [hidden[half, pl.ds(base + (8 + (p + 2) * pitch), 8), :] for p in range(rows)],
            add_tap,
        )
        for p in range(rows):
            back[pl.ds(base + p * pitch, 8), lane] = total[p]

    def leave(group):
        act_low = actives[group % 2][...].astype(low)
        hid_low = backs[group % 2][...].astype(low)
        mlp_sum[...] += lax.dot_general(
            act_low,
            fc_out[:, columns(group)],
            (((1,), (1,)), ((), ())),
            preferred_element_type=wide,
        )
        normed_sum[...] += lax.dot_general(
            hid_low,
            fc_in[:, columns(group)],
            (((1,), (1,)), ((), ())),
            preferred_element_type=wide,
        )
        part_in = jnp.dot(normed_turned[...], hid_low, preferred_element_type=wide)
        part_out = jnp.dot(grads_turned[...], act_low, preferred_element_type=wide)
        for half in range(2):
            lane = slice(half * lanes, (half + 1) * lanes)
            in_sum[group * 2 + half] += part_in[:, lane]
            out_sum[group * 2 + half] += part_out[:, lane]

    enter(0)
    for group in range(groups):
        if group + 1 < groups:
            enter(group + 1)
        if group > 0:
            leave(group - 1)
        for half in range(2):
            for block in range(blocks):
                forward(group, half, block)
        for half in range(2):
            for block in range(blocks):
                backward(group, half, block)
    leave(groups - 1)

    scale_grad = jnp.zeros_like(scale_two)
    shift_grad = jnp.zeros_like(scale_two)
    gain_grad = jnp.zeros_like(scale_two)
    for r in range(rows):
        mlp = mlp_sum[r * pitch : r * pitch + breadth, :]
        back = normed_sum[r * pitch : r * pitch + breadth, :]
        first = first_sum[0, r, 0:breadth, :]
        out_image[0, r] = (alive * (first + scale_two * mlp)).astype(jnp.bfloat16)
        grad_normed[0, r * pitch : r * pitch + breadth, :] = back
        grad_normed[0, r * pitch + breadth : (r + 1) * pitch, :] = jnp.zeros(
            (pitch - breadth, back.shape[1]), wide
        )
        grad = cot[0, r].astype(jnp.float32) * alive
        scale_grad += jnp.sum(grad * mlp, axis=0, keepdims=True)
        shift_grad += jnp.sum(back, axis=0, keepdims=True)
        gain_grad += jnp.sum(back * (first - mean_two) * rstd_two, axis=0, keepdims=True)
    sums[0:1, :] += shift_grad
    sums[1:2, :] += gain_grad
    scale_sum[...] += scale_grad

    @pl.when(image == pl.num_programs(0) - 1)
    def _():
        copies[...] = jnp.broadcast_to(sums[...][None], copies.shape)
        odd = lax.axis_index("strip") % 2

        @pl.when(odd == 0)
        def _():
            fc_kept[...] = in_sum[...].astype(low)
            fc_sent[...] = out_sum[...].astype(low)

        @pl.when(odd == 1)
        def _():
            fc_kept[...] = out_sum[...].astype(low)
            fc_sent[...] = in_sum[...].astype(low)

        store_taps(grad_taps, tap_sums, taps.shape[1])


def unpack_kernel(own, other, grad_in, grad_out):
    def spread(source, target):
        for g in range(source.shape[0]):
            target[:, g * lanes : (g + 1) * lanes] = source[g].astype(wide)

    odd = lax.axis_index("strip") % 2

    @pl.when(odd == 0)
    def _():
        spread(own, grad_in)
        spread(other, grad_out)

    @pl.when(odd == 1)
    def _():
        spread(other, grad_in)
        spread(own, grad_out)


def mlp_block(
    counts, first_sum, far, near, cot, cot_far, cot_near, params, stats, fc_in, fc_out, taps
):
    images, rows, breadth, width = cot.shape
    pitch = first_sum.shape[2]
    deep = fc_in.shape[1]
    groups = deep // lanes
    return call(
        mlp_kernel,
        images,
        [
            (counts, smem),
            (first_sum, spec_image(rows, pitch, width)),
            (far, spec_image(2, pitch, width)),
            (near, spec_image(2, pitch, width)),
            (cot, spec_image(rows, breadth, width)),
            (cot_far, spec_image(1, breadth, width)),
            (cot_near, spec_image(1, breadth, width)),
            (params, spec_whole(8, width)),
            (stats, spec_whole(*stats.shape)),
            (fc_in, spec_whole(width, deep)),
            (fc_out.T, spec_whole(width, deep)),
            (taps, spec_whole(9, deep)),
        ],
        [
            (cot.shape, low, spec_image(rows, breadth, width)),
            ((images, rows * pitch, width), wide, spec_image(rows * pitch, width)),
            (stats.shape, wide, spec_whole(*stats.shape)),
            ((1, width), wide, spec_whole(1, width)),
            ((groups, width, lanes), low, spec_whole(groups, width, lanes)),
            ((groups, width, lanes), low, spec_whole(groups, width, lanes)),
            ((9, deep), wide, spec_whole(9, deep)),
        ],
        [
            ((2, width), wide),
            (((rows + 4) * pitch, width), wide),
            (((rows + 2) * pitch, width), wide),
            (((rows + 4) * pitch, width), low),
            ((width, rows * pitch), low),
            (((rows + 2) * pitch, width), low),
            ((width, rows * pitch), low),
            ((2, (rows + 4) * pitch + 16, lanes), wide),
            ((2, (rows + 4) * pitch + 16, lanes), wide),
            ((2, (rows + 2) * pitch, lanes), wide),
            ((2, (rows + 2) * pitch, lanes), wide),
            ((2, (rows + 2) * pitch + 16, lanes), wide),
            ((rows * pitch, 2 * lanes), wide),
            ((rows * pitch, 2 * lanes), wide),
            ((rows * pitch, 2 * lanes), wide),
            ((rows * pitch, 2 * lanes), wide),
            ((rows * pitch, width), wide),
            ((rows * pitch, width), wide),
            ((groups, 9, 8, lanes), wide),
            ((groups, 9, 8, lanes), wide),
            ((groups, width, lanes), wide),
            ((groups, width, lanes), wide),
        ],
        53,
        "mlp",
        vmem=28,
        rows=rows,
        breadth=breadth,
        pitch=pitch,
    )


def body(
    images,
    counts,
    gain_one,
    shift_one,
    proj_in,
    kernel_five,
    kernel_seven,
    lka_proj,
    proj_out,
    scale_one,
    gain_two,
    shift_two,
    fc_in,
    kernel_three,
    fc_out,
    scale_two,
    cotangent,
):
    slots, rows, breadth, width = images.shape
    pitch = -(-(breadth + 2) // 8) * 8
    gap = -(-(breadth + 9) // 8) * 8
    flat = rows * pitch
    blank = jnp.zeros_like(gain_one)
    params = jnp.stack(
        [gain_one, shift_one, scale_one, gain_two, shift_two, scale_two, blank, blank]
    ).astype(wide)
    sizes = dict(rows=rows, breadth=breadth, pitch=pitch)
    vec = spec_whole(8, width)
    devices = device_count()
    blocks = (devices, 2, width)
    two = spec_whole(*blocks)
    square = spec_whole(width, width)
    image_spec = spec_image(rows, breadth, width)
    pairs = slots // 2
    chunks = [(0, pairs - 1), (pairs - 1, 1)]
    pair_width = 2 * width
    pair_square = spec_whole(pair_width, pair_width)
    pair_flat = (pairs, flat, pair_width)
    flat_spec = spec_image(flat, width)
    flat_shape = (slots, flat, width)
    row_shape = (slots, rows, pitch, width)
    groups = len(pair_groups(width))
    kinds = width // lanes + 1
    five_spec = spec_whole(*kernel_five.shape)
    seven_spec = spec_whole(*kernel_seven.shape)

    (first_part,) = call(
        stats_kernel,
        slots,
        [(counts, smem), (images, image_spec)],
        [(blocks, wide, two)],
        [((2, width), wide)],
        2,
        "input_sums",
    )
    first_part, tied_in = lax.optimization_barrier((first_part, proj_in))
    pair_in, pair_lka, pair_out = (pair_matrix(m) for m in (tied_in, lka_proj, proj_out))
    pair_in, images_after, cot_after = lax.optimization_barrier((pair_in, images, cotangent))
    image_far, image_near = far_and_near(
        *(
            jnp.concatenate(parts, axis=1)
            for parts in zip(edge_rows(images_after, 2), edge_rows(cot_after, 1))
        )
    )
    first_stats = from_all(first_part)
    gelu_low = pre_gelu = cot_far = cot_near = None
    cot_shape = (slots, 1, breadth, width)
    mids, rims = [], []
    for start, count in chunks:
        gelu_low, pre_gelu, mid, cot_far, cot_near = call(
            front_kernel,
            count,
            [
                (counts, smem),
                (images, spec_two(start, rows, breadth, width)),
                (image_far, spec_two(start, 3, breadth, width)),
                (image_near, spec_two(start, 3, breadth, width)),
                (params, vec),
                (first_stats, two),
                (pair_in, pair_square),
                (kernel_five, five_spec),
            ],
            [
                (pair_flat, low, spec_from(start, flat, pair_width), gelu_low),
                (pair_flat, low, spec_from(start, flat, pair_width), pre_gelu),
                ((count, rows, pitch, pair_width), low, spec_image(rows, pitch, pair_width)),
                (cot_shape, low, spec_two(start, 1, breadth, width), cot_far),
                (cot_shape, low, spec_two(start, 1, breadth, width), cot_near),
            ],
            [
                (((rows + 4) * pitch, pair_width), wide),
                ((groups, (rows + 4) * pitch + 16, lanes), wide),
                ((kinds, 25, 8, lanes), wide),
                (((rows + 4) * pitch, lanes), wide),
                ((flat, pair_width), wide),
            ],
            4.3 * count,
            f"normed_to_five_{start}",
            vmem=50,
            **sizes,
        )
        mids.append(mid)
        rims.append(far_and_near(mid, mid))
    lka_low = attend = first_sum = None
    second_part = jnp.zeros(blocks, wide)
    for (start, count), mid, (mid_far, mid_near) in zip(chunks, mids, rims):
        rim_spec = spec_image(rows, pitch, pair_width)
        pair_spec = spec_from(start, flat, pair_width)
        lka_low, attend, first_sum, second_part = call(
            attend_kernel,
            count,
            [
                (counts, smem),
                (images, spec_two(start, rows, breadth, width)),
                (mid, rim_spec),
                (mid_far, rim_spec),
                (mid_near, rim_spec),
                (gelu_low, pair_spec),
                (params, vec),
                (first_stats, two),
                (second_part, two),
                (pair_lka, pair_square),
                (pair_out, pair_square),
                (kernel_seven, seven_spec),
            ],
            [
                (pair_flat, low, pair_spec, lka_low),
                (pair_flat, low, pair_spec, attend),
                (flat_shape, wide, spec_two(start, flat, width), first_sum),
                (blocks, wide, two),
            ],
            [
                ((2, width), wide),
                ((groups, 3 * rows * gap + 48, lanes), wide),
                ((kinds, 49, 8, lanes), wide),
                ((flat, pair_width), wide),
                ((flat, pair_width), wide),
                ((flat, pair_width), wide),
            ],
            6.2 * count,
            f"seven_to_first_sum_{start}",
            vmem=20,
            gap=gap,
            start_pair=start,
            **sizes,
        )
    first_rows = first_sum.reshape(row_shape)
    sum_far, sum_near = far_and_near(*edge_rows(first_rows, 2))
    second_stats = from_all(second_part)
    out_image, grad_normed_two, third_part, scale_two_part, fc_kept, fc_sent, grad_kernel_three = mlp_block(
        counts,
        first_rows,
        sum_far,
        sum_near,
        cotangent,
        cot_far,
        cot_near,
        params,
        second_stats,
        fc_in,
        fc_out,
        kernel_three,
    )
    grad_second = from_all(third_part)
    got = lax.ppermute(fc_sent, "strip", near_pairs())
    got, grad_second = lax.optimization_barrier((got, grad_second))
    half = (fc_kept.astype(wide) + got.astype(wide)).astype(low)
    sides_of = [[d for d in range(devices) if d % 2 == k] for k in range(2)]
    fc_share = jnp.sum(
        lax.all_to_all(
            half.reshape(devices // 2, -1, lanes),
            ("dp", "strip"),
            0,
            0,
            axis_index_groups=sides_of,
        ).astype(wide),
        axis=0,
    ).astype(low)
    grad_first = grad_direct = None
    gates, rims = [], []
    lka_sum = out_sum = jnp.zeros((width, width), wide)
    scale_sum = jnp.zeros((1, width), wide)
    for start, count in chunks:
        pair_spec = spec_from(start, flat, pair_width)
        grad_first, grad_direct, grad_lka, lka_sum, out_sum, scale_sum = call(
            gate_kernel,
            count,
            [
                (counts, smem),
                (first_sum, spec_two(start, flat, width)),
                (images, spec_two(start, rows, breadth, width)),
                (cotangent, spec_two(start, rows, breadth, width)),
                (grad_normed_two, spec_two(start, flat, width)),
                (lka_low, pair_spec),
                (attend, pair_spec),
                (gelu_low, pair_spec),
                (params, vec),
                (second_stats, two),
                (grad_second, two),
                (pair_lka, pair_square),
                (pair_out, pair_square),
                (lka_sum, square),
                (out_sum, square),
                (scale_sum, spec_whole(1, width)),
            ],
            [
                (pair_flat, wide, pair_spec, grad_first),
                (pair_flat, low, pair_spec, grad_direct),
                ((count, rows, pitch, pair_width), low, spec_image(rows, pitch, pair_width)),
                ((width, width), wide, square),
                ((width, width), wide, square),
                ((1, width), wide, spec_whole(1, width)),
            ],
            [
                ((flat, pair_width), wide),
                ((flat, pair_width), wide),
                ((flat, pair_width), wide),
            ],
            3.2 * count,
            f"gate_backward_{start}",
            vmem=52,
            start_pair=start,
            **sizes,
        )
        gates.append(grad_lka)
        rims.append(far_and_near(grad_lka, grad_lka))
    grad_mid = None
    seven_sum = jnp.zeros(kernel_seven.shape, wide)
    for (start, count), grad_lka, mid, (lka_far, lka_near) in zip(chunks, gates, mids, rims):
        rim_spec = spec_image(rows, pitch, pair_width)
        grad_mid, seven_sum = call(
            seven_kernel,
            count,
            [
                (grad_lka, rim_spec),
                (lka_far, rim_spec),
                (lka_near, rim_spec),
                (mid, rim_spec),
                (kernel_seven, seven_spec),
                (seven_sum, seven_spec),
            ],
            [
                (
                    (pairs, rows, pitch, pair_width),
                    low,
                    spec_from(start, rows, pitch, pair_width),
                    grad_mid,
                ),
                (kernel_seven.shape, wide, seven_spec),
            ],
            [
                ((groups, 3 * rows * gap + 48, lanes), wide),
                ((groups, flat, lanes), wide),
                ((flat, pair_width), wide),
                ((kinds, 49, 8, lanes), wide),
                ((kinds, 49, 8, lanes), wide),
            ],
            7 * count,
            f"seven_backward_{start}",
            vmem=20,
            gap=gap,
            **sizes,
        )
    five_far, five_near = far_and_near(*edge_rows(grad_mid, 2))
    fc_share, five_far, five_near = lax.optimization_barrier((fc_share, five_far, five_near))
    fc_own = lax.all_to_all(
        jnp.broadcast_to(fc_share[None], (devices // 2,) + fc_share.shape),
        ("dp", "strip"),
        0,
        0,
        axis_index_groups=sides_of,
    ).reshape(fc_kept.shape)
    pair_spec = spec_image(flat, pair_width)
    deep = fc_in.shape[1]
    total_rows = pack_rows(width, deep)
    grad_partial, packed_kept, packed_sent = call(
        five_kernel,
        pairs,
        [
            (counts, smem),
            (images, spec_two(0, rows, breadth, width)),
            (grad_mid, spec_image(rows, pitch, pair_width)),
            (five_far, spec_image(2, pitch, pair_width)),
            (five_near, spec_image(2, pitch, pair_width)),
            (gelu_low, pair_spec),
            (pre_gelu, pair_spec),
            (grad_direct, pair_spec),
            (grad_first, pair_spec),
            (params, vec),
            (first_stats, two),
            (pair_in, pair_square),
            (kernel_five, five_spec),
            (lka_sum, square),
            (out_sum, square),
            (seven_sum, seven_spec),
            (grad_kernel_three, spec_whole(*kernel_three.shape)),
            (scale_sum, spec_whole(1, width)),
            (scale_two_part, spec_whole(1, width)),
        ],
        [
            (flat_shape, wide, spec_two(0, flat, width)),
            ((total_rows // 2 + 8, width), low, spec_whole(total_rows // 2 + 8, width)),
            ((total_rows // 2 + 8, width), low, spec_whole(total_rows // 2 + 8, width)),
        ],
        [
            ((width, width), wide),
            (kernel_five.shape, wide),
            ((2, width), wide),
            ((total_rows + 8, width), wide),
            ((groups, (rows + 4) * pitch + 16, lanes), wide),
            ((groups, flat, lanes), wide),
            ((flat, pair_width), wide),
            ((kinds, 25, 8, lanes), wide),
            ((kinds, 25, 8, lanes), wide),
            ((flat, pair_width), wide),
            ((flat, pair_width), wide),
        ],
        6 * pairs,
        "five_backward",
        vmem=52,
        **sizes,
    )
    fc_own, packed_sent = lax.optimization_barrier((fc_own, packed_sent))
    share, vectors = split_sums(packed_kept, packed_sent, 8)
    fc_other = lax.ppermute(fc_own, "strip", near_pairs())
    (grad_images,) = call(
        last_kernel,
        slots,
        [
            (counts, smem),
            (images, image_spec),
            (grad_partial, flat_spec),
            (params, vec),
            (first_stats, two),
            (vectors, spec_whole(8, width)),
        ],
        [(images.shape, wide, image_spec)],
        [],
        4,
        "input_gradient",
        vmem=56,
        **sizes,
    )
    grad_fc_in, grad_fc_out = call(
        unpack_kernel,
        1,
        [(half, spec_whole(*half.shape)) for half in (fc_own, fc_other)],
        [
            ((width, deep), wide, spec_whole(width, deep)),
            ((width, deep), wide, spec_whole(width, deep)),
        ],
        [],
        2,
        "weight_gradients",
    )
    matrices, (grad_images, (grad_fc_in, grad_fc_out)) = joined(
        share, [grad_images, (grad_fc_in, grad_fc_out)]
    )
    pieces = call(
        spread_kernel,
        1,
        [(matrices, spec_whole(total_rows, width))],
        [
            (shape, wide, spec_whole(*shape))
            for shape in [(width, width)] * 3
            + [kernel_five.shape, kernel_seven.shape, kernel_three.shape]
        ],
        [],
        2,
        "attention_gradients",
    )
    vectors = vectors.astype(wide)
    grad_second = jnp.sum(grad_second, axis=0)
    return (
        out_image,
        grad_images,
        vectors[1],
        vectors[0],
        pieces[0],
        pieces[3],
        pieces[4],
        pieces[1],
        pieces[2],
        vectors[2],
        grad_second[1],
        grad_second[0],
        grad_fc_in,
        pieces[5],
        grad_fc_out.T,
        vectors[3],
    )


def solution(mesh):
    split = P("dp", "strip", None, None)
    return jax.shard_map(
        body,
        mesh=mesh,
        in_specs=(split,) + (P(),) * 15 + (split,),
        out_specs=(split, split) + (P(),) * 14,
        check_vma=False,
    )
```
